32 devices in a mesh: wide: 8 (over z, x), narrow: 4 (over y, core).
Axes of the slice: x: 2, y: 2, z: 4, core: 2. Of those that a mesh axis runs over, the one named last changes fastest.
Arguments:
- tokens: bfloat16 [65536, 1024], P(('wide', 'narrow')), may hold values from -64 to 64
- slot_params: bfloat16 [1024, 128], replicated, may hold values from -2.5 to 2.5
- expert_in: bfloat16 [32, 1024, 4096], P('wide', None, 'narrow'), may hold values from -0.1875 to 0.1875
- expert_out: bfloat16 [32, 4096, 1024], P('wide', 'narrow'), may hold values from -0.09375 to 0.09375
Outputs:
- mixed: bfloat16 [65536, 1024], P(('wide', 'narrow'))
The draws below stay inside these ranges and needn't reach their ends.
All inputs are finite; a program needn't handle non-finite values.
Results may differ from the reference program's by a relative error of at most 0.0071.
Values may be sent and summed in bfloat16 or wider, within the bound.
No kernel may reach another device: no remote copies, remote signals or barrier semaphores. Data moves between devices by JAX's collectives and lax.ppermute only.
A program may use at most 128 MiB of HBM per device.

```python
import math
import jax
import jax.numpy as jnp
from jax import lax

D = 1024
EXPERT_UNITS = 4096
SLOT_PER = 4
EXPERTS = 32
SLOTS = 128
TOKENS = 65536


def slot_table(key):
    table = 3.0 * jax.random.normal(jax.random.fold_in(key, 11), (D, SLOTS), jnp.float32) / math.sqrt(D)
    table = jnp.clip(table, -2.5, 2.5)
    return table.astype(jnp.bfloat16).astype(jnp.float32)


def draw_slot_params(key, part):
    return slot_table(key).astype(jnp.bfloat16)


def draw_tokens(key, part):
    base = jax.random.normal(jax.random.fold_in(key, 12), (TOKENS, D), jnp.float32)
    base = jnp.clip(base, -6.0, 6.0)
    return base.astype(jnp.bfloat16)


def levels(key, extent, cuts, least, high):
    factor_of, own = 1.0, jax.random.fold_in(key, 6)
    for dim, shards_of in cuts:
        heights = jnp.exp(jax.random.uniform(jax.random.fold_in(own, dim), (shards_of,), jnp.float32, least / len(cuts), high / len(cuts)))
        factor_of = factor_of * jnp.repeat(heights, extent[dim] // shards_of).reshape([-1 if axis == dim else 1 for axis in range(len(extent))])
    return factor_of


def centred(rng, dims, width, bound, cuts=(), kind=jnp.bfloat16):
    factor_of = levels(rng, dims, cuts, -0.22, 0.18) if cuts else 1.0
    result = jax.random.normal(rng, dims, jnp.float32) * width * factor_of
    return jnp.minimum(jnp.maximum(result, -bound), bound).astype(kind)


def setup_inputs(seed: int = 0) -> dict:
    streams_of = jax.random.split(jax.random.key(seed), 5)
    tokens = draw_tokens(jax.random.fold_in(streams_of[4], 71), 0)
    slot_params = draw_slot_params(jax.random.fold_in(streams_of[4], 71), 0)
    expert_in = centred(streams_of[2], (EXPERTS, D, EXPERT_UNITS), D ** -0.5, 0.1875, ((0, 8), (2, 4)))
    expert_out = centred(streams_of[3], (EXPERTS, EXPERT_UNITS, D), EXPERT_UNITS ** -0.5, 0.09375, ((0, 8), (1, 4)))
    return {"tokens": tokens, "slot_params": slot_params, "expert_in": expert_in, "expert_out": expert_out}


def block_logits(block_tokens, slot_params):
    return jnp.dot(block_tokens, slot_params, preferred_element_type=jnp.float32)


def reference(tokens, slot_params, expert_in, expert_out):
    block_size = math.gcd(TOKENS, 8192)
    grouped = tokens.reshape(TOKENS // block_size, block_size, D)
    peaks = lax.map(lambda block_tokens: jnp.max(block_logits(block_tokens, slot_params), axis=0), grouped)
    column_peak = jnp.max(peaks, axis=0)

    def gather_step(carry, block_tokens):
        totals, sums = carry
        logits = block_logits(block_tokens, slot_params)
        weights = jnp.exp(logits - column_peak)
        totals = totals + jnp.sum(weights, axis=0)
        sums = sums + lax.dot_general(weights.astype(jnp.bfloat16), block_tokens, (((0,), (0,)), ((), ())), preferred_element_type=jnp.float32)
        return (totals, sums), None

    start_carry = (jnp.zeros((SLOTS,), jnp.float32), jnp.zeros((SLOTS, D), jnp.float32))
    (totals, sums), unused = lax.scan(gather_step, start_carry, grouped)
    slot_in = (sums / totals[:, None]).astype(jnp.bfloat16)
    stacked = slot_in.reshape(EXPERTS, SLOT_PER, D)

    def expert_step(operands):
        slot_rows, first_weight, second_weight = operands
        hidden = jax.nn.gelu(jnp.dot(slot_rows, first_weight, preferred_element_type=jnp.float32)).astype(jnp.bfloat16)
        return jnp.dot(hidden, second_weight, preferred_element_type=jnp.float32)

    outputs = lax.map(expert_step, (stacked, expert_in, expert_out)).reshape(SLOTS, D).astype(jnp.bfloat16)

    def combine_block(block_tokens):
        logits = block_logits(block_tokens, slot_params)
        mixing = jax.nn.softmax(logits, axis=1).astype(jnp.bfloat16)
        return jnp.dot(mixing, outputs, preferred_element_type=jnp.float32).astype(jnp.bfloat16)

    mixed = lax.map(combine_block, grouped).reshape(TOKENS, D)
    return mixed
```

```python
import jax
import jax.numpy as jnp
from jax import lax
from jax.sharding import PartitionSpec as P

SLOT_PER = 4
SIDE = 128


def pieces(value):
    high = lax.reduce_precision(value, 8, 7)
    rest = value - high
    middle = lax.reduce_precision(rest, 8, 7)
    return [high, middle, rest - middle]


def pack(mean, peak, total):
    columns = jnp.stack(pieces(peak) + pieces(total), axis=-1)
    side = jnp.pad(columns, ((0, 0), (0, SIDE - columns.shape[1])))
    return jnp.concatenate([mean, side], axis=1).astype(jnp.bfloat16)


def combine_parts(parts):
    width = parts.shape[2] - SIDE
    wide_parts = parts.astype(jnp.float32)
    side = wide_parts[:, :, width:]
    peaks = side[:, :, 0] + side[:, :, 1] + side[:, :, 2]
    totals = side[:, :, 3] + side[:, :, 4] + side[:, :, 5]
    peak = jnp.max(peaks, axis=0)
    shares = totals * jnp.exp(peaks - peak)
    total = jnp.sum(shares, axis=0)
    mean = jnp.sum(wide_parts[:, :, :width] * (shares / total)[:, :, None], axis=0)
    return mean, peak, total


def rotations(value, axis):
    size = lax.axis_size(axis)
    return [
        lax.ppermute(value, axis, [(i, (i + step) % size) for i in range(size)])
        for step in range(1, size)
    ]


def shards(tokens, slot_params, expert_in, expert_out):
    wide = lax.axis_size("wide")
    logits = jnp.dot(tokens, slot_params, preferred_element_type=jnp.float32)
    peak = jnp.max(logits, axis=0)
    weights = jnp.exp(logits - peak)
    total = jnp.sum(weights, axis=0)
    sums = lax.dot_general(
        weights.astype(jnp.bfloat16), tokens, (((0,), (0,)), ((), ())), preferred_element_type=jnp.float32
    )
    packed = pack(sums / total[:, None], peak, total)
    rows = packed.shape[0] // wide
    received = lax.all_to_all(packed, "wide", split_axis=0, concat_axis=0, tiled=True)
    packed = pack(*combine_parts(received.reshape(wide, rows, -1)))
    slot_in, _, _ = combine_parts(jnp.stack([packed] + rotations(packed, "narrow")))
    slot_in = slot_in.astype(jnp.bfloat16)
    slot_stack = slot_in.reshape(expert_in.shape[0], SLOT_PER, slot_in.shape[1])
    hidden = jax.nn.gelu(
        jnp.einsum("esd,edh->esh", slot_stack, expert_in, preferred_element_type=jnp.float32)
    ).astype(jnp.bfloat16)
    partial = jnp.einsum("esh,ehd->esd", hidden, expert_out, preferred_element_type=jnp.float32)
    partial = partial.reshape(rows, -1)
    others = rotations(partial.astype(jnp.bfloat16), "narrow")
    owned = (partial + sum(other.astype(jnp.float32) for other in others)).astype(jnp.bfloat16)
    blocks = jnp.stack([owned] + rotations(owned, "wide"))
    order = (lax.axis_index("wide") - jnp.arange(wide)) % wide
    slot_out = jnp.take(blocks, order, axis=0).reshape(wide * rows, -1)
    mixing = jax.nn.softmax(logits, axis=1).astype(jnp.bfloat16)
    mixed = jnp.dot(mixing, slot_out, preferred_element_type=jnp.float32)
    return mixed.astype(jnp.bfloat16)


def solution(mesh):
    return jax.shard_map(
        shards,
        mesh=mesh,
        in_specs=(
            P(("wide", "narrow"), None),
            P(),
            P("wide", None, "narrow"),
            P("wide", "narrow", None),
        ),
        out_specs=P(("wide", "narrow"), None),
        check_vma=False,
    )
```

```python
import functools

import jax
import jax.numpy as jnp
from jax import lax
from jax.experimental import pallas as pl
from jax.experimental.pallas import tpu as pltpu
from jax.sharding import PartitionSpec as P

SLOT_PER = 4
SIDE = 128
CHUNK = 256
F32 = jnp.float32
BF16 = jnp.bfloat16
VMEM = pl.BlockSpec(memory_space=pltpu.VMEM)
SMEM = pl.BlockSpec(memory_space=pltpu.SMEM)
ANY = pl.BlockSpec(memory_space=pl.ANY)
MIB = 1024 * 1024


def params(mib):
    return pltpu.CompilerParams(vmem_limit_bytes=mib * MIB)


def dot(lhs, rhs, dims):
    return lax.dot_general(lhs, rhs, ((dims[0], dims[1]), ((), ())), preferred_element_type=F32)


def side_state(peak, total):
    lane = lax.broadcasted_iota(jnp.int32, (peak.shape[0], SIDE), 1)
    return jnp.where(lane == 0, peak, jnp.where(lane == 1, total, 0.0))


def side_message(peak, total):
    lane = lax.broadcasted_iota(jnp.int32, (peak.shape[0], SIDE), 1)
    out = jnp.zeros((peak.shape[0], SIDE), F32)
    for index, value in enumerate((peak, total)):
        for piece in range(3):
            part = value.astype(BF16).astype(F32)
            out = jnp.where(lane == 3 * index + piece, part, out)
            value = value - part
    return out.astype(BF16)


def gather_kernel(place, tokens, slot_params, logits, keep, side, send, held, table, sems):
    chunks = tokens.shape[0] // CHUNK
    copies = [
        pltpu.make_async_copy(tokens.at[pl.ds(i * CHUNK, CHUNK)], held.at[pl.ds(i * CHUNK, CHUNK)], sems.at[i])
        for i in range(chunks)
    ]
    for copy in copies:
        copy.start()
    slots = slot_params.shape[1]
    row = lax.broadcasted_iota(jnp.int32, (slots, slots), 0)
    column = lax.broadcasted_iota(jnp.int32, (slots, slots), 1)
    swap = jnp.where(row == (column ^ place[0]), 1.0, 0.0).astype(BF16)
    table[...] = dot(swap, slot_params[...], ((1,), (1,))).astype(BF16)
    peak = None
    for i in range(chunks):
        copies[i].wait()
        part = dot(table[...], held[pl.ds(i * CHUNK, CHUNK), :], ((1,), (1,)))
        logits[:, pl.ds(i * CHUNK, CHUNK)] = part
        part_peak = jnp.max(part, axis=1, keepdims=True)
        peak = part_peak if peak is None else jnp.maximum(peak, part_peak)
    weights = jnp.exp(logits[...] - peak)
    total = jnp.sum(weights, axis=1, keepdims=True)
    sums = dot(weights.astype(BF16), held[...], ((1,), (0,)))
    half = sums.shape[1] // 2
    low, high = sums[:, :half], sums[:, half:]
    first = place[1] == 0
    keep[...] = jnp.where(first, low, high)
    side[...] = side_state(peak, total)
    send[:, :half] = jnp.where(first, high, low).astype(BF16)
    send[:, half:] = side_message(peak, total)


def merge(keep, side, received, rows):
    width = keep.shape[1]
    mine, other = side[rows, :], received[rows, width:].astype(F32)
    peak_mine, total_mine = mine[:, 0:1], mine[:, 1:2]
    peak_other = other[:, 0:1] + other[:, 1:2] + other[:, 2:3]
    total_other = other[:, 3:4] + other[:, 4:5] + other[:, 5:6]
    peak = jnp.maximum(peak_mine, peak_other)
    scale_mine, scale_other = jnp.exp(peak_mine - peak), jnp.exp(peak_other - peak)
    total = total_mine * scale_mine + total_other * scale_other
    sums = keep[rows, :] * scale_mine + received[rows, :width].astype(F32) * scale_other
    return sums, peak, total


def merge_kernel(rows, keep, side, received, keep_out, side_out, send):
    width = keep.shape[1]
    blocks = keep.shape[0] // rows
    for block in range(blocks):
        sums, peak, total = merge(keep, side, received, pl.ds(block * rows, rows))
        target = pl.ds(block // 2 * rows, rows)
        if block % 2 == 0:
            keep_out[target, :] = sums
            side_out[target, :] = side_state(peak, total)
        if block % 2 == 1 or blocks == 1:
            send[target, :width] = sums.astype(BF16)
            send[target, width:] = side_message(peak, total)


def merge_call(keep, side, received, rows):
    left = max(keep.shape[0] // 2, rows)
    width = keep.shape[1]
    return pl.pallas_call(
        functools.partial(merge_kernel, rows),
        out_shape=(
            jax.ShapeDtypeStruct((left, width), F32),
            jax.ShapeDtypeStruct((left, SIDE), F32),
            jax.ShapeDtypeStruct((left, width + SIDE), BF16),
        ),
        in_specs=[VMEM] * 3,
        out_specs=(VMEM,) * 3,
        name="merge",
    )(keep, side, received)


def finish_kernel(keep, side, received, slot_in):
    sums, _, total = merge(keep, side, received, pl.ds(0, keep.shape[0]))
    slot_in[...] = (sums / total).astype(BF16)


def expert_kernel(place, mine, other, expert_in, expert_out, keep, send, first_held, second_held, sems):
    experts = expert_in.shape[0]
    first_copies = [
        pltpu.make_async_copy(expert_in.at[e], first_held.at[e], sems.at[0, e]) for e in range(experts)
    ]
    second_copies = [
        pltpu.make_async_copy(expert_out.at[e], second_held.at[e], sems.at[1, e]) for e in range(experts)
    ]
    for e in range(experts):
        first_copies[e].start()
        second_copies[e].start()
    half = mine.shape[1]
    first = place[1] == 0
    slot_in = jnp.concatenate(
        [jnp.where(first, mine[...], other[...]), jnp.where(first, other[...], mine[...])], axis=1
    )
    row = lax.broadcasted_iota(jnp.int32, (mine.shape[0], 1), 0)
    result = jnp.zeros((mine.shape[0], expert_out.shape[2]), F32)
    for e in range(experts):
        first_copies[e].wait()
        hidden = jax.nn.gelu(dot(slot_in, first_held[e], ((1,), (0,)))).astype(BF16)
        second_copies[e].wait()
        out = dot(hidden, second_held[e], ((1,), (0,)))
        result = jnp.where(row // SLOT_PER == e, out, result)
    low, high = result[:, :half], result[:, half:]
    keep[...] = jnp.where(first, low, high)
    send[...] = jnp.where(first, high, low).astype(BF16)


def combine_kernel(logits, combine):
    value = logits[...]
    weights = jnp.exp(value - jnp.max(value, axis=0, keepdims=True))
    weights = weights / jnp.sum(weights, axis=0, keepdims=True)
    combine[...] = weights.T.astype(BF16)


def mix_kernel(place, combine, slot_out, mixed):
    mixed[...] = dot(combine[...], slot_out[...], ((1,), (0,))).astype(BF16)


def mix_second_kernel(place, combine, slot_out, before, mixed):
    mixed[...] = dot(combine[...], slot_out[...], ((1,), (0,))).astype(BF16)


def mix_call(which, combine, slot_out, before=None):
    tokens, slots = combine.shape
    width = slot_out.shape[1]
    block = 512
    in_specs = [
        pl.BlockSpec((block, slots), lambda i, which: (i, 0)),
        pl.BlockSpec((slots, width), lambda i, which: (0, 0)),
    ]
    operands = [which, combine, slot_out]
    if before is not None:
        in_specs.append(ANY)
        operands.append(before)
    return pl.pallas_call(
        mix_kernel if before is None else mix_second_kernel,
        out_shape=jax.ShapeDtypeStruct((tokens, 2 * width), BF16),
        grid_spec=pltpu.PrefetchScalarGridSpec(
            num_scalar_prefetch=1,
            grid=(tokens // block,),
            in_specs=in_specs,
            out_specs=pl.BlockSpec((block, width), lambda i, which: (i, which[0])),
        ),
        input_output_aliases={} if before is None else {3: 0},
        cost_estimate=pl.CostEstimate(
            flops=2 * tokens * slots * width, bytes_accessed=2 * tokens * (width + slots), transcendentals=0
        ),
        compiler_params=params(16),
        name="mix",
    )(*operands)


def exchange(value, axis, bit):
    return lax.ppermute(value, axis, [(i, i ^ bit) for i in range(lax.axis_size(axis))])


def bits(axis, first=1):
    found, bit = [], first
    while bit < lax.axis_size(axis):
        found.append(bit)
        bit *= 2
    return found


def shards(tokens, slot_params, expert_in, expert_out):
    count, model = tokens.shape
    slots = slot_params.shape[1]
    rows = slots // lax.axis_size("wide")
    half = model // 2
    side_of = lax.axis_index("narrow") % 2
    place = jnp.stack([lax.axis_index("wide") * rows, side_of]).astype(jnp.int32)

    logits, keep, side, send = pl.pallas_call(
        gather_kernel,
        out_shape=(
            jax.ShapeDtypeStruct((slots, count), F32),
            jax.ShapeDtypeStruct((slots, half), F32),
            jax.ShapeDtypeStruct((slots, SIDE), F32),
            jax.ShapeDtypeStruct((slots, half + SIDE), BF16),
        ),
        in_specs=[SMEM, ANY, VMEM],
        out_specs=(VMEM,) * 4,
        scratch_shapes=[
            pltpu.VMEM((count, model), BF16),
            pltpu.VMEM((slots, model), BF16),
            pltpu.SemaphoreType.DMA((count // CHUNK,)),
        ],
        compiler_params=params(40),
        name="gather",
    )(place, tokens, slot_params)
    received = exchange(send, "narrow", 1)
    combine = pl.pallas_call(
        combine_kernel,
        out_shape=jax.ShapeDtypeStruct((count, slots), BF16),
        grid=(count // 512,),
        in_specs=[pl.BlockSpec((slots, 512), lambda i: (0, i))],
        out_specs=pl.BlockSpec((512, slots), lambda i: (i, 0)),
        cost_estimate=pl.CostEstimate(
            flops=8 * count * slots, bytes_accessed=6 * count * slots, transcendentals=count * slots
        ),
        compiler_params=params(16),
        name="combine",
    )(logits)
    for bit in bits("wide"):
        keep, side, send = merge_call(keep, side, received, rows)
        received = exchange(send, "wide", bit)
    for bit in bits("narrow", 2):
        keep, side, send = merge_call(keep, side, received, rows)
        received = exchange(send, "narrow", bit)
    mine = pl.pallas_call(
        finish_kernel,
        out_shape=jax.ShapeDtypeStruct((rows, half), BF16),
        in_specs=[VMEM] * 3,
        out_specs=VMEM,
        name="finish",
    )(keep, side, received)
    other = exchange(mine, "narrow", 1)
    keep, send = pl.pallas_call(
        expert_kernel,
        out_shape=(jax.ShapeDtypeStruct((rows, half), F32), jax.ShapeDtypeStruct((rows, half), BF16)),
        in_specs=[SMEM, VMEM, VMEM, ANY, ANY],
        out_specs=(VMEM, VMEM),
        scratch_shapes=[
            pltpu.VMEM(expert_in.shape, BF16),
            pltpu.VMEM(expert_out.shape, BF16),
            pltpu.SemaphoreType.DMA((2, expert_in.shape[0])),
        ],
        compiler_params=params(40),
        name="experts",
    )(place, mine, other, expert_in, expert_out)
    keep = keep + exchange(send, "narrow", 1).astype(F32)
    for bit in bits("narrow", 2):
        keep = keep + exchange(keep.astype(BF16), "narrow", bit).astype(F32)
    block = keep.astype(BF16)
    for bit in reversed(bits("wide")):
        other = exchange(block, "wide", bit)
        pieces = zip(block.reshape(-1, rows, half), other.reshape(-1, rows, half))
        block = jnp.concatenate([part for pair in pieces for part in pair], axis=0)
    other = exchange(block, "narrow", 1)
    mixed = mix_call(place[1:], combine, block)
    return mix_call(1 - place[1:], combine, other, mixed)


def solution(mesh):
    return jax.shard_map(
        shards,
        mesh=mesh,
        in_specs=(
            P(("wide", "narrow"), None),
            P(),
            P("wide", None, "narrow"),
            P("wide", "narrow", None),
        ),
        out_specs=P(("wide", "narrow"), None),
        check_vma=False,
    )
```

```python
import jax
import jax.numpy as jnp
from jax import lax
from jax.experimental import pallas as pl
from jax.experimental.pallas import tpu as pltpu
from jax.sharding import PartitionSpec as P

SLOT_PER = 4
SIDE = 128
CHUNK = 256
F32 = jnp.float32
BF16 = jnp.bfloat16
VMEM = pl.BlockSpec(memory_space=pltpu.VMEM)
SMEM = pl.BlockSpec(memory_space=pltpu.SMEM)
ANY = pl.BlockSpec(memory_space=pl.ANY)
MIB = 1024 * 1024


def params(mib):
    return pltpu.CompilerParams(vmem_limit_bytes=mib * MIB)


def cost(flops, moved, transcendentals=0):
    return pl.CostEstimate(flops=flops, bytes_accessed=moved, transcendentals=transcendentals)


def dot(lhs, rhs):
    return jnp.dot(lhs, rhs, preferred_element_type=F32)


def side_state(peak, total):
    lane = lax.broadcasted_iota(jnp.int32, (peak.shape[0], SIDE), 1)
    return jnp.where(lane == 0, peak, jnp.where(lane == 1, total, 0.0))


def side_message(peak, total):
    lane = lax.broadcasted_iota(jnp.int32, (peak.shape[0], SIDE), 1)
    out = jnp.zeros((peak.shape[0], SIDE), F32)
    for index, value in enumerate((peak, total)):
        for piece in range(3):
            part = value.astype(BF16).astype(F32)
            out = jnp.where(lane == 3 * index + piece, part, out)
            value = value - part
    return out.astype(BF16)


def read_message(side):
    value = side.astype(F32)
    return (
        value[:, 0:1] + value[:, 1:2] + value[:, 2:3],
        value[:, 3:4] + value[:, 4:5] + value[:, 5:6],
    )


def gather_kernel(place, tokens, slot_params, logits, keep, side, send, held, table, sems):
    chunks = tokens.shape[0] // CHUNK
    slots = slot_params.shape[1]
    table_copy = pltpu.make_async_copy(slot_params, table, sems.at[chunks])
    table_copy.start()
    copies = [
        pltpu.make_async_copy(tokens.at[pl.ds(i * CHUNK, CHUNK)], held.at[pl.ds(i * CHUNK, CHUNK)], sems.at[i])
        for i in range(chunks)
    ]
    for copy in copies:
        copy.start()
    high = jnp.full((8, slots), -jnp.inf, F32)
    table_copy.wait()
    for i in range(chunks):
        copies[i].wait()
        part = dot(held[pl.ds(i * CHUNK, CHUNK), :], table[...])
        logits[pl.ds(i * CHUNK, CHUNK), :] = part
        high = jnp.maximum(high, jnp.max(part.reshape(CHUNK // 8, 8, slots), axis=0))
    peak = jnp.max(high, axis=0, keepdims=True)
    total = jnp.zeros((8, slots), F32)
    turned = []
    for i in range(chunks):
        weights = jnp.exp(logits[pl.ds(i * CHUNK, CHUNK), :] - peak)
        total = total + jnp.sum(weights.reshape(CHUNK // 8, 8, slots), axis=0)
        turned.append(weights.T.astype(BF16))
    sums = dot(jnp.concatenate(turned, axis=1), held[...])
    total = jnp.sum(total, axis=0, keepdims=True)
    peak = jnp.broadcast_to(peak, (8, slots)).T[:, 0:1]
    total = jnp.broadcast_to(total, (8, slots)).T[:, 0:1]
    half = sums.shape[1] // 2
    left, right = sums[:, :half], sums[:, half:]
    first = place[0] == 0
    keep[...] = jnp.where(first, left, right)
    side[...] = side_state(peak, total)
    send[:, :half] = jnp.where(first, right, left).astype(BF16)
    send[:, half:] = side_message(peak, total)


def merge(keep, side, received):
    width = keep.shape[1]
    peak_mine, total_mine = side[:, 0:1], side[:, 1:2]
    peak_other, total_other = read_message(received[:, width:])
    peak = jnp.maximum(peak_mine, peak_other)
    scale_mine, scale_other = jnp.exp(peak_mine - peak), jnp.exp(peak_other - peak)
    total = total_mine * scale_mine + total_other * scale_other
    sums = keep[...] * scale_mine + received[:, :width].astype(F32) * scale_other
    return sums, peak, total


def pair_kernel(keep, side, received, send):
    width = keep.shape[1]
    sums, peak, total = merge(keep, side, received)
    send[:, :width] = sums.astype(BF16)
    send[:, width:] = side_message(peak, total)


def merge_all_kernel(received, combine, keep, side, send):
    groups, width = received.shape[0], received.shape[2] - SIDE
    states = [read_message(received[g, :, width:]) for g in range(groups)]
    peak = states[0][0]
    for other, _ in states[1:]:
        peak = jnp.maximum(peak, other)
    total = jnp.zeros_like(peak)
    sums = jnp.zeros(keep.shape, F32)
    for g, (peak_other, total_other) in enumerate(states):
        scale = jnp.exp(peak_other - peak)
        total = total + total_other * scale
        sums = sums + received[g, :, :width].astype(F32) * scale
    keep[...] = sums
    side[...] = side_state(peak, total)
    send[:, :width] = sums.astype(BF16)
    send[:, width:] = side_message(peak, total)


def finish_kernel(keep, side, received, first_held, slot_in):
    sums, _, total = merge(keep, side, received)
    slot_in[...] = (sums / total).astype(BF16)


def step_kernel(keep, side, received, keep_out, side_out, send):
    width = keep.shape[1]
    sums, peak, total = merge(keep, side, received)
    keep_out[...] = sums
    side_out[...] = side_state(peak, total)
    send[:, :width] = sums.astype(BF16)
    send[:, width:] = side_message(peak, total)


def load_kernel(after, weights, held, sems):
    copies = [pltpu.make_async_copy(weights.at[e], held.at[e], sems.at[e]) for e in range(weights.shape[0])]
    for copy in copies:
        copy.start()
    for copy in copies:
        copy.wait()


def load_call(after, weights, room):
    return pl.pallas_call(
        load_kernel,
        out_shape=jax.ShapeDtypeStruct(weights.shape, weights.dtype),
        in_specs=[ANY, ANY],
        out_specs=VMEM,
        scratch_shapes=[pltpu.SemaphoreType.DMA((weights.shape[0],))],
        cost_estimate=cost(0, 2 * weights.size),
        compiler_params=params(room),
        name="load",
    )(after, weights)


def expert_kernel(place, mine, other, expert_in, expert_out, keep, send, held, sems):
    experts = expert_in.shape[0]
    copies = [pltpu.make_async_copy(expert_out.at[e], held.at[e], sems.at[e]) for e in range(experts)]
    for copy in copies:
        copy.start()
    half = mine.shape[1]
    first = place[0] == 0
    slot_in = jnp.concatenate(
        [jnp.where(first, mine[...], other[...]), jnp.where(first, other[...], mine[...])], axis=1
    )
    hidden = [jax.nn.gelu(dot(slot_in, expert_in[e])).astype(BF16) for e in range(experts)]
    row = lax.broadcasted_iota(jnp.int32, (mine.shape[0], 1), 0)
    result = jnp.zeros((mine.shape[0], expert_out.shape[2]), F32)
    for e in range(experts):
        copies[e].wait()
        result = jnp.where(row // SLOT_PER == e, dot(hidden[e], held[e]), result)
    left, right = result[:, :half], result[:, half:]
    keep[...] = jnp.where(first, left, right)
    send[...] = jnp.where(first, right, left).astype(BF16)


def combine_kernel(logits, after, combine):
    value = logits[...]
    weights = jnp.exp(value - jnp.max(value, axis=1, keepdims=True))
    combine[...] = (weights / jnp.sum(weights, axis=1, keepdims=True)).astype(BF16)


def mix_kernel(place, combine, slot_out, *refs):
    mixed, held, sems = refs[-3:]
    width = slot_out.shape[1]
    block = held.shape[0] // sems.shape[0]
    columns = pl.ds(pl.multiple_of(place[0] * width, width), width)
    copies = []
    for i in range(sems.shape[0]):
        rows = pl.ds(i * block, block)
        held[rows, :] = dot(combine[rows, :], slot_out[...]).astype(BF16)
        copies.append(pltpu.make_async_copy(held.at[rows], mixed.at[rows, columns], sems.at[i]))
        copies[-1].start()
    for copy in copies:
        copy.wait()


def mix_call(which, combine, slot_out, before=None):
    tokens, slots = combine.shape
    width = slot_out.shape[1]
    more = [] if before is None else [before]
    return pl.pallas_call(
        mix_kernel,
        out_shape=jax.ShapeDtypeStruct((tokens, 2 * width), BF16),
        in_specs=[SMEM, VMEM, VMEM] + [ANY] * len(more),
        out_specs=ANY,
        scratch_shapes=[pltpu.VMEM((tokens, width), BF16), pltpu.SemaphoreType.DMA((8,))],
        input_output_aliases={3: 0} if more else {},
        cost_estimate=cost(2 * tokens * slots * width, 2 * tokens * (width + slots)),
        compiler_params=params(16),
        name="mix",
    )(which, combine, slot_out, *more)


def exchange(value, axis, bit):
    return lax.ppermute(value, axis, [(i, i ^ bit) for i in range(lax.axis_size(axis))])


def later_bits(axis):
    found, bit = [], 2
    while bit < lax.axis_size(axis):
        found.append(bit)
        bit *= 2
    return found


def shards(tokens, slot_params, expert_in, expert_out):
    count, model = tokens.shape
    slots = slot_params.shape[1]
    groups = lax.axis_size("wide")
    rows = slots // groups
    half = model // 2
    place = (lax.axis_index("narrow") % 2).astype(jnp.int32).reshape(1)

    def state(height):
        return (
            jax.ShapeDtypeStruct((height, half), F32),
            jax.ShapeDtypeStruct((height, SIDE), F32),
            jax.ShapeDtypeStruct((height, half + SIDE), BF16),
        )

    logits, keep, side, send = pl.pallas_call(
        gather_kernel,
        out_shape=(jax.ShapeDtypeStruct((count, slots), F32),) + state(slots),
        in_specs=[SMEM, ANY, ANY],
        out_specs=(VMEM,) * 4,
        scratch_shapes=[
            pltpu.VMEM((count, model), BF16),
            pltpu.VMEM((model, slots), BF16),
            pltpu.SemaphoreType.DMA((count // CHUNK + 1,)),
        ],
        compiler_params=params(52),
        name="gather",
    )(place, tokens, slot_params)
    received = exchange(send, "narrow", 1)
    send = pl.pallas_call(
        pair_kernel,
        out_shape=state(slots)[2],
        in_specs=[VMEM] * 3,
        out_specs=VMEM,
        compiler_params=params(8),
        name="pair",
    )(keep, side, received)
    received = lax.all_to_all(send.reshape(groups, rows, -1), "wide", split_axis=0, concat_axis=0, tiled=True)
    combine = pl.pallas_call(
        combine_kernel,
        out_shape=jax.ShapeDtypeStruct((count, slots), BF16),
        in_specs=[VMEM, ANY],
        out_specs=VMEM,
        cost_estimate=cost(8 * count * slots, 6 * count * slots, count * slots),
        compiler_params=params(8),
        name="combine",
    )(logits, send)
    keep, side, send = pl.pallas_call(
        merge_all_kernel,
        out_shape=state(rows),
        in_specs=[VMEM, ANY],
        out_specs=(VMEM,) * 3,
        compiler_params=params(8),
        name="merge",
    )(received, combine)
    first_held = load_call(send, expert_in, 44)
    more = later_bits("narrow")
    for bit in more[:-1]:
        received = exchange(send, "narrow", bit)
        keep, side, send = pl.pallas_call(
            step_kernel,
            out_shape=state(rows),
            in_specs=[VMEM] * 3,
            out_specs=(VMEM,) * 3,
            compiler_params=params(8),
            name="step",
        )(keep, side, received)
    received = exchange(send, "narrow", more[-1])
    mine = pl.pallas_call(
        finish_kernel,
        out_shape=jax.ShapeDtypeStruct((rows, half), BF16),
        in_specs=[VMEM] * 3 + [ANY],
        out_specs=VMEM,
        compiler_params=params(8),
        name="finish",
    )(keep, side, received, first_held)
    other = exchange(mine, "narrow", 1)
    keep, send = pl.pallas_call(
        expert_kernel,
        out_shape=(jax.ShapeDtypeStruct((rows, half), F32), jax.ShapeDtypeStruct((rows, half), BF16)),
        in_specs=[SMEM, VMEM, VMEM, VMEM, ANY],
        out_specs=(VMEM, VMEM),
        scratch_shapes=[
            pltpu.VMEM(expert_out.shape, BF16),
            pltpu.SemaphoreType.DMA((expert_out.shape[0],)),
        ],
        compiler_params=params(42),
        name="experts",
    )(place, mine, other, first_held, expert_out)
    keep = keep + exchange(send, "narrow", 1).astype(F32)
    for bit in more:
        keep = keep + exchange(keep.astype(BF16), "narrow", bit).astype(F32)
    block = jnp.broadcast_to(keep.astype(BF16), (groups, rows, half))
    block = lax.all_to_all(block, "wide", split_axis=0, concat_axis=0, tiled=True).reshape(slots, half)
    other = exchange(block, "narrow", 1)
    mixed = mix_call(place, combine, block)
    return mix_call(1 - place, combine, other, mixed)


def solution(mesh):
    return jax.shard_map(
        shards,
        mesh=mesh,
        in_specs=(
            P(("wide", "narrow"), None),
            P(),
            P("wide", None, "narrow"),
            P("wide", "narrow", None),
        ),
        out_specs=P(("wide", "narrow"), None),
        check_vma=False,
    )
```

```python
import jax
import jax.numpy as jnp
from jax import lax
from jax.experimental import pallas as pl
from jax.experimental.pallas import tpu as pltpu
from jax.sharding import Mesh, PartitionSpec as P

SLOT_PER = 4
SIDE = 128
CHUNK = 256
F32 = jnp.float32
BF16 = jnp.bfloat16
VMEM = pl.BlockSpec(memory_space=pltpu.VMEM)
SMEM = pl.BlockSpec(memory_space=pltpu.SMEM)
HBM = pl.BlockSpec(memory_space=pltpu.HBM)
MIB = 1024 * 1024


def params(mib):
    return pltpu.CompilerParams(vmem_limit_bytes=mib * MIB)


def cost(flops, moved, transcendentals=0):
    return pl.CostEstimate(flops=flops, bytes_accessed=moved, transcendentals=transcendentals)


def in_hbm(value):
    return pltpu.with_memory_space_constraint(value, pltpu.HBM)


def dot(lhs, rhs):
    return jnp.dot(lhs, rhs, preferred_element_type=F32)


def side_state(peak, total):
    lane = lax.broadcasted_iota(jnp.int32, (peak.shape[0], SIDE), 1)
    return jnp.where(lane == 0, peak, jnp.where(lane == 1, total, 0.0))


def side_message(peak, total):
    lane = lax.broadcasted_iota(jnp.int32, (peak.shape[0], SIDE), 1)
    out = jnp.zeros((peak.shape[0], SIDE), F32)
    for index, value in enumerate((peak, total)):
        for piece in range(3):
            part = value.astype(BF16).astype(F32)
            out = jnp.where(lane == 3 * index + piece, part, out)
            value = value - part
    return out.astype(BF16)


def read_message(side):
    value = side.astype(F32)
    return (
        value[:, 0:1] + value[:, 1:2] + value[:, 2:3],
        value[:, 3:4] + value[:, 4:5] + value[:, 5:6],
    )


def gather_kernel(place, tokens, slot_params, logits, keep, side, send, held, table, own, sems, out_sems):
    chunks = tokens.shape[0] // CHUNK
    slots = slot_params.shape[1]
    spans = [pl.ds(i * CHUNK, CHUNK) for i in range(chunks)]
    table_copy = pltpu.make_async_copy(slot_params, table, sems.at[chunks])
    table_copy.start()
    copies = [pltpu.make_async_copy(tokens.at[span], held.at[span], sems.at[i]) for i, span in enumerate(spans)]
    for copy in copies:
        copy.start()
    high = jnp.full((8, slots), -jnp.inf, F32)
    table_copy.wait()
    out_copies = []
    for i, span in enumerate(spans):
        copies[i].wait()
        part = dot(held[span, :], table[...])
        own[span, :] = part
        high = jnp.maximum(high, jnp.max(part.reshape(CHUNK // 8, 8, slots), axis=0))
        out_copies.append(pltpu.make_async_copy(own.at[span], logits.at[span], out_sems.at[i]))
        out_copies[-1].start()
    peak = jnp.max(high, axis=0, keepdims=True)
    total = jnp.zeros((8, slots), F32)
    turned = []
    for span in spans:
        weights = jnp.exp(own[span, :] - peak)
        total = total + jnp.sum(weights.reshape(CHUNK // 8, 8, slots), axis=0)
        turned.append(weights.T.astype(BF16))
    sums = dot(jnp.concatenate(turned, axis=1), held[...])
    total = jnp.sum(total, axis=0, keepdims=True)
    peak = jnp.broadcast_to(peak, (8, slots)).T[:, 0:1]
    total = jnp.broadcast_to(total, (8, slots)).T[:, 0:1]
    half = sums.shape[1] // 2
    left, right = sums[:, :half], sums[:, half:]
    first = place[0] == 0
    keep[...] = jnp.where(first, left, right)
    side[...] = side_state(peak, total)
    send[:, :half] = jnp.where(first, right, left).astype(BF16)
    send[:, half:] = side_message(peak, total)
    for copy in out_copies:
        copy.wait()


def pair_kernel(keep, side, received, send):
    groups, rest, rows, _ = send.shape
    width = keep.shape[1]
    for g in range(groups):
        span = pl.ds(g * rows, rows)
        peak_mine, total_mine = side[span, 0:1], side[span, 1:2]
        peak_other, total_other = read_message(received[span, width:])
        peak = jnp.maximum(peak_mine, peak_other)
        scale_mine, scale_other = jnp.exp(peak_mine - peak), jnp.exp(peak_other - peak)
        total = total_mine * scale_mine + total_other * scale_other
        sums = keep[span, :] * scale_mine + received[span, :width].astype(F32) * scale_other
        sums, message = sums.astype(BF16), side_message(peak, total)
        for r in range(rest):
            send[g, r, :, :width] = sums
            send[g, r, :, width:] = message


def finish_kernel(received, combine, slot_in):
    width = slot_in.shape[1]
    states = [read_message(received[d, :, width:]) for d in range(received.shape[0])]
    peak = states[0][0]
    for other, _ in states[1:]:
        peak = jnp.maximum(peak, other)
    total = jnp.zeros_like(peak)
    sums = jnp.zeros(slot_in.shape, F32)
    for d, (peak_other, total_other) in enumerate(states):
        scale = jnp.exp(peak_other - peak)
        total = total + total_other * scale
        sums = sums + received[d, :, :width].astype(F32) * scale
    slot_in[...] = (sums / total).astype(BF16)


def expert_kernel(place, mine, other, expert_in, expert_out, keep, send, in_held, out_held, sems):
    experts, depth = expert_in.shape[:2]
    parts = 2
    span = depth // parts
    in_copies, out_copies = [], []
    for e in range(experts):
        in_copies.append(
            [
                pltpu.make_async_copy(
                    expert_in.at[e, pl.ds(p * span, span)], in_held.at[e, pl.ds(p * span, span)], sems.at[e, p]
                )
                for p in range(parts)
            ]
        )
        out_copies.append(pltpu.make_async_copy(expert_out.at[e], out_held.at[e], sems.at[e, parts]))
        for copy in in_copies[-1]:
            copy.start()
        out_copies[-1].start()
    half = mine.shape[1]
    first = place[0] == 0
    slot_in = jnp.concatenate(
        [jnp.where(first, mine[...], other[...]), jnp.where(first, other[...], mine[...])], axis=1
    )
    row = lax.broadcasted_iota(jnp.int32, (mine.shape[0], 1), 0)
    result = jnp.zeros((mine.shape[0], expert_out.shape[2]), F32)
    for e in range(experts):
        hidden = 0.0
        for p in range(parts):
            in_copies[e][p].wait()
            hidden = hidden + dot(slot_in[:, p * span : (p + 1) * span], in_held[e, pl.ds(p * span, span), :])
        hidden = jax.nn.gelu(hidden).astype(BF16)
        out_copies[e].wait()
        result = jnp.where(row // SLOT_PER == e, dot(hidden, out_held[e]), result)
    left, right = result[:, :half], result[:, half:]
    keep[...] = jnp.where(first, left, right)
    send[...] = jnp.where(first, right, left).astype(BF16)


def combine_kernel(logits, after, combine):
    value = logits[...]
    weights = jnp.exp(value - jnp.max(value, axis=1, keepdims=True))
    combine[...] = (weights / jnp.sum(weights, axis=1, keepdims=True)).astype(BF16)


def mix_kernel(place, combine, slot_out, *refs):
    mixed, held, sems = refs[-3:]
    width = slot_out.shape[1]
    block = held.shape[0] // sems.shape[0]
    columns = pl.ds(pl.multiple_of(place[0] * width, width), width)
    copies = []
    for i in range(sems.shape[0]):
        rows = pl.ds(i * block, block)
        held[rows, :] = dot(combine[rows, :], slot_out[...]).astype(BF16)
        copies.append(pltpu.make_async_copy(held.at[rows], mixed.at[rows, columns], sems.at[i]))
        copies[-1].start()
    for copy in copies:
        copy.wait()


def mix_call(which, combine, slot_out, before=None):
    tokens, slots = combine.shape
    width = slot_out.shape[1]
    more = [] if before is None else [before]
    return pl.pallas_call(
        mix_kernel,
        out_shape=jax.ShapeDtypeStruct((tokens, 2 * width), BF16),
        in_specs=[SMEM, VMEM, VMEM] + [HBM] * len(more),
        out_specs=HBM,
        scratch_shapes=[pltpu.VMEM((tokens, width), BF16), pltpu.SemaphoreType.DMA((8,))],
        input_output_aliases={3: 0} if more else {},
        cost_estimate=cost(2 * tokens * slots * width, 2 * tokens * (width + slots)),
        compiler_params=params(16),
        name="mix",
    )(which, combine, slot_out, *more)


def swap_pair(value):
    return lax.ppermute(value, "pair", [(0, 1), (1, 0)])


def shards(tokens, slot_params, expert_in, expert_out):
    count, model = tokens.shape
    slots = slot_params.shape[1]
    groups, rest = lax.axis_size("wide"), lax.axis_size("rest")
    rows = slots // groups
    half = model // 2
    place = lax.axis_index("pair").astype(jnp.int32).reshape(1)

    logits, keep, side, send = pl.pallas_call(
        gather_kernel,
        out_shape=(
            pltpu.HBM((count, slots), F32),
            jax.ShapeDtypeStruct((slots, half), F32),
            jax.ShapeDtypeStruct((slots, SIDE), F32),
            jax.ShapeDtypeStruct((slots, half + SIDE), BF16),
        ),
        in_specs=[SMEM, HBM, HBM],
        out_specs=(HBM, VMEM, VMEM, VMEM),
        scratch_shapes=[
            pltpu.VMEM((count, model), BF16),
            pltpu.VMEM((model, slots), BF16),
            pltpu.VMEM((count, slots), F32),
            pltpu.SemaphoreType.DMA((count // CHUNK + 1,)),
            pltpu.SemaphoreType.DMA((count // CHUNK,)),
        ],
        compiler_params=params(40),
        name="gather",
    )(place, in_hbm(tokens), in_hbm(slot_params))
    received = swap_pair(send)
    send = pl.pallas_call(
        pair_kernel,
        out_shape=jax.ShapeDtypeStruct((groups, rest, rows, half + SIDE), BF16),
        in_specs=[VMEM] * 3,
        out_specs=VMEM,
        compiler_params=params(16),
        name="pair",
    )(keep, side, received)
    received = lax.all_to_all(
        send.reshape(groups * rest, rows, -1), ("wide", "rest"), split_axis=0, concat_axis=0, tiled=True
    )
    block = 512
    combine = pl.pallas_call(
        combine_kernel,
        out_shape=jax.ShapeDtypeStruct((count, slots), BF16),
        grid=(count // block,),
        in_specs=[pl.BlockSpec((block, slots), lambda i: (i, 0)), HBM],
        out_specs=pl.BlockSpec((block, slots), lambda i: (i, 0)),
        cost_estimate=cost(8 * count * slots, 6 * count * slots, count * slots),
        compiler_params=params(16),
        name="combine",
    )(in_hbm(logits), send)
    mine = pl.pallas_call(
        finish_kernel,
        out_shape=jax.ShapeDtypeStruct((rows, half), BF16),
        in_specs=[VMEM, pl.BlockSpec(memory_space=pl.ANY)],
        out_specs=VMEM,
        compiler_params=params(16),
        name="finish",
    )(received, combine)
    other = swap_pair(mine)
    keep, send = pl.pallas_call(
        expert_kernel,
        out_shape=(jax.ShapeDtypeStruct((rows, half), F32), jax.ShapeDtypeStruct((rows, half), BF16)),
        in_specs=[SMEM, VMEM, VMEM, HBM, HBM],
        out_specs=(VMEM, VMEM),
        scratch_shapes=[
            pltpu.VMEM(expert_in.shape, BF16),
            pltpu.VMEM(expert_out.shape, BF16),
            pltpu.SemaphoreType.DMA((expert_in.shape[0], 3)),
        ],
        compiler_params=params(40),
        name="experts",
    )(place, mine, other, in_hbm(expert_in), in_hbm(expert_out))
    partial = (keep + swap_pair(send).astype(F32)).astype(BF16)
    partials = jnp.broadcast_to(partial, (groups * rest, rows, half))
    partials = lax.all_to_all(partials, ("wide", "rest"), split_axis=0, concat_axis=0, tiled=True)
    slot_out = jnp.sum(partials.reshape(groups, rest, rows, half).astype(F32), axis=1)
    slot_out = slot_out.astype(BF16).reshape(slots, half)
    other = swap_pair(slot_out)
    mixed = mix_call(place, combine, slot_out)
    return mix_call(1 - place, combine, other, mixed)


def solution(mesh):
    wide, narrow = mesh.shape["wide"], mesh.shape["narrow"]
    cut = Mesh(mesh.devices.reshape(wide, narrow // 2, 2), ("wide", "rest", "pair"))
    narrow_axes = ("rest", "pair")
    return jax.shard_map(
        shards,
        mesh=cut,
        in_specs=(
            P(("wide",) + narrow_axes, None),
            P(),
            P("wide", None, narrow_axes),
            P("wide", narrow_axes, None),
        ),
        out_specs=P(("wide",) + narrow_axes, None),
        check_vma=False,
    )
```

```python
import math

import jax
import jax.numpy as jnp
from jax import lax
from jax.experimental import pallas as pl
from jax.experimental.pallas import tpu as pltpu
from jax.sharding import Mesh, PartitionSpec as P

SLOT_PER = 4
SIDE = 128
CHUNK = 256
F32 = jnp.float32
BF16 = jnp.bfloat16
VMEM = pl.BlockSpec(memory_space=pltpu.VMEM)
SMEM = pl.BlockSpec(memory_space=pltpu.SMEM)
HBM = pl.BlockSpec(memory_space=pltpu.HBM)
MIB = 1024 * 1024


def params(mib):
    return pltpu.CompilerParams(vmem_limit_bytes=mib * MIB)


def cost(flops, moved, transcendentals=0):
    return pl.CostEstimate(flops=flops, bytes_accessed=moved, transcendentals=transcendentals)


def in_hbm(value):
    return pltpu.with_memory_space_constraint(value, pltpu.HBM)


def dot(lhs, rhs):
    return jnp.dot(lhs, rhs, preferred_element_type=F32)


def side_state(peak, total):
    lane = lax.broadcasted_iota(jnp.int32, (peak.shape[0], SIDE), 1)
    return jnp.where(lane == 0, peak, jnp.where(lane == 1, total, 0.0))


def side_message(peak, total):
    lane = lax.broadcasted_iota(jnp.int32, (peak.shape[0], SIDE), 1)
    out = jnp.zeros((peak.shape[0], SIDE), F32)
    for index, value in enumerate((peak, total)):
        for piece in range(3):
            part = value.astype(BF16).astype(F32)
            out = jnp.where(lane == 3 * index + piece, part, out)
            value = value - part
    return out.astype(BF16)


def read_message(side):
    value = side.astype(F32)
    return (
        value[:, 0:1] + value[:, 1:2] + value[:, 2:3],
        value[:, 3:4] + value[:, 4:5] + value[:, 5:6],
    )


def gather_kernel(place, tokens, slot_params, logits, keep, side, send, held, table, sems):
    chunks = tokens.shape[0] // CHUNK
    slots = slot_params.shape[1]
    spans = [pl.ds(i * CHUNK, CHUNK) for i in range(chunks)]
    table_copy = pltpu.make_async_copy(slot_params, table, sems.at[chunks])
    table_copy.start()
    copies = [pltpu.make_async_copy(tokens.at[span], held.at[span], sems.at[i]) for i, span in enumerate(spans)]
    for copy in copies:
        copy.start()
    high = jnp.full((8, slots), -jnp.inf, F32)
    table_copy.wait()
    for i, span in enumerate(spans):
        copies[i].wait()
        part = dot(held[span, :], table[...])
        logits[span, :] = part
        high = jnp.maximum(high, jnp.max(part.reshape(CHUNK // 8, 8, slots), axis=0))
    peak = jnp.max(high, axis=0, keepdims=True)
    total = jnp.zeros((8, slots), F32)
    turned = []
    for span in spans:
        weights = jnp.exp(logits[span, :] - peak)
        total = total + jnp.sum(weights.reshape(CHUNK // 8, 8, slots), axis=0)
        turned.append(weights.T.astype(BF16))
    sums = dot(jnp.concatenate(turned, axis=1), held[...])
    total = jnp.sum(total, axis=0, keepdims=True)
    peak = jnp.broadcast_to(peak, (8, slots)).T[:, 0:1]
    total = jnp.broadcast_to(total, (8, slots)).T[:, 0:1]
    half = sums.shape[1] // 2
    left, right = sums[:, :half], sums[:, half:]
    first = place[0] == 0
    keep[...] = jnp.where(first, left, right)
    side[...] = side_state(peak, total)
    send[:, :half] = jnp.where(first, right, left).astype(BF16)
    send[:, half:] = side_message(peak, total)


def pair_kernel(keep, side, received, combine, send):
    width = keep.shape[1]
    peak_mine, total_mine = side[:, 0:1], side[:, 1:2]
    peak_other, total_other = read_message(received[:, width:])
    peak = jnp.maximum(peak_mine, peak_other)
    scale_mine, scale_other = jnp.exp(peak_mine - peak), jnp.exp(peak_other - peak)
    total = total_mine * scale_mine + total_other * scale_other
    sums = keep[...] * scale_mine + received[:, :width].astype(F32) * scale_other
    send[:, :width] = sums.astype(BF16)
    send[:, width:] = side_message(peak, total)


def add_parts(parts, width):
    states = [read_message(part[:, width:]) for part in parts]
    peak = states[0][0]
    for other, _ in states[1:]:
        peak = jnp.maximum(peak, other)
    total = jnp.zeros_like(peak)
    sums = jnp.zeros((parts[0].shape[0], width), F32)
    for part, (peak_other, total_other) in zip(parts, states):
        scale = jnp.exp(peak_other - peak)
        total = total + total_other * scale
        sums = sums + part[:, :width].astype(F32) * scale
    return sums, peak, total


def merge_kernel(received, send):
    width = send.shape[1] - SIDE
    sums, peak, total = add_parts([received[g] for g in range(received.shape[0])], width)
    send[:, :width] = sums.astype(BF16)
    send[:, width:] = side_message(peak, total)


def finish_kernel(place, *refs):
    slot_in = refs[-1]
    half = slot_in.shape[1] // 2
    parts = (len(refs) - 2) // 2
    means = []
    for side in range(2):
        sums, _, total = add_parts([ref[...] for ref in refs[side * parts : (side + 1) * parts]], half)
        means.append((sums / total).astype(BF16))
    first = place[0] == 0
    slot_in[:, :half] = jnp.where(first, means[0], means[1])
    slot_in[:, half:] = jnp.where(first, means[1], means[0])


def load_kernel(after, weights, held, sems):
    copies = [pltpu.make_async_copy(weights.at[e], held.at[e], sems.at[e]) for e in range(held.shape[0])]
    for copy in copies:
        copy.start()
    for copy in copies:
        copy.wait()


def expert_kernel(place, slot_in, early, expert_in, expert_out, keep, send, in_held, out_held, sems):
    experts, ahead = expert_in.shape[0], early.shape[0]
    in_copies, out_copies = {}, {}
    for e in range(experts):
        if e >= ahead:
            in_copies[e] = pltpu.make_async_copy(expert_in.at[e], in_held.at[e - ahead], sems.at[0, e])
            in_copies[e].start()
        out_copies[e] = pltpu.make_async_copy(expert_out.at[e], out_held.at[e], sems.at[1, e])
        out_copies[e].start()
    row = lax.broadcasted_iota(jnp.int32, (slot_in.shape[0], 1), 0)
    result = jnp.zeros((slot_in.shape[0], expert_out.shape[2]), F32)
    hidden = [jax.nn.gelu(dot(slot_in[...], early[e])).astype(BF16) for e in range(ahead)]
    for e in range(experts):
        if e >= ahead:
            in_copies[e].wait()
            hidden.append(jax.nn.gelu(dot(slot_in[...], in_held[e - ahead])).astype(BF16))
        out_copies[e].wait()
        result = jnp.where(row // SLOT_PER == e, dot(hidden[e], out_held[e]), result)
    half = keep.shape[1]
    left, right = result[:, :half], result[:, half:]
    first = place[0] == 0
    keep[...] = jnp.where(first, left, right)
    send[...] = jnp.where(first, right, left).astype(BF16)


def combine_kernel(logits, after, combine):
    value = logits[...]
    weights = jnp.exp(value - jnp.max(value, axis=1, keepdims=True))
    combine[...] = (weights / jnp.sum(weights, axis=1, keepdims=True)).astype(BF16)


def mix_kernel(place, combine, slot_out, *refs):
    mixed, held, sems = refs[-3:]
    width = slot_out.shape[1]
    block = held.shape[0] // sems.shape[0]
    columns = pl.ds(pl.multiple_of(place[0] * width, width), width)
    copies = []
    for i in range(sems.shape[0]):
        rows = pl.ds(i * block, block)
        held[rows, :] = dot(combine[rows, :], slot_out[...]).astype(BF16)
        copies.append(pltpu.make_async_copy(held.at[rows], mixed.at[rows, columns], sems.at[i]))
        copies[-1].start()
    for copy in copies:
        copy.wait()


def mix_call(which, combine, slot_out, before=None):
    tokens, slots = combine.shape
    width = slot_out.shape[1]
    more = [] if before is None else [before]
    return pl.pallas_call(
        mix_kernel,
        out_shape=jax.ShapeDtypeStruct((tokens, 2 * width), BF16),
        in_specs=[SMEM, VMEM, VMEM] + [HBM] * len(more),
        out_specs=HBM,
        scratch_shapes=[pltpu.VMEM((tokens, width), BF16), pltpu.SemaphoreType.DMA((8,))],
        input_output_aliases={3: 0} if more else {},
        cost_estimate=cost(2 * tokens * slots * width, 2 * tokens * (width + slots)),
        compiler_params=params(16),
        name="mix",
    )(which, combine, slot_out, *more)


def move(value, axes, offsets):
    sizes = [lax.axis_size(axis) for axis in axes]
    moves = []
    for index in range(math.prod(sizes)):
        source, target, stride = index, 0, 1
        for size, offset in zip(reversed(sizes), reversed(offsets)):
            target += (source % size + offset) % size * stride
            source //= size
            stride *= size
        moves.append((index, target))
    return lax.ppermute(value, axes, moves)


def swap_pair(value):
    return move(value, ("pair",), (1,))


def shards(tokens, slot_params, expert_in, expert_out):
    count, model = tokens.shape
    slots = slot_params.shape[1]
    groups, rest = lax.axis_size("wide"), lax.axis_size("rest")
    rows = slots // groups
    half = model // 2
    place = lax.axis_index("pair").astype(jnp.int32).reshape(1)
    any_space = pl.BlockSpec(memory_space=pl.ANY)

    logits, keep, side, send = pl.pallas_call(
        gather_kernel,
        out_shape=(
            jax.ShapeDtypeStruct((count, slots), F32),
            jax.ShapeDtypeStruct((slots, half), F32),
            jax.ShapeDtypeStruct((slots, SIDE), F32),
            jax.ShapeDtypeStruct((slots, half + SIDE), BF16),
        ),
        in_specs=[SMEM, HBM, HBM],
        out_specs=(VMEM,) * 4,
        scratch_shapes=[
            pltpu.VMEM((count, model), BF16),
            pltpu.VMEM((model, slots), BF16),
            pltpu.SemaphoreType.DMA((count // CHUNK + 1,)),
        ],
        compiler_params=params(40),
        name="gather",
    )(place, in_hbm(tokens), in_hbm(slot_params))
    received = swap_pair(send)
    combine = pl.pallas_call(
        combine_kernel,
        out_shape=jax.ShapeDtypeStruct((count, slots), BF16),
        in_specs=[VMEM, any_space],
        out_specs=VMEM,
        cost_estimate=cost(8 * count * slots, 6 * count * slots, count * slots),
        compiler_params=params(16),
        name="combine",
    )(logits, send)
    send = pl.pallas_call(
        pair_kernel,
        out_shape=jax.ShapeDtypeStruct((slots, half + SIDE), BF16),
        in_specs=[VMEM] * 3 + [any_space],
        out_specs=VMEM,
        compiler_params=params(16),
        name="pair",
    )(keep, side, received, combine)
    received = lax.all_to_all(send.reshape(groups, rows, -1), "wide", split_axis=0, concat_axis=0, tiled=True)
    send = pl.pallas_call(
        merge_kernel,
        out_shape=jax.ShapeDtypeStruct((rows, half + SIDE), BF16),
        in_specs=[VMEM],
        out_specs=VMEM,
        compiler_params=params(16),
        name="merge",
    )(received)
    axes = ("rest", "pair")
    mine = [send] + [move(send, axes, (r, 0)) for r in range(1, rest)]
    others = [move(send, axes, (r, 1)) for r in reversed(range(rest))]
    ahead = expert_in.shape[0] // 2
    early = pl.pallas_call(
        load_kernel,
        out_shape=jax.ShapeDtypeStruct((ahead,) + expert_in.shape[1:], BF16),
        in_specs=[any_space, HBM],
        out_specs=VMEM,
        scratch_shapes=[pltpu.SemaphoreType.DMA((ahead,))],
        cost_estimate=cost(0, expert_in.size),
        compiler_params=params(16),
        name="load",
    )(send, in_hbm(expert_in))
    slot_in = pl.pallas_call(
        finish_kernel,
        out_shape=jax.ShapeDtypeStruct((rows, model), BF16),
        in_specs=[SMEM] + [VMEM] * (2 * rest) + [any_space],
        out_specs=VMEM,
        compiler_params=params(16),
        name="finish",
    )(place, *mine, *others, early)
    keep, send = pl.pallas_call(
        expert_kernel,
        out_shape=(jax.ShapeDtypeStruct((rows, half), F32), jax.ShapeDtypeStruct((rows, half), BF16)),
        in_specs=[SMEM, VMEM, VMEM, HBM, HBM],
        out_specs=(VMEM, VMEM),
        scratch_shapes=[
            pltpu.VMEM((expert_in.shape[0] - ahead,) + expert_in.shape[1:], BF16),
            pltpu.VMEM(expert_out.shape, BF16),
            pltpu.SemaphoreType.DMA((2, expert_in.shape[0])),
        ],
        compiler_params=params(40),
        name="experts",
    )(place, slot_in, early, in_hbm(expert_in), in_hbm(expert_out))
    partial = keep + swap_pair(send).astype(F32)
    travelling = partial.astype(BF16)
    for r in range(1, rest):
        partial = partial + move(travelling, ("rest",), (r,)).astype(F32)
    block = jnp.broadcast_to(partial.astype(BF16), (groups, rows, half))
    slot_out = lax.all_to_all(block, "wide", split_axis=0, concat_axis=0, tiled=True).reshape(slots, half)
    other = swap_pair(slot_out)
    mixed = mix_call(place, combine, slot_out)
    return mix_call(1 - place, combine, other, mixed)


def solution(mesh):
    wide, narrow = mesh.shape["wide"], mesh.shape["narrow"]
    cut = Mesh(mesh.devices.reshape(wide, narrow // 2, 2), ("wide", "rest", "pair"))
    narrow_axes = ("rest", "pair")
    return jax.shard_map(
        shards,
        mesh=cut,
        in_specs=(
            P(("wide",) + narrow_axes, None),
            P(),
            P("wide", None, narrow_axes),
            P("wide", narrow_axes, None),
        ),
        out_specs=P(("wide",) + narrow_axes, None),
        check_vma=False,
    )
```

```python
import functools
import math

import jax
import jax.numpy as jnp
from jax import lax
from jax.experimental import pallas as pl
from jax.experimental.pallas import tpu as pltpu
from jax.sharding import Mesh, PartitionSpec as P

SLOT_PER = 4
SIDE = 128
TOKEN_GROUPS = 4
F32 = jnp.float32
BF16 = jnp.bfloat16
VMEM = pl.BlockSpec(memory_space=pltpu.VMEM)
SMEM = pl.BlockSpec(memory_space=pltpu.SMEM)
HBM = pl.BlockSpec(memory_space=pltpu.HBM)
MIB = 1024 * 1024


def params(mib):
    return pltpu.CompilerParams(vmem_limit_bytes=mib * MIB)


def cost(flops, moved, transcendentals=0):
    return pl.CostEstimate(flops=flops, bytes_accessed=moved, transcendentals=transcendentals)


def in_hbm(value):
    return pltpu.with_memory_space_constraint(value, pltpu.HBM)


def dot(lhs, rhs):
    return jnp.dot(lhs, rhs, preferred_element_type=F32)


def side_state(peak, total):
    lane = lax.broadcasted_iota(jnp.int32, (peak.shape[0], SIDE), 1)
    return jnp.where(lane == 0, peak, jnp.where(lane == 1, total, 0.0))


def side_message(peak, total):
    lane = lax.broadcasted_iota(jnp.int32, (peak.shape[0], SIDE), 1)
    out = jnp.zeros((peak.shape[0], SIDE), F32)
    for index, value in enumerate((peak, total)):
        for piece in range(3):
            part = value.astype(BF16).astype(F32)
            out = jnp.where(lane == 3 * index + piece, part, out)
            value = value - part
    return out.astype(BF16)


def read_message(side):
    value = side.astype(F32)
    return (
        value[:, 0:1] + value[:, 1:2] + value[:, 2:3],
        value[:, 3:4] + value[:, 4:5] + value[:, 5:6],
    )


def gather_kernel(
    place, tokens, slot_params, expert_in, logits, keep, side, send, early, held, table, sums, sems, early_sems
):
    slots = slot_params.shape[1]
    groups = sums.shape[0]
    size = tokens.shape[0] // groups
    spans = [pl.ds(g * size, size) for g in range(groups)]
    table_copy = pltpu.make_async_copy(slot_params, table, sems.at[groups])
    table_copy.start()
    copies = [pltpu.make_async_copy(tokens.at[span], held.at[span], sems.at[g]) for g, span in enumerate(spans)]
    for copy in copies:
        copy.start()
    early_copies = [
        pltpu.make_async_copy(expert_in.at[e], early.at[e], early_sems.at[e]) for e in range(early.shape[0])
    ]
    for copy in early_copies:
        copy.start()
    table_copy.wait()
    parts, peaks, totals = [], [], []
    for g in range(groups + 1):
        if g < groups:
            copies[g].wait()
            parts.append(dot(held[spans[g], :], table[...]))
            logits[spans[g], :] = parts[g]
            peaks.append(jnp.max(parts[g], axis=0, keepdims=True))
        if g > 0:
            weights = jnp.exp(parts[g - 1] - peaks[g - 1])
            totals.append(jnp.sum(weights, axis=0, keepdims=True))
            sums[g - 1] = dot(weights.T.astype(BF16), held[spans[g - 1], :])
    peak = functools.reduce(jnp.maximum, peaks)
    scales = [jnp.exp(part - peak) for part in peaks]
    total = sum(scale * part for scale, part in zip(scales, totals))
    row = lax.broadcasted_iota(jnp.int32, (8, slots), 0)
    columns = jnp.zeros((8, slots), F32)
    for index, value in enumerate([peak, total] + scales):
        columns = jnp.where(row == index, value, columns)
    columns = columns.T
    peak, total = columns[:, 0:1], columns[:, 1:2]
    result = sum(columns[:, 2 + g : 3 + g] * sums[g] for g in range(groups))
    half = result.shape[1] // 2
    left, right = result[:, :half], result[:, half:]
    first = place[0] == 0
    keep[...] = jnp.where(first, left, right)
    side[...] = side_state(peak, total)
    send[:, :half] = jnp.where(first, right, left).astype(BF16)
    send[:, half:] = side_message(peak, total)
    for copy in early_copies:
        copy.wait()


def pair_kernel(keep, side, received, combine, send):
    width = keep.shape[1]
    peak_mine, total_mine = side[:, 0:1], side[:, 1:2]
    peak_other, total_other = read_message(received[:, width:])
    peak = jnp.maximum(peak_mine, peak_other)
    scale_mine, scale_other = jnp.exp(peak_mine - peak), jnp.exp(peak_other - peak)
    total = total_mine * scale_mine + total_other * scale_other
    sums = keep[...] * scale_mine + received[:, :width].astype(F32) * scale_other
    send[:, :width] = sums.astype(BF16)
    send[:, width:] = side_message(peak, total)


def add_parts(parts, width):
    states = [read_message(part[:, width:]) for part in parts]
    peak = states[0][0]
    for other, _ in states[1:]:
        peak = jnp.maximum(peak, other)
    total = jnp.zeros_like(peak)
    sums = jnp.zeros((parts[0].shape[0], width), F32)
    for part, (peak_other, total_other) in zip(parts, states):
        scale = jnp.exp(peak_other - peak)
        total = total + total_other * scale
        sums = sums + part[:, :width].astype(F32) * scale
    return sums, peak, total


def merge_kernel(received, send):
    width = send.shape[1] - SIDE
    sums, peak, total = add_parts([received[g] for g in range(received.shape[0])], width)
    send[:, :width] = sums.astype(BF16)
    send[:, width:] = side_message(peak, total)


def finish_kernel(place, *refs):
    slot_in = refs[-1]
    half = slot_in.shape[1] // 2
    parts = (len(refs) - 2) // 2
    means = []
    for side in range(2):
        sums, _, total = add_parts([ref[...] for ref in refs[side * parts : (side + 1) * parts]], half)
        means.append((sums / total).astype(BF16))
    first = place[0] == 0
    slot_in[:, :half] = jnp.where(first, means[0], means[1])
    slot_in[:, half:] = jnp.where(first, means[1], means[0])


def load_kernel(after, weights, held, sems):
    first = weights.shape[0] - held.shape[0]
    copies = [pltpu.make_async_copy(weights.at[first + e], held.at[e], sems.at[e]) for e in range(held.shape[0])]
    for copy in copies:
        copy.start()
    for copy in copies:
        copy.wait()


def expert_kernel(place, slot_in, early, later, expert_out, keep, send, held, sems):
    experts = expert_out.shape[0]
    copies = [pltpu.make_async_copy(expert_out.at[e], held.at[e], sems.at[e]) for e in range(experts)]
    for copy in copies:
        copy.start()
    weights = [early[e] for e in range(early.shape[0])] + [later[e] for e in range(later.shape[0])]
    hidden = [jax.nn.gelu(dot(slot_in[...], weight)).astype(BF16) for weight in weights]
    row = lax.broadcasted_iota(jnp.int32, (slot_in.shape[0], 1), 0)
    result = jnp.zeros((slot_in.shape[0], expert_out.shape[2]), F32)
    for e in range(experts):
        if e % 2 == 0:
            for copy in copies[e : e + 2]:
                copy.wait()
        result = jnp.where(row // SLOT_PER == e, dot(hidden[e], held[e]), result)
    half = keep.shape[1]
    left, right = result[:, :half], result[:, half:]
    first = place[0] == 0
    keep[...] = jnp.where(first, left, right)
    send[...] = jnp.where(first, right, left).astype(BF16)


def combine_kernel(logits, after, combine):
    value = logits[...]
    weights = jnp.exp(value - jnp.max(value, axis=1, keepdims=True))
    combine[...] = (weights / jnp.sum(weights, axis=1, keepdims=True)).astype(BF16)


def mix_kernel(place, combine, slot_out, mixed, rest, held, sems):
    width = slot_out.shape[1]
    tokens, done = combine.shape[0], held.shape[0]
    block = done // sems.shape[0]
    columns = pl.ds(pl.multiple_of(place[0] * width, width), width)
    copies = []
    for i in range(tokens // block):
        rows = pl.ds(i * block, block)
        value = dot(combine[rows, :], slot_out[...]).astype(BF16)
        if i < sems.shape[0]:
            held[rows, :] = value
            copies.append(pltpu.make_async_copy(held.at[rows], mixed.at[rows, columns], sems.at[i]))
            copies[-1].start()
        else:
            rest[pl.ds(i * block - done, block), :] = value
    for copy in copies:
        copy.wait()


def mix_other_kernel(place, combine, slot_out, rest, before, mixed, held, sems):
    width = slot_out.shape[1]
    blocks = sems.shape[0] - 1
    tokens = combine.shape[0]
    done = tokens - rest.shape[0]
    mine = pl.ds(pl.multiple_of(place[0] * width, width), width)
    other = pl.ds(pl.multiple_of((1 - place[0]) * width, width), width)
    copies = [pltpu.make_async_copy(rest, mixed.at[pl.ds(done, tokens - done), mine], sems.at[blocks])]
    copies[0].start()
    block = tokens // blocks
    for i in range(blocks):
        rows = pl.ds(i * block, block)
        held[rows, :] = dot(combine[rows, :], slot_out[...]).astype(BF16)
        copies.append(pltpu.make_async_copy(held.at[rows], mixed.at[rows, other], sems.at[i]))
        copies[-1].start()
    for copy in copies:
        copy.wait()


def move(value, axes, offsets):
    sizes = [lax.axis_size(axis) for axis in axes]
    moves = []
    for index in range(math.prod(sizes)):
        source, target, stride = index, 0, 1
        for size, offset in zip(reversed(sizes), reversed(offsets)):
            target += (source % size + offset) % size * stride
            source //= size
            stride *= size
        moves.append((index, target))
    return lax.ppermute(value, axes, moves)


def swap_pair(value):
    return move(value, ("pair",), (1,))


def shards(tokens, slot_params, expert_in, expert_out):
    count, model = tokens.shape
    slots = slot_params.shape[1]
    groups, rest = lax.axis_size("wide"), lax.axis_size("rest")
    rows = slots // groups
    half = model // 2
    place = lax.axis_index("pair").astype(jnp.int32).reshape(1)
    any_space = pl.BlockSpec(memory_space=pl.ANY)

    ahead = expert_in.shape[0] // 2
    logits, keep, side, send, early = pl.pallas_call(
        gather_kernel,
        out_shape=(
            jax.ShapeDtypeStruct((count, slots), F32),
            jax.ShapeDtypeStruct((slots, half), F32),
            jax.ShapeDtypeStruct((slots, SIDE), F32),
            jax.ShapeDtypeStruct((slots, half + SIDE), BF16),
            jax.ShapeDtypeStruct((ahead,) + expert_in.shape[1:], BF16),
        ),
        in_specs=[SMEM, HBM, HBM, HBM],
        out_specs=(VMEM,) * 5,
        scratch_shapes=[
            pltpu.VMEM((count, model), BF16),
            pltpu.VMEM((model, slots), BF16),
            pltpu.VMEM((TOKEN_GROUPS, slots, model), F32),
            pltpu.SemaphoreType.DMA((TOKEN_GROUPS + 1,)),
            pltpu.SemaphoreType.DMA((ahead,)),
        ],
        compiler_params=params(32),
        name="gather",
    )(place, in_hbm(tokens), in_hbm(slot_params), in_hbm(expert_in))
    received = swap_pair(send)
    combine = pl.pallas_call(
        combine_kernel,
        out_shape=jax.ShapeDtypeStruct((count, slots), BF16),
        in_specs=[VMEM, any_space],
        out_specs=VMEM,
        cost_estimate=cost(8 * count * slots, 6 * count * slots, count * slots),
        compiler_params=params(16),
        name="combine",
    )(logits, send)
    send = pl.pallas_call(
        pair_kernel,
        out_shape=jax.ShapeDtypeStruct((slots, half + SIDE), BF16),
        in_specs=[VMEM] * 3 + [any_space],
        out_specs=VMEM,
        compiler_params=params(16),
        name="pair",
    )(keep, side, received, combine)
    received = lax.all_to_all(send.reshape(groups, rows, -1), "wide", split_axis=0, concat_axis=0, tiled=True)
    send = pl.pallas_call(
        merge_kernel,
        out_shape=jax.ShapeDtypeStruct((rows, half + SIDE), BF16),
        in_specs=[VMEM],
        out_specs=VMEM,
        compiler_params=params(16),
        name="merge",
    )(received)
    axes = ("rest", "pair")
    mine = [send] + [move(send, axes, (r, 0)) for r in range(1, rest)]
    others = [move(send, axes, (r, 1)) for r in reversed(range(rest))]
    later = pl.pallas_call(
        load_kernel,
        out_shape=jax.ShapeDtypeStruct((expert_in.shape[0] - ahead,) + expert_in.shape[1:], BF16),
        in_specs=[any_space, HBM],
        out_specs=VMEM,
        scratch_shapes=[pltpu.SemaphoreType.DMA((expert_in.shape[0] - ahead,))],
        cost_estimate=cost(0, expert_in.size),
        compiler_params=params(16),
        name="load",
    )(send, in_hbm(expert_in))
    slot_in = pl.pallas_call(
        finish_kernel,
        out_shape=jax.ShapeDtypeStruct((rows, model), BF16),
        in_specs=[SMEM] + [VMEM] * (2 * rest) + [any_space],
        out_specs=VMEM,
        compiler_params=params(16),
        name="finish",
    )(place, *mine, *others, later)
    keep, send = pl.pallas_call(
        expert_kernel,
        out_shape=(jax.ShapeDtypeStruct((rows, half), F32), jax.ShapeDtypeStruct((rows, half), BF16)),
        in_specs=[SMEM, VMEM, VMEM, VMEM, HBM],
        out_specs=(VMEM, VMEM),
        scratch_shapes=[
            pltpu.VMEM(expert_out.shape, BF16),
            pltpu.SemaphoreType.DMA((expert_out.shape[0],)),
        ],
        compiler_params=params(24),
        name="experts",
    )(place, slot_in, early, later, in_hbm(expert_out))
    partial = keep + swap_pair(send).astype(F32)
    travelling = partial.astype(BF16)
    for r in range(1, rest):
        partial = partial + move(travelling, ("rest",), (r,)).astype(F32)
    block = jnp.broadcast_to(partial.astype(BF16), (groups, rows, half))
    slot_out = lax.all_to_all(block, "wide", split_axis=0, concat_axis=0, tiled=True).reshape(slots, half)
    other = swap_pair(slot_out)
    done, blocks = count // 2, 8
    mixed, left = pl.pallas_call(
        mix_kernel,
        out_shape=(
            pltpu.HBM((count, model), BF16),
            jax.ShapeDtypeStruct((count - done, half), BF16),
        ),
        in_specs=[SMEM, VMEM, VMEM],
        out_specs=(HBM, VMEM),
        scratch_shapes=[pltpu.VMEM((done, half), BF16), pltpu.SemaphoreType.DMA((blocks // 2,))],
        cost_estimate=cost(2 * count * slots * half, 2 * count * (half + slots)),
        compiler_params=params(16),
        name="mix",
    )(place, combine, slot_out)
    return pl.pallas_call(
        mix_other_kernel,
        out_shape=jax.ShapeDtypeStruct((count, model), BF16),
        in_specs=[SMEM, VMEM, VMEM, VMEM, HBM],
        out_specs=HBM,
        scratch_shapes=[pltpu.VMEM((count, half), BF16), pltpu.SemaphoreType.DMA((blocks + 1,))],
        input_output_aliases={4: 0},
        cost_estimate=cost(2 * count * slots * half, 2 * count * (half + slots)),
        compiler_params=params(16),
        name="mix_other",
    )(place, combine, other, left, mixed)


def solution(mesh):
    wide, narrow = mesh.shape["wide"], mesh.shape["narrow"]
    cut = Mesh(mesh.devices.reshape(wide, narrow // 2, 2), ("wide", "rest", "pair"))
    narrow_axes = ("rest", "pair")
    return jax.shard_map(
        shards,
        mesh=cut,
        in_specs=(
            P(("wide",) + narrow_axes, None),
            P(),
            P("wide", None, narrow_axes),
            P("wide", narrow_axes, None),
        ),
        out_specs=P(("wide",) + narrow_axes, None),
        check_vma=False,
    )
```

```python
import functools
import math

import jax
import jax.numpy as jnp
from jax import lax
from jax.experimental import pallas as pl
from jax.experimental.pallas import tpu as pltpu
from jax.sharding import Mesh, PartitionSpec as P

SLOT_PER = 4
SIDE = 128
TOKEN_GROUPS = 4
F32 = jnp.float32
BF16 = jnp.bfloat16
VMEM = pl.BlockSpec(memory_space=pltpu.VMEM)
SMEM = pl.BlockSpec(memory_space=pltpu.SMEM)
HBM = pl.BlockSpec(memory_space=pltpu.HBM)
MIB = 1024 * 1024


def params(mib):
    return pltpu.CompilerParams(vmem_limit_bytes=mib * MIB)


def cost(flops, moved, transcendentals=0):
    return pl.CostEstimate(flops=flops, bytes_accessed=moved, transcendentals=transcendentals)


def in_hbm(value):
    return pltpu.with_memory_space_constraint(value, pltpu.HBM)


def dot(lhs, rhs):
    return jnp.dot(lhs, rhs, preferred_element_type=F32)


def side_state(peak, total):
    lane = lax.broadcasted_iota(jnp.int32, (peak.shape[0], SIDE), 1)
    return jnp.where(lane == 0, peak, jnp.where(lane == 1, total, 0.0))


def side_message(peak, total):
    lane = lax.broadcasted_iota(jnp.int32, (peak.shape[0], SIDE), 1)
    out = jnp.zeros((peak.shape[0], SIDE), F32)
    for index, value in enumerate((peak, total)):
        for piece in range(3):
            part = value.astype(BF16).astype(F32)
            out = jnp.where(lane == 3 * index + piece, part, out)
            value = value - part
    return out.astype(BF16)


def read_message(side):
    value = side.astype(F32)
    return (
        value[:, 0:1] + value[:, 1:2] + value[:, 2:3],
        value[:, 3:4] + value[:, 4:5] + value[:, 5:6],
    )


def gather_kernel(
    place, tokens, slot_params, expert_in, logits, keep, side, send, early, held, table, sums, sems, early_sems
):
    slots = slot_params.shape[1]
    groups = sums.shape[0]
    size = tokens.shape[0] // groups
    spans = [pl.ds(g * size, size) for g in range(groups)]
    table_copy = pltpu.make_async_copy(slot_params, table, sems.at[groups])
    table_copy.start()
    copies = [pltpu.make_async_copy(tokens.at[span], held.at[span], sems.at[g]) for g, span in enumerate(spans)]
    for copy in copies:
        copy.start()
    early_copies = [
        pltpu.make_async_copy(expert_in.at[e], early.at[e], early_sems.at[e]) for e in range(early.shape[0])
    ]
    table_copy.wait()
    parts, peaks, totals = [], [], []
    for g in range(groups + 1):
        if g < groups:
            copies[g].wait()
            if g == groups // 2:
                for copy in early_copies:
                    copy.start()
            parts.append(dot(held[spans[g], :], table[...]))
            logits[spans[g], :] = parts[g]
            peaks.append(jnp.max(parts[g], axis=0, keepdims=True))
        if g > 0:
            weights = jnp.exp(parts[g - 1] - peaks[g - 1])
            totals.append(jnp.sum(weights, axis=0, keepdims=True))
            sums[g - 1] = dot(weights.T.astype(BF16), held[spans[g - 1], :])
    peak = functools.reduce(jnp.maximum, peaks)
    scales = [jnp.exp(part - peak) for part in peaks]
    total = sum(scale * part for scale, part in zip(scales, totals))
    row = lax.broadcasted_iota(jnp.int32, (8, slots), 0)
    columns = jnp.zeros((8, slots), F32)
    for index, value in enumerate([peak, total] + scales):
        columns = jnp.where(row == index, value, columns)
    columns = columns.T
    peak, total = columns[:, 0:1], columns[:, 1:2]
    result = sum(columns[:, 2 + g : 3 + g] * sums[g] for g in range(groups))
    half = result.shape[1] // 2
    left, right = result[:, :half], result[:, half:]
    first = place[0] == 0
    keep[...] = jnp.where(first, left, right)
    side[...] = side_state(peak, total)
    send[:, :half] = jnp.where(first, right, left).astype(BF16)
    send[:, half:] = side_message(peak, total)
    for copy in early_copies:
        copy.wait()


def pair_kernel(keep, side, received, combine, send):
    width = keep.shape[1]
    peak_mine, total_mine = side[:, 0:1], side[:, 1:2]
    peak_other, total_other = read_message(received[:, width:])
    peak = jnp.maximum(peak_mine, peak_other)
    scale_mine, scale_other = jnp.exp(peak_mine - peak), jnp.exp(peak_other - peak)
    total = total_mine * scale_mine + total_other * scale_other
    sums = keep[...] * scale_mine + received[:, :width].astype(F32) * scale_other
    send[:, :width] = sums.astype(BF16)
    send[:, width:] = side_message(peak, total)


def add_parts(parts, width):
    states = [read_message(part[:, width:]) for part in parts]
    peak = states[0][0]
    for other, _ in states[1:]:
        peak = jnp.maximum(peak, other)
    total = jnp.zeros_like(peak)
    sums = jnp.zeros((parts[0].shape[0], width), F32)
    for part, (peak_other, total_other) in zip(parts, states):
        scale = jnp.exp(peak_other - peak)
        total = total + total_other * scale
        sums = sums + part[:, :width].astype(F32) * scale
    return sums, peak, total


def merge_kernel(received, send):
    width = send.shape[1] - SIDE
    sums, peak, total = add_parts([received[g] for g in range(received.shape[0])], width)
    send[:, :width] = sums.astype(BF16)
    send[:, width:] = side_message(peak, total)


def finish_kernel(place, *refs):
    slot_in = refs[-1]
    half = slot_in.shape[1] // 2
    parts = (len(refs) - 2) // 2
    means = []
    for side in range(2):
        sums, _, total = add_parts([ref[...] for ref in refs[side * parts : (side + 1) * parts]], half)
        means.append((sums / total).astype(BF16))
    first = place[0] == 0
    slot_in[:, :half] = jnp.where(first, means[0], means[1])
    slot_in[:, half:] = jnp.where(first, means[1], means[0])


def load_kernel(after, weights, held, sems):
    first = weights.shape[0] - held.shape[0]
    copies = [pltpu.make_async_copy(weights.at[first + e], held.at[e], sems.at[e]) for e in range(held.shape[0])]
    for copy in copies:
        copy.start()
    for copy in copies:
        copy.wait()


def second_product(hidden, weights):
    row = lax.broadcasted_iota(jnp.int32, (hidden[0].shape[0], 1), 0)
    result = 0.0
    for e, value in enumerate(hidden):
        result = jnp.where(row // SLOT_PER == e, dot(value, weights[e]), result)
    return result


def expert_kernel(place, slot_in, early, later, expert_out, hidden, own, send, held, sems):
    experts, half = expert_out.shape[0], own.shape[2]
    copies = []
    for target, side in ((held, 1 - place[0]), (own, place[0])):
        columns = pl.ds(pl.multiple_of(side * half, half), half)
        for e in range(experts):
            copies.append(
                pltpu.make_async_copy(expert_out.at[e, :, columns], target.at[e], sems.at[len(copies)])
            )
            copies[-1].start()
    weights = [early[e] for e in range(early.shape[0])] + [later[e] for e in range(later.shape[0])]
    values = [jax.nn.gelu(dot(slot_in[...], weight)).astype(BF16) for weight in weights]
    for e in range(experts):
        hidden[e] = values[e]
    for copy in copies[:experts]:
        copy.wait()
    send[...] = second_product(values, held).astype(BF16)
    for copy in copies[experts:]:
        copy.wait()


def own_kernel(hidden, own, after, keep):
    keep[...] = second_product([hidden[e] for e in range(hidden.shape[0])], own)


def combine_kernel(logits, after, combine):
    value = logits[...]
    weights = jnp.exp(value - jnp.max(value, axis=1, keepdims=True))
    combine[...] = (weights / jnp.sum(weights, axis=1, keepdims=True)).astype(BF16)


def mix_kernel(place, combine, slot_out, mixed, rest, held, sems):
    width = slot_out.shape[1]
    tokens, done = combine.shape[0], held.shape[0]
    block = done // sems.shape[0]
    columns = pl.ds(pl.multiple_of(place[0] * width, width), width)
    copies = []
    for i in range(tokens // block):
        rows = pl.ds(i * block, block)
        value = dot(combine[rows, :], slot_out[...]).astype(BF16)
        if i < sems.shape[0]:
            held[rows, :] = value
            copies.append(pltpu.make_async_copy(held.at[rows], mixed.at[rows, columns], sems.at[i]))
            copies[-1].start()
        else:
            rest[pl.ds(i * block - done, block), :] = value
    for copy in copies:
        copy.wait()


def mix_other_kernel(place, combine, slot_out, rest, before, mixed, held, sems):
    width = slot_out.shape[1]
    blocks = sems.shape[0] - 1
    tokens = combine.shape[0]
    done = tokens - rest.shape[0]
    mine = pl.ds(pl.multiple_of(place[0] * width, width), width)
    other = pl.ds(pl.multiple_of((1 - place[0]) * width, width), width)
    copies = [pltpu.make_async_copy(rest, mixed.at[pl.ds(done, tokens - done), mine], sems.at[blocks])]
    copies[0].start()
    block = tokens // blocks
    for i in range(blocks):
        rows = pl.ds(i * block, block)
        held[rows, :] = dot(combine[rows, :], slot_out[...]).astype(BF16)
        copies.append(pltpu.make_async_copy(held.at[rows], mixed.at[rows, other], sems.at[i]))
        copies[-1].start()
    for copy in copies:
        copy.wait()


def move(value, axes, offsets):
    sizes = [lax.axis_size(axis) for axis in axes]
    moves = []
    for index in range(math.prod(sizes)):
        source, target, stride = index, 0, 1
        for size, offset in zip(reversed(sizes), reversed(offsets)):
            target += (source % size + offset) % size * stride
            source //= size
            stride *= size
        moves.append((index, target))
    return lax.ppermute(value, axes, moves)


def swap_pair(value):
    return move(value, ("pair",), (1,))


def shards(tokens, slot_params, expert_in, expert_out):
    count, model = tokens.shape
    slots = slot_params.shape[1]
    groups, rest = lax.axis_size("wide"), lax.axis_size("rest")
    rows = slots // groups
    half = model // 2
    place = lax.axis_index("pair").astype(jnp.int32).reshape(1)
    any_space = pl.BlockSpec(memory_space=pl.ANY)

    ahead = expert_in.shape[0] // 2
    logits, keep, side, send, early = pl.pallas_call(
        gather_kernel,
        out_shape=(
            jax.ShapeDtypeStruct((count, slots), F32),
            jax.ShapeDtypeStruct((slots, half), F32),
            jax.ShapeDtypeStruct((slots, SIDE), F32),
            jax.ShapeDtypeStruct((slots, half + SIDE), BF16),
            jax.ShapeDtypeStruct((ahead,) + expert_in.shape[1:], BF16),
        ),
        in_specs=[SMEM, HBM, HBM, HBM],
        out_specs=(VMEM,) * 5,
        scratch_shapes=[
            pltpu.VMEM((count, model), BF16),
            pltpu.VMEM((model, slots), BF16),
            pltpu.VMEM((TOKEN_GROUPS, slots, model), F32),
            pltpu.SemaphoreType.DMA((TOKEN_GROUPS + 1,)),
            pltpu.SemaphoreType.DMA((ahead,)),
        ],
        compiler_params=params(32),
        name="gather",
    )(place, in_hbm(tokens), in_hbm(slot_params), in_hbm(expert_in))
    received = swap_pair(send)
    combine = pl.pallas_call(
        combine_kernel,
        out_shape=jax.ShapeDtypeStruct((count, slots), BF16),
        in_specs=[VMEM, any_space],
        out_specs=VMEM,
        cost_estimate=cost(8 * count * slots, 6 * count * slots, count * slots),
        compiler_params=params(16),
        name="combine",
    )(logits, send)
    send = pl.pallas_call(
        pair_kernel,
        out_shape=jax.ShapeDtypeStruct((slots, half + SIDE), BF16),
        in_specs=[VMEM] * 3 + [any_space],
        out_specs=VMEM,
        compiler_params=params(16),
        name="pair",
    )(keep, side, received, combine)
    received = lax.all_to_all(send.reshape(groups, rows, -1), "wide", split_axis=0, concat_axis=0, tiled=True)
    send = pl.pallas_call(
        merge_kernel,
        out_shape=jax.ShapeDtypeStruct((rows, half + SIDE), BF16),
        in_specs=[VMEM],
        out_specs=VMEM,
        compiler_params=params(16),
        name="merge",
    )(received)
    axes = ("rest", "pair")
    mine = [send] + [move(send, axes, (r, 0)) for r in range(1, rest)]
    others = [move(send, axes, (r, 1)) for r in reversed(range(rest))]
    later = pl.pallas_call(
        load_kernel,
        out_shape=jax.ShapeDtypeStruct((expert_in.shape[0] - ahead,) + expert_in.shape[1:], BF16),
        in_specs=[any_space, HBM],
        out_specs=VMEM,
        scratch_shapes=[pltpu.SemaphoreType.DMA((expert_in.shape[0] - ahead,))],
        cost_estimate=cost(0, expert_in.size),
        compiler_params=params(16),
        name="load",
    )(send, in_hbm(expert_in))
    slot_in = pl.pallas_call(
        finish_kernel,
        out_shape=jax.ShapeDtypeStruct((rows, model), BF16),
        in_specs=[SMEM] + [VMEM] * (2 * rest) + [any_space],
        out_specs=VMEM,
        compiler_params=params(16),
        name="finish",
    )(place, *mine, *others, later)
    experts, units = expert_out.shape[:2]
    hidden, own, send = pl.pallas_call(
        expert_kernel,
        out_shape=(
            jax.ShapeDtypeStruct((experts, rows, units), BF16),
            jax.ShapeDtypeStruct((experts, units, half), BF16),
            jax.ShapeDtypeStruct((rows, half), BF16),
        ),
        in_specs=[SMEM, VMEM, VMEM, VMEM, HBM],
        out_specs=(VMEM,) * 3,
        scratch_shapes=[
            pltpu.VMEM((experts, units, half), BF16),
            pltpu.SemaphoreType.DMA((2 * experts,)),
        ],
        compiler_params=params(24),
        name="experts",
    )(place, slot_in, early, later, in_hbm(expert_out))
    received = swap_pair(send)
    keep = pl.pallas_call(
        own_kernel,
        out_shape=jax.ShapeDtypeStruct((rows, half), F32),
        in_specs=[VMEM, VMEM, any_space],
        out_specs=VMEM,
        cost_estimate=cost(2 * rows * units * half * experts, 2 * experts * units * half),
        compiler_params=params(16),
        name="own",
    )(hidden, own, send)
    partial = (keep + received.astype(F32)).astype(BF16)
    partials = jnp.broadcast_to(partial, (groups * rest, rows, half))
    partials = lax.all_to_all(partials, ("wide", "rest"), split_axis=0, concat_axis=0, tiled=True)
    slot_out = jnp.sum(partials.reshape(groups, rest, rows, half).astype(F32), axis=1)
    slot_out = slot_out.astype(BF16).reshape(slots, half)
    other = swap_pair(slot_out)
    done, blocks = count // 2, 8
    mixed, left = pl.pallas_call(
        mix_kernel,
        out_shape=(
            pltpu.HBM((count, model), BF16),
            jax.ShapeDtypeStruct((count - done, half), BF16),
        ),
        in_specs=[SMEM, VMEM, VMEM],
        out_specs=(HBM, VMEM),
        scratch_shapes=[pltpu.VMEM((done, half), BF16), pltpu.SemaphoreType.DMA((blocks // 2,))],
        cost_estimate=cost(2 * count * slots * half, 2 * count * (half + slots)),
        compiler_params=params(16),
        name="mix",
    )(place, combine, slot_out)
    return pl.pallas_call(
        mix_other_kernel,
        out_shape=jax.ShapeDtypeStruct((count, model), BF16),
        in_specs=[SMEM, VMEM, VMEM, VMEM, HBM],
        out_specs=HBM,
        scratch_shapes=[pltpu.VMEM((count, half), BF16), pltpu.SemaphoreType.DMA((blocks + 1,))],
        input_output_aliases={4: 0},
        cost_estimate=cost(2 * count * slots * half, 2 * count * (half + slots)),
        compiler_params=params(16),
        name="mix_other",
    )(place, combine, other, left, mixed)


def solution(mesh):
    wide, narrow = mesh.shape["wide"], mesh.shape["narrow"]
    cut = Mesh(mesh.devices.reshape(wide, narrow // 2, 2), ("wide", "rest", "pair"))
    narrow_axes = ("rest", "pair")
    return jax.shard_map(
        shards,
        mesh=cut,
        in_specs=(
            P(("wide",) + narrow_axes, None),
            P(),
            P("wide", None, narrow_axes),
            P("wide", narrow_axes, None),
        ),
        out_specs=P(("wide",) + narrow_axes, None),
        check_vma=False,
    )
```

```python
import functools
import math

import jax
import jax.numpy as jnp
from jax import lax
from jax.experimental import pallas as pl
from jax.experimental.pallas import tpu as pltpu
from jax.sharding import Mesh, PartitionSpec as P

SLOT_PER = 4
SIDE = 128
TOKEN_GROUPS = 4
F32 = jnp.float32
BF16 = jnp.bfloat16
VMEM = pl.BlockSpec(memory_space=pltpu.VMEM)
SMEM = pl.BlockSpec(memory_space=pltpu.SMEM)
HBM = pl.BlockSpec(memory_space=pltpu.HBM)
MIB = 1024 * 1024


def params(mib):
    return pltpu.CompilerParams(vmem_limit_bytes=mib * MIB)


def cost(flops, moved, transcendentals=0):
    return pl.CostEstimate(flops=flops, bytes_accessed=moved, transcendentals=transcendentals)


def in_hbm(value):
    return pltpu.with_memory_space_constraint(value, pltpu.HBM)


def dot(lhs, rhs):
    return jnp.dot(lhs, rhs, preferred_element_type=F32)


def side_state(peak, total):
    lane = lax.broadcasted_iota(jnp.int32, (peak.shape[0], SIDE), 1)
    return jnp.where(lane == 0, peak, jnp.where(lane == 1, total, 0.0))


def side_message(peak, total):
    lane = lax.broadcasted_iota(jnp.int32, (peak.shape[0], SIDE), 1)
    out = jnp.zeros((peak.shape[0], SIDE), F32)
    for index, value in enumerate((peak, total)):
        for piece in range(3):
            part = value.astype(BF16).astype(F32)
            out = jnp.where(lane == 3 * index + piece, part, out)
            value = value - part
    return out.astype(BF16)


def read_message(side):
    value = side.astype(F32)
    return (
        value[:, 0:1] + value[:, 1:2] + value[:, 2:3],
        value[:, 3:4] + value[:, 4:5] + value[:, 5:6],
    )


def gather_kernel(
    place, tokens, slot_params, logits, keep, side, send, held, table, sums, sems
):
    slots = slot_params.shape[1]
    groups = sums.shape[0]
    size = tokens.shape[0] // groups
    spans = [pl.ds(g * size, size) for g in range(groups)]
    table_copy = pltpu.make_async_copy(slot_params, table, sems.at[groups])
    table_copy.start()
    copies = [pltpu.make_async_copy(tokens.at[span], held.at[span], sems.at[g]) for g, span in enumerate(spans)]
    for copy in copies:
        copy.start()
    table_copy.wait()
    parts, peaks, totals = [], [], []
    for g in range(groups + 1):
        if g < groups:
            copies[g].wait()
            parts.append(dot(held[spans[g], :], table[...]))
            logits[spans[g], :] = parts[g]
            peaks.append(jnp.max(parts[g], axis=0, keepdims=True))
        if g > 0:
            weights = jnp.exp(parts[g - 1] - peaks[g - 1])
            totals.append(jnp.sum(weights, axis=0, keepdims=True))
            sums[g - 1] = dot(weights.T.astype(BF16), held[spans[g - 1], :])
    peak = functools.reduce(jnp.maximum, peaks)
    scales = [jnp.exp(part - peak) for part in peaks]
    total = sum(scale * part for scale, part in zip(scales, totals))
    row = lax.broadcasted_iota(jnp.int32, (8, slots), 0)
    columns = jnp.zeros((8, slots), F32)
    for index, value in enumerate([peak, total] + scales):
        columns = jnp.where(row == index, value, columns)
    columns = columns.T
    peak, total = columns[:, 0:1], columns[:, 1:2]
    result = sum(columns[:, 2 + g : 3 + g] * sums[g] for g in range(groups))
    half = result.shape[1] // 2
    left, right = result[:, :half], result[:, half:]
    first = place[0] == 0
    keep[...] = jnp.where(first, left, right)
    side[...] = side_state(peak, total)
    send[:, :half] = jnp.where(first, right, left).astype(BF16)
    send[:, half:] = side_message(peak, total)


def pair_kernel(keep, side, received, combine, send):
    width = keep.shape[1]
    peak_mine, total_mine = side[:, 0:1], side[:, 1:2]
    peak_other, total_other = read_message(received[:, width:])
    peak = jnp.maximum(peak_mine, peak_other)
    scale_mine, scale_other = jnp.exp(peak_mine - peak), jnp.exp(peak_other - peak)
    total = total_mine * scale_mine + total_other * scale_other
    sums = keep[...] * scale_mine + received[:, :width].astype(F32) * scale_other
    send[:, :width] = sums.astype(BF16)
    send[:, width:] = side_message(peak, total)


def add_parts(parts, width):
    states = [read_message(part[:, width:]) for part in parts]
    peak = states[0][0]
    for other, _ in states[1:]:
        peak = jnp.maximum(peak, other)
    total = jnp.zeros_like(peak)
    sums = jnp.zeros((parts[0].shape[0], width), F32)
    for part, (peak_other, total_other) in zip(parts, states):
        scale = jnp.exp(peak_other - peak)
        total = total + total_other * scale
        sums = sums + part[:, :width].astype(F32) * scale
    return sums, peak, total


def merge_kernel(received, send):
    width = send.shape[1] - SIDE
    sums, peak, total = add_parts([received[g] for g in range(received.shape[0])], width)
    send[:, :width] = sums.astype(BF16)
    send[:, width:] = side_message(peak, total)


def finish_kernel(place, *refs):
    slot_in = refs[-1]
    half = slot_in.shape[1] // 2
    parts = (len(refs) - 1) // 2
    means = []
    for side in range(2):
        sums, _, total = add_parts([ref[...] for ref in refs[side * parts : (side + 1) * parts]], half)
        means.append((sums / total).astype(BF16))
    first = place[0] == 0
    slot_in[:, :half] = jnp.where(first, means[0], means[1])
    slot_in[:, half:] = jnp.where(first, means[1], means[0])


def second_product(hidden, weights, columns):
    row = lax.broadcasted_iota(jnp.int32, (hidden[0].shape[0], 1), 0)
    result = 0.0
    for e, value in enumerate(hidden):
        result = jnp.where(row // SLOT_PER == e, dot(value, weights[e, :, columns]), result)
    return result


def column_half(side, half):
    return pl.ds(pl.multiple_of(side * half, half), half)


def expert_kernel(place, slot_in, expert_in, expert_out, hidden, send):
    values = []
    for e in range(expert_in.shape[0]):
        values.append(jax.nn.gelu(dot(slot_in[...], expert_in[e])).astype(BF16))
        hidden[e] = values[e]
    send[...] = second_product(values, expert_out, column_half(1 - place[0], send.shape[1])).astype(BF16)


def own_kernel(place, hidden, expert_out, after, keep):
    values = [hidden[e] for e in range(hidden.shape[0])]
    keep[...] = second_product(values, expert_out, column_half(place[0], keep.shape[1]))


def combine_kernel(logits, after, combine):
    value = logits[...]
    weights = jnp.exp(value - jnp.max(value, axis=1, keepdims=True))
    combine[...] = (weights / jnp.sum(weights, axis=1, keepdims=True)).astype(BF16)


def mix_kernel(place, combine, slot_out, mixed, rest, held, sems):
    width = slot_out.shape[1]
    tokens, done = combine.shape[0], held.shape[0]
    block = done // sems.shape[0]
    columns = pl.ds(pl.multiple_of(place[0] * width, width), width)
    copies = []
    for i in range(tokens // block):
        rows = pl.ds(i * block, block)
        value = dot(combine[rows, :], slot_out[...]).astype(BF16)
        if i < sems.shape[0]:
            held[rows, :] = value
            copies.append(pltpu.make_async_copy(held.at[rows], mixed.at[rows, columns], sems.at[i]))
            copies[-1].start()
        else:
            rest[pl.ds(i * block - done, block), :] = value
    for copy in copies:
        copy.wait()


def mix_other_kernel(place, combine, slot_out, rest, before, mixed, held, sems):
    width = slot_out.shape[1]
    blocks = sems.shape[0] - 1
    tokens = combine.shape[0]
    done = tokens - rest.shape[0]
    mine = pl.ds(pl.multiple_of(place[0] * width, width), width)
    other = pl.ds(pl.multiple_of((1 - place[0]) * width, width), width)
    copies = [pltpu.make_async_copy(rest, mixed.at[pl.ds(done, tokens - done), mine], sems.at[blocks])]
    copies[0].start()
    block = tokens // blocks
    for i in range(blocks):
        rows = pl.ds(i * block, block)
        held[rows, :] = dot(combine[rows, :], slot_out[...]).astype(BF16)
        copies.append(pltpu.make_async_copy(held.at[rows], mixed.at[rows, other], sems.at[i]))
        copies[-1].start()
    for copy in copies:
        copy.wait()


def move(value, axes, offsets):
    sizes = [lax.axis_size(axis) for axis in axes]
    moves = []
    for index in range(math.prod(sizes)):
        source, target, stride = index, 0, 1
        for size, offset in zip(reversed(sizes), reversed(offsets)):
            target += (source % size + offset) % size * stride
            source //= size
            stride *= size
        moves.append((index, target))
    return lax.ppermute(value, axes, moves)


def swap_pair(value):
    return move(value, ("pair",), (1,))


def shards(tokens, slot_params, expert_in, expert_out):
    count, model = tokens.shape
    slots = slot_params.shape[1]
    groups, rest = lax.axis_size("wide"), lax.axis_size("rest")
    rows = slots // groups
    half = model // 2
    place = lax.axis_index("pair").astype(jnp.int32).reshape(1)
    any_space = pl.BlockSpec(memory_space=pl.ANY)

    logits, keep, side, send = pl.pallas_call(
        gather_kernel,
        out_shape=(
            jax.ShapeDtypeStruct((count, slots), F32),
            jax.ShapeDtypeStruct((slots, half), F32),
            jax.ShapeDtypeStruct((slots, SIDE), F32),
            jax.ShapeDtypeStruct((slots, half + SIDE), BF16),
        ),
        in_specs=[SMEM, HBM, HBM],
        out_specs=(VMEM,) * 4,
        scratch_shapes=[
            pltpu.VMEM((count, model), BF16),
            pltpu.VMEM((model, slots), BF16),
            pltpu.VMEM((TOKEN_GROUPS, slots, model), F32),
            pltpu.SemaphoreType.DMA((TOKEN_GROUPS + 1,)),
        ],
        compiler_params=params(40),
        name="gather",
    )(place, in_hbm(tokens), in_hbm(slot_params))
    received = swap_pair(send)
    combine = pl.pallas_call(
        combine_kernel,
        out_shape=jax.ShapeDtypeStruct((count, slots), BF16),
        in_specs=[VMEM, any_space],
        out_specs=VMEM,
        cost_estimate=cost(8 * count * slots, 6 * count * slots, count * slots),
        compiler_params=params(16),
        name="combine",
    )(logits, send)
    send = pl.pallas_call(
        pair_kernel,
        out_shape=jax.ShapeDtypeStruct((slots, half + SIDE), BF16),
        in_specs=[VMEM] * 3 + [any_space],
        out_specs=VMEM,
        cost_estimate=cost(0, 6 * slots * model, 128 * slots * model),
        compiler_params=params(16),
        name="pair",
    )(keep, side, received, combine)
    received = lax.all_to_all(send.reshape(groups, rows, -1), "wide", split_axis=0, concat_axis=0, tiled=True)
    send = pl.pallas_call(
        merge_kernel,
        out_shape=jax.ShapeDtypeStruct((rows, half + SIDE), BF16),
        in_specs=[VMEM],
        out_specs=VMEM,
        compiler_params=params(16),
        name="merge",
    )(received)
    axes = ("rest", "pair")
    mine = [send] + [move(send, axes, (r, 0)) for r in range(1, rest)]
    others = [move(send, axes, (r, 1)) for r in reversed(range(rest))]
    slot_in = pl.pallas_call(
        finish_kernel,
        out_shape=jax.ShapeDtypeStruct((rows, model), BF16),
        in_specs=[SMEM] + [VMEM] * (2 * rest),
        out_specs=VMEM,
        compiler_params=params(16),
        name="finish",
    )(place, *mine, *others)
    experts, units = expert_out.shape[:2]
    hidden, send = pl.pallas_call(
        expert_kernel,
        out_shape=(
            jax.ShapeDtypeStruct((experts, rows, units), BF16),
            jax.ShapeDtypeStruct((rows, half), BF16),
        ),
        in_specs=[SMEM, VMEM, VMEM, VMEM],
        out_specs=(VMEM, VMEM),
        compiler_params=params(8),
        name="experts",
    )(place, slot_in, expert_in, expert_out)
    received = swap_pair(send)
    keep = pl.pallas_call(
        own_kernel,
        out_shape=jax.ShapeDtypeStruct((rows, half), F32),
        in_specs=[SMEM, VMEM, VMEM, any_space],
        out_specs=VMEM,
        cost_estimate=cost(2 * rows * units * half * experts, 2 * experts * units * half),
        compiler_params=params(8),
        name="own",
    )(place, hidden, expert_out, send)
    partial = (keep + received.astype(F32)).astype(BF16)
    partials = jnp.broadcast_to(partial, (groups * rest, rows, half))
    partials = lax.all_to_all(partials, ("wide", "rest"), split_axis=0, concat_axis=0, tiled=True)
    slot_out = jnp.sum(partials.reshape(groups, rest, rows, half).astype(F32), axis=1)
    slot_out = slot_out.astype(BF16).reshape(slots, half)
    other = swap_pair(slot_out)
    done, blocks = count // 2, 8
    mixed, left = pl.pallas_call(
        mix_kernel,
        out_shape=(
            pltpu.HBM((count, model), BF16),
            jax.ShapeDtypeStruct((count - done, half), BF16),
        ),
        in_specs=[SMEM, VMEM, VMEM],
        out_specs=(HBM, VMEM),
        scratch_shapes=[pltpu.VMEM((done, half), BF16), pltpu.SemaphoreType.DMA((blocks // 2,))],
        cost_estimate=cost(2 * count * slots * half, 2 * count * (half + slots)),
        compiler_params=params(16),
        name="mix",
    )(place, combine, slot_out)
    return pl.pallas_call(
        mix_other_kernel,
        out_shape=jax.ShapeDtypeStruct((count, model), BF16),
        in_specs=[SMEM, VMEM, VMEM, VMEM, HBM],
        out_specs=HBM,
        scratch_shapes=[pltpu.VMEM((count, half), BF16), pltpu.SemaphoreType.DMA((blocks + 1,))],
        input_output_aliases={4: 0},
        cost_estimate=cost(2 * count * slots * half, 2 * count * (half + slots)),
        compiler_params=params(16),
        name="mix_other",
    )(place, combine, other, left, mixed)


def solution(mesh):
    wide, narrow = mesh.shape["wide"], mesh.shape["narrow"]
    cut = Mesh(mesh.devices.reshape(wide, narrow // 2, 2), ("wide", "rest", "pair"))
    narrow_axes = ("rest", "pair")
    return jax.shard_map(
        shards,
        mesh=cut,
        in_specs=(
            P(("wide",) + narrow_axes, None),
            P(),
            P("wide", None, narrow_axes),
            P("wide", narrow_axes, None),
        ),
        out_specs=P(("wide",) + narrow_axes, None),
        check_vma=False,
    )
```

```python
import math

import jax
import jax.numpy as jnp
from jax import lax
from jax.experimental import pallas as pl
from jax.experimental.pallas import tpu as pltpu
from jax.sharding import Mesh, PartitionSpec as P

SLOT_PER = 4
SIDE = 128
CHUNK = 256
F32 = jnp.float32
BF16 = jnp.bfloat16
VMEM = pl.BlockSpec(memory_space=pltpu.VMEM)
SMEM = pl.BlockSpec(memory_space=pltpu.SMEM)
HBM = pl.BlockSpec(memory_space=pltpu.HBM)
MIB = 1024 * 1024


def params(mib):
    return pltpu.CompilerParams(vmem_limit_bytes=mib * MIB)


def cost(flops, moved, transcendentals=0):
    return pl.CostEstimate(flops=flops, bytes_accessed=moved, transcendentals=transcendentals)


def in_hbm(value):
    return pltpu.with_memory_space_constraint(value, pltpu.HBM)


def dot(lhs, rhs):
    return jnp.dot(lhs, rhs, preferred_element_type=F32)


def side_state(peak, total):
    lane = lax.broadcasted_iota(jnp.int32, (peak.shape[0], SIDE), 1)
    return jnp.where(lane == 0, peak, jnp.where(lane == 1, total, 0.0))


def side_message(peak, total):
    lane = lax.broadcasted_iota(jnp.int32, (peak.shape[0], SIDE), 1)
    out = jnp.zeros((peak.shape[0], SIDE), F32)
    for index, value in enumerate((peak, total)):
        for piece in range(3):
            part = value.astype(BF16).astype(F32)
            out = jnp.where(lane == 3 * index + piece, part, out)
            value = value - part
    return out.astype(BF16)


def read_message(side):
    value = side.astype(F32)
    return (
        value[:, 0:1] + value[:, 1:2] + value[:, 2:3],
        value[:, 3:4] + value[:, 4:5] + value[:, 5:6],
    )


def gather_kernel(place, tokens, slot_params, logits, keep, side, send, held, raw, table, sems):
    chunks = tokens.shape[0] // CHUNK
    spans = [pl.ds(i * CHUNK, CHUNK) for i in range(chunks)]
    table_copy = pltpu.make_async_copy(slot_params, raw, sems.at[chunks])
    table_copy.start()
    copies = [pltpu.make_async_copy(tokens.at[span], held.at[span], sems.at[i]) for i, span in enumerate(spans)]
    for copy in copies:
        copy.start()
    table_copy.wait()
    table[...] = raw[...].astype(F32).T.astype(BF16)
    high = None
    for copy, span in zip(copies, spans):
        copy.wait()
        part = lax.dot_general(table[...], held[span, :], (((1,), (1,)), ((), ())), preferred_element_type=F32)
        logits[:, span] = part
        high = part if high is None else jnp.maximum(high, part)
    peak = jnp.max(high, axis=1, keepdims=True)
    weights = jnp.exp(logits[...] - peak)
    total = jnp.sum(weights, axis=1, keepdims=True)
    result = dot(weights.astype(BF16), held[...])
    half = result.shape[1] // 2
    left, right = result[:, :half], result[:, half:]
    first = place[0] == 0
    keep[...] = jnp.where(first, left, right)
    side[...] = side_state(peak, total)
    send[:, :half] = jnp.where(first, right, left).astype(BF16)
    send[:, half:] = side_message(peak, total)


def pair_kernel(keep, side, received, combine, send):
    width = keep.shape[1]
    peak_mine, total_mine = side[:, 0:1], side[:, 1:2]
    peak_other, total_other = read_message(received[:, width:])
    peak = jnp.maximum(peak_mine, peak_other)
    scale_mine, scale_other = jnp.exp(peak_mine - peak), jnp.exp(peak_other - peak)
    total = total_mine * scale_mine + total_other * scale_other
    sums = keep[...] * scale_mine + received[:, :width].astype(F32) * scale_other
    send[:, :width] = sums.astype(BF16)
    send[:, width:] = side_message(peak, total)


def add_parts(parts, width):
    states = [read_message(part[:, width:]) for part in parts]
    peak = states[0][0]
    for other, _ in states[1:]:
        peak = jnp.maximum(peak, other)
    total = jnp.zeros_like(peak)
    sums = jnp.zeros((parts[0].shape[0], width), F32)
    for part, (peak_other, total_other) in zip(parts, states):
        scale = jnp.exp(peak_other - peak)
        total = total + total_other * scale
        sums = sums + part[:, :width].astype(F32) * scale
    return sums, peak, total


def merge_kernel(received, send):
    width = send.shape[1] - SIDE
    sums, peak, total = add_parts([received[g] for g in range(received.shape[0])], width)
    send[:, :width] = sums.astype(BF16)
    send[:, width:] = side_message(peak, total)


def finish_kernel(place, *refs):
    slot_in = refs[-1]
    half = slot_in.shape[1] // 2
    parts = (len(refs) - 1) // 2
    means = []
    for side in range(2):
        sums, _, total = add_parts([ref[...] for ref in refs[side * parts : (side + 1) * parts]], half)
        means.append((sums / total).astype(BF16))
    first = place[0] == 0
    slot_in[:, :half] = jnp.where(first, means[0], means[1])
    slot_in[:, half:] = jnp.where(first, means[1], means[0])


def second_product(hidden, weights, columns):
    row = lax.broadcasted_iota(jnp.int32, (hidden[0].shape[0], 1), 0)
    result = 0.0
    for e, value in enumerate(hidden):
        result = jnp.where(row // SLOT_PER == e, dot(value, weights[e, :, columns]), result)
    return result


def column_half(side, half):
    return pl.ds(pl.multiple_of(side * half, half), half)


def expert_kernel(place, slot_in, expert_in, expert_out, hidden, send):
    values = []
    for e in range(expert_in.shape[0]):
        values.append(jax.nn.gelu(dot(slot_in[...], expert_in[e])).astype(BF16))
        hidden[e] = values[e]
    send[...] = second_product(values, expert_out, column_half(1 - place[0], send.shape[1])).astype(BF16)


def own_kernel(place, hidden, expert_out, after, keep):
    values = [hidden[e] for e in range(hidden.shape[0])]
    keep[...] = second_product(values, expert_out, column_half(place[0], keep.shape[1]))


def combine_kernel(logits, after, combine):
    value = logits[...]
    weights = jnp.exp(value - jnp.max(value, axis=0, keepdims=True))
    combine[...] = (weights / jnp.sum(weights, axis=0, keepdims=True)).T.astype(BF16)


def mix_kernel(place, combine, slot_out, mixed, rest, held, sems):
    width = slot_out.shape[1]
    tokens, done = combine.shape[0], held.shape[0]
    block = done // sems.shape[0]
    columns = pl.ds(pl.multiple_of(place[0] * width, width), width)
    copies = []
    for i in range(tokens // block):
        rows = pl.ds(i * block, block)
        value = dot(combine[rows, :], slot_out[...]).astype(BF16)
        if i < sems.shape[0]:
            held[rows, :] = value
            copies.append(pltpu.make_async_copy(held.at[rows], mixed.at[rows, columns], sems.at[i]))
            copies[-1].start()
        else:
            rest[pl.ds(i * block - done, block), :] = value
    for copy in copies:
        copy.wait()


def mix_other_kernel(place, combine, slot_out, rest, before, mixed, held, sems):
    width = slot_out.shape[1]
    blocks = sems.shape[0] - 1
    tokens = combine.shape[0]
    done = tokens - rest.shape[0]
    mine = pl.ds(pl.multiple_of(place[0] * width, width), width)
    other = pl.ds(pl.multiple_of((1 - place[0]) * width, width), width)
    copies = [pltpu.make_async_copy(rest, mixed.at[pl.ds(done, tokens - done), mine], sems.at[blocks])]
    copies[0].start()
    block = tokens // blocks
    for i in range(blocks):
        rows = pl.ds(i * block, block)
        held[rows, :] = dot(combine[rows, :], slot_out[...]).astype(BF16)
        copies.append(pltpu.make_async_copy(held.at[rows], mixed.at[rows, other], sems.at[i]))
        copies[-1].start()
    for copy in copies:
        copy.wait()


def move(value, axes, offsets):
    sizes = [lax.axis_size(axis) for axis in axes]
    moves = []
    for index in range(math.prod(sizes)):
        source, target, stride = index, 0, 1
        for size, offset in zip(reversed(sizes), reversed(offsets)):
            target += (source % size + offset) % size * stride
            source //= size
            stride *= size
        moves.append((index, target))
    return lax.ppermute(value, axes, moves)


def swap_pair(value):
    return move(value, ("pair",), (1,))


def shards(tokens, slot_params, expert_in, expert_out):
    count, model = tokens.shape
    slots = slot_params.shape[1]
    groups, rest = lax.axis_size("wide"), lax.axis_size("rest")
    rows = slots // groups
    half = model // 2
    place = lax.axis_index("pair").astype(jnp.int32).reshape(1)
    any_space = pl.BlockSpec(memory_space=pl.ANY)

    logits, keep, side, send = pl.pallas_call(
        gather_kernel,
        out_shape=(
            jax.ShapeDtypeStruct((slots, count), F32),
            jax.ShapeDtypeStruct((slots, half), F32),
            jax.ShapeDtypeStruct((slots, SIDE), F32),
            jax.ShapeDtypeStruct((slots, half + SIDE), BF16),
        ),
        in_specs=[SMEM, HBM, HBM],
        out_specs=(VMEM,) * 4,
        scratch_shapes=[
            pltpu.VMEM((count, model), BF16),
            pltpu.VMEM((model, slots), BF16),
            pltpu.VMEM((slots, model), BF16),
            pltpu.SemaphoreType.DMA((count // CHUNK + 1,)),
        ],
        compiler_params=params(40),
        name="gather",
    )(place, in_hbm(tokens), in_hbm(slot_params))
    received = swap_pair(send)
    combine = pl.pallas_call(
        combine_kernel,
        out_shape=jax.ShapeDtypeStruct((count, slots), BF16),
        in_specs=[VMEM, any_space],
        out_specs=VMEM,
        cost_estimate=cost(8 * count * slots, 6 * count * slots, count * slots),
        compiler_params=params(16),
        name="combine",
    )(logits, send)
    send = pl.pallas_call(
        pair_kernel,
        out_shape=jax.ShapeDtypeStruct((slots, half + SIDE), BF16),
        in_specs=[VMEM] * 3 + [any_space],
        out_specs=VMEM,
        cost_estimate=cost(0, 6 * slots * model, 128 * slots * model),
        compiler_params=params(16),
        name="pair",
    )(keep, side, received, combine)
    received = lax.all_to_all(send.reshape(groups, rows, -1), "wide", split_axis=0, concat_axis=0, tiled=True)
    send = pl.pallas_call(
        merge_kernel,
        out_shape=jax.ShapeDtypeStruct((rows, half + SIDE), BF16),
        in_specs=[VMEM],
        out_specs=VMEM,
        compiler_params=params(16),
        name="merge",
    )(received)
    axes = ("rest", "pair")
    mine = [send] + [move(send, axes, (r, 0)) for r in range(1, rest)]
    others = [move(send, axes, (r, 1)) for r in reversed(range(rest))]
    slot_in = pl.pallas_call(
        finish_kernel,
        out_shape=jax.ShapeDtypeStruct((rows, model), BF16),
        in_specs=[SMEM] + [VMEM] * (2 * rest),
        out_specs=VMEM,
        compiler_params=params(16),
        name="finish",
    )(place, *mine, *others)
    experts, units = expert_out.shape[:2]
    hidden, send = pl.pallas_call(
        expert_kernel,
        out_shape=(
            jax.ShapeDtypeStruct((experts, rows, units), BF16),
            jax.ShapeDtypeStruct((rows, half), BF16),
        ),
        in_specs=[SMEM, VMEM, VMEM, VMEM],
        out_specs=(VMEM, VMEM),
        compiler_params=params(8),
        name="experts",
    )(place, slot_in, expert_in, expert_out)
    received = swap_pair(send)
    keep = pl.pallas_call(
        own_kernel,
        out_shape=jax.ShapeDtypeStruct((rows, half), F32),
        in_specs=[SMEM, VMEM, VMEM, any_space],
        out_specs=VMEM,
        cost_estimate=cost(2 * rows * units * half * experts, 2 * experts * units * half),
        compiler_params=params(8),
        name="own",
    )(place, hidden, expert_out, send)
    partial = (keep + received.astype(F32)).astype(BF16)
    partials = jnp.broadcast_to(partial, (groups * rest, rows, half))
    partials = lax.all_to_all(partials, ("wide", "rest"), split_axis=0, concat_axis=0, tiled=True)
    slot_out = jnp.sum(partials.reshape(groups, rest, rows, half).astype(F32), axis=1)
    slot_out = slot_out.astype(BF16).reshape(slots, half)
    other = swap_pair(slot_out)
    done, blocks = count // 2, 8
    mixed, left = pl.pallas_call(
        mix_kernel,
        out_shape=(
            pltpu.HBM((count, model), BF16),
            jax.ShapeDtypeStruct((count - done, half), BF16),
        ),
        in_specs=[SMEM, VMEM, VMEM],
        out_specs=(HBM, VMEM),
        scratch_shapes=[pltpu.VMEM((done, half), BF16), pltpu.SemaphoreType.DMA((blocks // 2,))],
        cost_estimate=cost(2 * count * slots * half, 2 * count * (half + slots)),
        compiler_params=params(16),
        name="mix",
    )(place, combine, slot_out)
    return pl.pallas_call(
        mix_other_kernel,
        out_shape=jax.ShapeDtypeStruct((count, model), BF16),
        in_specs=[SMEM, VMEM, VMEM, VMEM, HBM],
        out_specs=HBM,
        scratch_shapes=[pltpu.VMEM((count, half), BF16), pltpu.SemaphoreType.DMA((blocks + 1,))],
        input_output_aliases={4: 0},
        cost_estimate=cost(2 * count * slots * half, 2 * count * (half + slots)),
        compiler_params=params(16),
        name="mix_other",
    )(place, combine, other, left, mixed)


def solution(mesh):
    wide, narrow = mesh.shape["wide"], mesh.shape["narrow"]
    cut = Mesh(mesh.devices.reshape(wide, narrow // 2, 2), ("wide", "rest", "pair"))
    narrow_axes = ("rest", "pair")
    return jax.shard_map(
        shards,
        mesh=cut,
        in_specs=(
            P(("wide",) + narrow_axes, None),
            P(),
            P("wide", None, narrow_axes),
            P("wide", narrow_axes, None),
        ),
        out_specs=P(("wide",) + narrow_axes, None),
        check_vma=False,
    )
```

```python
import math

import jax
import jax.numpy as jnp
from jax import lax
from jax.experimental import pallas as pl
from jax.experimental.pallas import tpu as pltpu
from jax.sharding import Mesh, PartitionSpec as P

SLOT_PER = 4
SIDE = 128
CHUNK = 256
F32 = jnp.float32
BF16 = jnp.bfloat16
VMEM = pl.BlockSpec(memory_space=pltpu.VMEM)
SMEM = pl.BlockSpec(memory_space=pltpu.SMEM)
HBM = pl.BlockSpec(memory_space=pltpu.HBM)
MIB = 1024 * 1024


def params(mib):
    return pltpu.CompilerParams(vmem_limit_bytes=mib * MIB)


def cost(flops, moved, transcendentals=0):
    return pl.CostEstimate(flops=flops, bytes_accessed=moved, transcendentals=transcendentals)


def in_hbm(value):
    return pltpu.with_memory_space_constraint(value, pltpu.HBM)


def dot(lhs, rhs):
    return jnp.dot(lhs, rhs, preferred_element_type=F32)


def side_state(peak, total):
    lane = lax.broadcasted_iota(jnp.int32, (peak.shape[0], SIDE), 1)
    return jnp.where(lane == 0, peak, jnp.where(lane == 1, total, 0.0))


def side_message(peak, total):
    lane = lax.broadcasted_iota(jnp.int32, (peak.shape[0], SIDE), 1)
    out = jnp.zeros((peak.shape[0], SIDE), F32)
    for index, value in enumerate((peak, total)):
        for piece in range(3):
            part = value.astype(BF16).astype(F32)
            out = jnp.where(lane == 3 * index + piece, part, out)
            value = value - part
    return out.astype(BF16)


def read_message(side):
    value = side.astype(F32)
    return (
        value[:, 0:1] + value[:, 1:2] + value[:, 2:3],
        value[:, 3:4] + value[:, 4:5] + value[:, 5:6],
    )


def column_half(side, half):
    return pl.ds(pl.multiple_of(side * half, half), half)


def gather_kernel(place, tokens, slot_params, logits, turned, held, side, send, table, sems):
    chunks = tokens.shape[0] // CHUNK
    slots = slot_params.shape[1]
    spans = [pl.ds(i * CHUNK, CHUNK) for i in range(chunks)]
    table_copy = pltpu.make_async_copy(slot_params, table, sems.at[chunks])
    table_copy.start()
    copies = [pltpu.make_async_copy(tokens.at[span], held.at[span], sems.at[i]) for i, span in enumerate(spans)]
    for copy in copies:
        copy.start()
    high = jnp.full((8, slots), -jnp.inf, F32)
    table_copy.wait()
    for copy, span in zip(copies, spans):
        copy.wait()
        part = dot(held[span, :], table[...])
        logits[span, :] = part
        high = jnp.maximum(high, jnp.max(part.reshape(CHUNK // 8, 8, slots), axis=0))
    peak = jnp.max(high, axis=0, keepdims=True)
    total = jnp.zeros((8, slots), F32)
    columns = []
    for span in spans:
        weights = jnp.exp(logits[span, :] - peak)
        total = total + jnp.sum(weights.reshape(CHUNK // 8, 8, slots), axis=0)
        columns.append(weights.T.astype(BF16))
    weights = jnp.concatenate(columns, axis=1)
    turned[...] = weights
    half = held.shape[1] // 2
    send[:, :half] = dot(weights, held[:, column_half(1 - place[0], half)]).astype(BF16)
    total = jnp.sum(total, axis=0, keepdims=True)
    peak = jnp.broadcast_to(peak, (8, slots)).T[:, 0:1]
    total = jnp.broadcast_to(total, (8, slots)).T[:, 0:1]
    side[...] = side_state(peak, total)
    send[:, half:] = side_message(peak, total)


def own_sums_kernel(place, turned, held, after, keep):
    keep[...] = dot(turned[...], held[:, column_half(place[0], keep.shape[1])])


def pair_kernel(keep, side, received, send):
    width = keep.shape[1]
    peak_mine, total_mine = side[:, 0:1], side[:, 1:2]
    peak_other, total_other = read_message(received[:, width:])
    peak = jnp.maximum(peak_mine, peak_other)
    scale_mine, scale_other = jnp.exp(peak_mine - peak), jnp.exp(peak_other - peak)
    total = total_mine * scale_mine + total_other * scale_other
    sums = keep[...] * scale_mine + received[:, :width].astype(F32) * scale_other
    send[:, :width] = sums.astype(BF16)
    send[:, width:] = side_message(peak, total)


def add_parts(parts, width):
    states = [read_message(part[:, width:]) for part in parts]
    peak = states[0][0]
    for other, _ in states[1:]:
        peak = jnp.maximum(peak, other)
    total = jnp.zeros_like(peak)
    sums = jnp.zeros((parts[0].shape[0], width), F32)
    for part, (peak_other, total_other) in zip(parts, states):
        scale = jnp.exp(peak_other - peak)
        total = total + total_other * scale
        sums = sums + part[:, :width].astype(F32) * scale
    return sums, peak, total


def merge_kernel(received, send):
    width = send.shape[1] - SIDE
    sums, peak, total = add_parts([received[g] for g in range(received.shape[0])], width)
    send[:, :width] = sums.astype(BF16)
    send[:, width:] = side_message(peak, total)


def finish_kernel(place, *refs):
    slot_in = refs[-1]
    half = slot_in.shape[1] // 2
    parts = (len(refs) - 2) // 2
    means = []
    for side in range(2):
        sums, _, total = add_parts([ref[...] for ref in refs[side * parts : (side + 1) * parts]], half)
        means.append((sums / total).astype(BF16))
    first = place[0] == 0
    slot_in[:, :half] = jnp.where(first, means[0], means[1])
    slot_in[:, half:] = jnp.where(first, means[1], means[0])


def second_product(hidden, weights, columns):
    row = lax.broadcasted_iota(jnp.int32, (hidden[0].shape[0], 1), 0)
    result = 0.0
    for e, value in enumerate(hidden):
        result = jnp.where(row // SLOT_PER == e, dot(value, weights[e, :, columns]), result)
    return result


def expert_kernel(place, slot_in, expert_in, expert_out, hidden, send):
    values = []
    for e in range(expert_in.shape[0]):
        values.append(jax.nn.gelu(dot(slot_in[...], expert_in[e])).astype(BF16))
        hidden[e] = values[e]
    send[...] = second_product(values, expert_out, column_half(1 - place[0], send.shape[1])).astype(BF16)


def own_kernel(place, hidden, expert_out, after, keep):
    values = [hidden[e] for e in range(hidden.shape[0])]
    keep[...] = second_product(values, expert_out, column_half(place[0], keep.shape[1]))


def combine_kernel(logits, after, combine):
    value = logits[...]
    weights = jnp.exp(value - jnp.max(value, axis=1, keepdims=True))
    combine[...] = (weights / jnp.sum(weights, axis=1, keepdims=True)).astype(BF16)


def mix_kernel(place, combine, slot_out, mixed, rest, held, sems):
    width = slot_out.shape[1]
    tokens, done = combine.shape[0], held.shape[0]
    block = done // sems.shape[0]
    columns = pl.ds(pl.multiple_of(place[0] * width, width), width)
    copies = []
    for i in range(tokens // block):
        rows = pl.ds(i * block, block)
        value = dot(combine[rows, :], slot_out[...]).astype(BF16)
        if i < sems.shape[0]:
            held[rows, :] = value
            copies.append(pltpu.make_async_copy(held.at[rows], mixed.at[rows, columns], sems.at[i]))
            copies[-1].start()
        else:
            rest[pl.ds(i * block - done, block), :] = value
    for copy in copies:
        copy.wait()


def mix_other_kernel(place, combine, slot_out, rest, before, mixed, held, sems):
    width = slot_out.shape[1]
    blocks = sems.shape[0] - 1
    tokens = combine.shape[0]
    done = tokens - rest.shape[0]
    mine = pl.ds(pl.multiple_of(place[0] * width, width), width)
    other = pl.ds(pl.multiple_of((1 - place[0]) * width, width), width)
    copies = [pltpu.make_async_copy(rest, mixed.at[pl.ds(done, tokens - done), mine], sems.at[blocks])]
    copies[0].start()
    block = tokens // blocks
    for i in range(blocks):
        rows = pl.ds(i * block, block)
        held[rows, :] = dot(combine[rows, :], slot_out[...]).astype(BF16)
        copies.append(pltpu.make_async_copy(held.at[rows], mixed.at[rows, other], sems.at[i]))
        copies[-1].start()
    for copy in copies:
        copy.wait()


def move(value, axes, offsets):
    sizes = [lax.axis_size(axis) for axis in axes]
    moves = []
    for index in range(math.prod(sizes)):
        source, target, stride = index, 0, 1
        for size, offset in zip(reversed(sizes), reversed(offsets)):
            target += (source % size + offset) % size * stride
            source //= size
            stride *= size
        moves.append((index, target))
    return lax.ppermute(value, axes, moves)


def swap_pair(value):
    return move(value, ("pair",), (1,))


def shards(tokens, slot_params, expert_in, expert_out):
    count, model = tokens.shape
    slots = slot_params.shape[1]
    groups, rest = lax.axis_size("wide"), lax.axis_size("rest")
    rows = slots // groups
    half = model // 2
    place = lax.axis_index("pair").astype(jnp.int32).reshape(1)
    any_space = pl.BlockSpec(memory_space=pl.ANY)

    logits, turned, held, side, send = pl.pallas_call(
        gather_kernel,
        out_shape=(
            jax.ShapeDtypeStruct((count, slots), F32),
            jax.ShapeDtypeStruct((slots, count), BF16),
            jax.ShapeDtypeStruct((count, model), BF16),
            jax.ShapeDtypeStruct((slots, SIDE), F32),
            jax.ShapeDtypeStruct((slots, half + SIDE), BF16),
        ),
        in_specs=[SMEM, HBM, HBM],
        out_specs=(VMEM,) * 5,
        scratch_shapes=[pltpu.VMEM((model, slots), BF16), pltpu.SemaphoreType.DMA((count // CHUNK + 1,))],
        compiler_params=params(24),
        name="gather",
    )(place, in_hbm(tokens), in_hbm(slot_params))
    received = swap_pair(send)
    keep = pl.pallas_call(
        own_sums_kernel,
        out_shape=jax.ShapeDtypeStruct((slots, half), F32),
        in_specs=[SMEM, VMEM, VMEM, any_space],
        out_specs=VMEM,
        cost_estimate=cost(2 * slots * count * half, 2 * count * (half + slots)),
        compiler_params=params(16),
        name="own_sums",
    )(place, turned, held, send)
    send = pl.pallas_call(
        pair_kernel,
        out_shape=jax.ShapeDtypeStruct((slots, half + SIDE), BF16),
        in_specs=[VMEM] * 3,
        out_specs=VMEM,
        cost_estimate=cost(0, 6 * slots * model, 128 * slots * model),
        compiler_params=params(16),
        name="pair",
    )(keep, side, received)
    received = lax.all_to_all(send.reshape(groups, rows, -1), "wide", split_axis=0, concat_axis=0, tiled=True)
    send = pl.pallas_call(
        merge_kernel,
        out_shape=jax.ShapeDtypeStruct((rows, half + SIDE), BF16),
        in_specs=[VMEM],
        out_specs=VMEM,
        compiler_params=params(16),
        name="merge",
    )(received)
    axes = ("rest", "pair")
    mine = [send] + [move(send, axes, (r, 0)) for r in range(1, rest)]
    others = [move(send, axes, (r, 1)) for r in reversed(range(rest))]
    combine = pl.pallas_call(
        combine_kernel,
        out_shape=jax.ShapeDtypeStruct((count, slots), BF16),
        in_specs=[VMEM, any_space],
        out_specs=VMEM,
        cost_estimate=cost(8 * count * slots, 6 * count * slots, count * slots),
        compiler_params=params(16),
        name="combine",
    )(logits, send)
    slot_in = pl.pallas_call(
        finish_kernel,
        out_shape=jax.ShapeDtypeStruct((rows, model), BF16),
        in_specs=[SMEM] + [VMEM] * (2 * rest) + [any_space],
        out_specs=VMEM,
        compiler_params=params(16),
        name="finish",
    )(place, *mine, *others, combine)
    experts, units = expert_out.shape[:2]
    hidden, send = pl.pallas_call(
        expert_kernel,
        out_shape=(
            jax.ShapeDtypeStruct((experts, rows, units), BF16),
            jax.ShapeDtypeStruct((rows, half), BF16),
        ),
        in_specs=[SMEM, VMEM, VMEM, VMEM],
        out_specs=(VMEM, VMEM),
        compiler_params=params(8),
        name="experts",
    )(place, slot_in, expert_in, expert_out)
    received = swap_pair(send)
    keep = pl.pallas_call(
        own_kernel,
        out_shape=jax.ShapeDtypeStruct((rows, half), F32),
        in_specs=[SMEM, VMEM, VMEM, any_space],
        out_specs=VMEM,
        cost_estimate=cost(2 * rows * units * half * experts, 2 * experts * units * half),
        compiler_params=params(8),
        name="own",
    )(place, hidden, expert_out, send)
    partial = (keep + received.astype(F32)).astype(BF16)
    partials = jnp.broadcast_to(partial, (groups * rest, rows, half))
    partials = lax.all_to_all(partials, ("wide", "rest"), split_axis=0, concat_axis=0, tiled=True)
    slot_out = jnp.sum(partials.reshape(groups, rest, rows, half).astype(F32), axis=1)
    slot_out = slot_out.astype(BF16).reshape(slots, half)
    other = swap_pair(slot_out)
    done, blocks = count // 2, 8
    mixed, left = pl.pallas_call(
        mix_kernel,
        out_shape=(
            pltpu.HBM((count, model), BF16),
            jax.ShapeDtypeStruct((count - done, half), BF16),
        ),
        in_specs=[SMEM, VMEM, VMEM],
        out_specs=(HBM, VMEM),
        scratch_shapes=[pltpu.VMEM((done, half), BF16), pltpu.SemaphoreType.DMA((blocks // 2,))],
        cost_estimate=cost(2 * count * slots * half, 2 * count * (half + slots)),
        compiler_params=params(16),
        name="mix",
    )(place, combine, slot_out)
    return pl.pallas_call(
        mix_other_kernel,
        out_shape=jax.ShapeDtypeStruct((count, model), BF16),
        in_specs=[SMEM, VMEM, VMEM, VMEM, HBM],
        out_specs=HBM,
        scratch_shapes=[pltpu.VMEM((count, half), BF16), pltpu.SemaphoreType.DMA((blocks + 1,))],
        input_output_aliases={4: 0},
        cost_estimate=cost(2 * count * slots * half, 2 * count * (half + slots)),
        compiler_params=params(16),
        name="mix_other",
    )(place, combine, other, left, mixed)


def solution(mesh):
    wide, narrow = mesh.shape["wide"], mesh.shape["narrow"]
    cut = Mesh(mesh.devices.reshape(wide, narrow // 2, 2), ("wide", "rest", "pair"))
    narrow_axes = ("rest", "pair")
    return jax.shard_map(
        shards,
        mesh=cut,
        in_specs=(
            P(("wide",) + narrow_axes, None),
            P(),
            P("wide", None, narrow_axes),
            P("wide", narrow_axes, None),
        ),
        out_specs=P(("wide",) + narrow_axes, None),
        check_vma=False,
    )
```

```python
import math

import jax
import jax.numpy as jnp
from jax import lax
from jax.experimental import pallas as pl
from jax.experimental.pallas import tpu as pltpu
from jax.sharding import Mesh, PartitionSpec as P

SLOT_PER = 4
SIDE = 128
CHUNK = 256
F32 = jnp.float32
BF16 = jnp.bfloat16
VMEM = pl.BlockSpec(memory_space=pltpu.VMEM)
SMEM = pl.BlockSpec(memory_space=pltpu.SMEM)
HBM = pl.BlockSpec(memory_space=pltpu.HBM)
MIB = 1024 * 1024


def params(mib):
    return pltpu.CompilerParams(vmem_limit_bytes=mib * MIB)


def cost(flops, moved, transcendentals=0):
    return pl.CostEstimate(flops=flops, bytes_accessed=moved, transcendentals=transcendentals)


def in_hbm(value):
    return pltpu.with_memory_space_constraint(value, pltpu.HBM)


def dot(lhs, rhs):
    return jnp.dot(lhs, rhs, preferred_element_type=F32)


def side_state(peak, total):
    lane = lax.broadcasted_iota(jnp.int32, (peak.shape[0], SIDE), 1)
    return jnp.where(lane == 0, peak, jnp.where(lane == 1, total, 0.0))


def side_message(peak, total):
    lane = lax.broadcasted_iota(jnp.int32, (peak.shape[0], SIDE), 1)
    out = jnp.zeros((peak.shape[0], SIDE), F32)
    for index, value in enumerate((peak, total)):
        for piece in range(3):
            part = value.astype(BF16).astype(F32)
            out = jnp.where(lane == 3 * index + piece, part, out)
            value = value - part
    return out.astype(BF16)


def read_message(side):
    value = side.astype(F32)
    return (
        value[:, 0:1] + value[:, 1:2] + value[:, 2:3],
        value[:, 3:4] + value[:, 4:5] + value[:, 5:6],
    )


def column_half(side, half):
    return pl.ds(pl.multiple_of(side * half, half), half)


def gather_kernel(place, tokens, slot_params, logits, turned, held, side, send, table, sems):
    chunks = tokens.shape[0] // CHUNK
    slots = slot_params.shape[1]
    spans = [pl.ds(i * CHUNK, CHUNK) for i in range(chunks)]
    table_copy = pltpu.make_async_copy(slot_params, table, sems.at[chunks])
    table_copy.start()
    copies = [pltpu.make_async_copy(tokens.at[span], held.at[span], sems.at[i]) for i, span in enumerate(spans)]
    for copy in copies:
        copy.start()
    high = jnp.full((8, slots), -jnp.inf, F32)
    table_copy.wait()
    for copy, span in zip(copies, spans):
        copy.wait()
        part = dot(held[span, :], table[...])
        logits[span, :] = part
        high = jnp.maximum(high, jnp.max(part.reshape(CHUNK // 8, 8, slots), axis=0))
    peak = jnp.max(high, axis=0, keepdims=True)
    total = jnp.zeros((8, slots), F32)
    columns = []
    for span in spans:
        weights = jnp.exp(logits[span, :] - peak)
        total = total + jnp.sum(weights.reshape(CHUNK // 8, 8, slots), axis=0)
        columns.append(weights.astype(BF16).T)
    weights = jnp.concatenate(columns, axis=1)
    turned[...] = weights
    half = held.shape[1] // 2
    send[:, :half] = dot(weights, held[:, column_half(1 - place[0], half)]).astype(BF16)
    total = jnp.sum(total, axis=0, keepdims=True)
    peak = jnp.broadcast_to(peak, (8, slots)).T[:, 0:1]
    total = jnp.broadcast_to(total, (8, slots)).T[:, 0:1]
    side[...] = side_state(peak, total)
    send[:, half:] = side_message(peak, total)


def own_sums_kernel(place, turned, held, after, keep):
    keep[...] = dot(turned[...], held[:, column_half(place[0], keep.shape[1])])


def pair_kernel(keep, side, received, send):
    width = keep.shape[1]
    peak_mine, total_mine = side[:, 0:1], side[:, 1:2]
    peak_other, total_other = read_message(received[:, width:])
    peak = jnp.maximum(peak_mine, peak_other)
    scale_mine, scale_other = jnp.exp(peak_mine - peak), jnp.exp(peak_other - peak)
    total = total_mine * scale_mine + total_other * scale_other
    sums = keep[...] * scale_mine + received[:, :width].astype(F32) * scale_other
    send[:, :width] = sums.astype(BF16)
    send[:, width:] = side_message(peak, total)


def add_parts(parts, width):
    states = [read_message(part[:, width:]) for part in parts]
    peak = states[0][0]
    for other, _ in states[1:]:
        peak = jnp.maximum(peak, other)
    total = jnp.zeros_like(peak)
    sums = jnp.zeros((parts[0].shape[0], width), F32)
    for part, (peak_other, total_other) in zip(parts, states):
        scale = jnp.exp(peak_other - peak)
        total = total + total_other * scale
        sums = sums + part[:, :width].astype(F32) * scale
    return sums, peak, total


def merge_kernel(received, send):
    width = send.shape[1] - SIDE
    sums, peak, total = add_parts([received[g] for g in range(received.shape[0])], width)
    send[:, :width] = sums.astype(BF16)
    send[:, width:] = side_message(peak, total)


def finish_kernel(place, *refs):
    slot_in = refs[-1]
    half = slot_in.shape[1] // 2
    parts = (len(refs) - 2) // 2
    means = []
    for side in range(2):
        sums, _, total = add_parts([ref[...] for ref in refs[side * parts : (side + 1) * parts]], half)
        means.append((sums / total).astype(BF16))
    first = place[0] == 0
    slot_in[:, :half] = jnp.where(first, means[0], means[1])
    slot_in[:, half:] = jnp.where(first, means[1], means[0])


def second_product(hidden, weights, columns):
    row = lax.broadcasted_iota(jnp.int32, (hidden[0].shape[0], 1), 0)
    result = 0.0
    for e, value in enumerate(hidden):
        result = jnp.where(row // SLOT_PER == e, dot(value, weights[e, :, columns]), result)
    return result


def expert_kernel(place, slot_in, expert_in, expert_out, hidden, send):
    values = []
    for e in range(expert_in.shape[0]):
        values.append(jax.nn.gelu(dot(slot_in[...], expert_in[e])).astype(BF16))
        hidden[e] = values[e]
    send[...] = second_product(values, expert_out, column_half(1 - place[0], send.shape[1])).astype(BF16)


def own_kernel(place, hidden, expert_out, after, keep):
    values = [hidden[e] for e in range(hidden.shape[0])]
    keep[...] = second_product(values, expert_out, column_half(place[0], keep.shape[1]))


def combine_kernel(logits, after, combine):
    value = logits[...]
    weights = jnp.exp(value - jnp.max(value, axis=1, keepdims=True))
    combine[...] = (weights / jnp.sum(weights, axis=1, keepdims=True)).astype(BF16)


def mix_kernel(place, combine, slot_out, mixed, rest, held, sems):
    width = slot_out.shape[1]
    tokens, done = combine.shape[0], held.shape[0]
    block = done // sems.shape[0]
    columns = pl.ds(pl.multiple_of(place[0] * width, width), width)
    copies = []
    for i in range(tokens // block):
        rows = pl.ds(i * block, block)
        value = dot(combine[rows, :], slot_out[...]).astype(BF16)
        if i < sems.shape[0]:
            held[rows, :] = value
            copies.append(pltpu.make_async_copy(held.at[rows], mixed.at[rows, columns], sems.at[i]))
            copies[-1].start()
        else:
            rest[pl.ds(i * block - done, block), :] = value
    for copy in copies:
        copy.wait()


def mix_other_kernel(place, combine, slot_out, rest, before, mixed, held, sems):
    width = slot_out.shape[1]
    blocks = sems.shape[0] - 1
    tokens = combine.shape[0]
    done = tokens - rest.shape[0]
    mine = pl.ds(pl.multiple_of(place[0] * width, width), width)
    other = pl.ds(pl.multiple_of((1 - place[0]) * width, width), width)
    copies = [pltpu.make_async_copy(rest, mixed.at[pl.ds(done, tokens - done), mine], sems.at[blocks])]
    copies[0].start()
    block = tokens // blocks
    for i in range(blocks):
        rows = pl.ds(i * block, block)
        held[rows, :] = dot(combine[rows, :], slot_out[...]).astype(BF16)
        copies.append(pltpu.make_async_copy(held.at[rows], mixed.at[rows, other], sems.at[i]))
        copies[-1].start()
    for copy in copies:
        copy.wait()


def move(value, axes, offsets):
    sizes = [lax.axis_size(axis) for axis in axes]
    moves = []
    for index in range(math.prod(sizes)):
        source, target, stride = index, 0, 1
        for size, offset in zip(reversed(sizes), reversed(offsets)):
            target += (source % size + offset) % size * stride
            source //= size
            stride *= size
        moves.append((index, target))
    return lax.ppermute(value, axes, moves)


def swap_pair(value):
    return move(value, ("pair",), (1,))


def shards(tokens, slot_params, expert_in, expert_out):
    count, model = tokens.shape
    slots = slot_params.shape[1]
    groups, rest = lax.axis_size("wide"), lax.axis_size("rest")
    rows = slots // groups
    half = model // 2
    place = lax.axis_index("pair").astype(jnp.int32).reshape(1)
    any_space = pl.BlockSpec(memory_space=pl.ANY)

    logits, turned, held, side, send = pl.pallas_call(
        gather_kernel,
        out_shape=(
            jax.ShapeDtypeStruct((count, slots), F32),
            jax.ShapeDtypeStruct((slots, count), BF16),
            jax.ShapeDtypeStruct((count, model), BF16),
            jax.ShapeDtypeStruct((slots, SIDE), F32),
            jax.ShapeDtypeStruct((slots, half + SIDE), BF16),
        ),
        in_specs=[SMEM, HBM, HBM],
        out_specs=(VMEM,) * 5,
        scratch_shapes=[pltpu.VMEM((model, slots), BF16), pltpu.SemaphoreType.DMA((count // CHUNK + 1,))],
        compiler_params=params(24),
        name="gather",
    )(place, in_hbm(tokens), in_hbm(slot_params))
    received = swap_pair(send)
    keep = pl.pallas_call(
        own_sums_kernel,
        out_shape=jax.ShapeDtypeStruct((slots, half), F32),
        in_specs=[SMEM, VMEM, VMEM, any_space],
        out_specs=VMEM,
        cost_estimate=cost(2 * slots * count * half, 2 * count * (half + slots)),
        compiler_params=params(16),
        name="own_sums",
    )(place, turned, held, send)
    send = pl.pallas_call(
        pair_kernel,
        out_shape=jax.ShapeDtypeStruct((slots, half + SIDE), BF16),
        in_specs=[VMEM] * 3,
        out_specs=VMEM,
        cost_estimate=cost(0, 6 * slots * model, 128 * slots * model),
        compiler_params=params(16),
        name="pair",
    )(keep, side, received)
    received = lax.all_to_all(send.reshape(groups, rows, -1), "wide", split_axis=0, concat_axis=0, tiled=True)
    send = pl.pallas_call(
        merge_kernel,
        out_shape=jax.ShapeDtypeStruct((rows, half + SIDE), BF16),
        in_specs=[VMEM],
        out_specs=VMEM,
        compiler_params=params(16),
        name="merge",
    )(received)
    axes = ("rest", "pair")
    mine = [send] + [move(send, axes, (r, 0)) for r in range(1, rest)]
    others = [move(send, axes, (r, 1)) for r in reversed(range(rest))]
    combine = pl.pallas_call(
        combine_kernel,
        out_shape=jax.ShapeDtypeStruct((count, slots), BF16),
        in_specs=[VMEM, any_space],
        out_specs=VMEM,
        cost_estimate=cost(8 * count * slots, 6 * count * slots, count * slots),
        compiler_params=params(16),
        name="combine",
    )(logits, send)
    slot_in = pl.pallas_call(
        finish_kernel,
        out_shape=jax.ShapeDtypeStruct((rows, model), BF16),
        in_specs=[SMEM] + [VMEM] * (2 * rest) + [any_space],
        out_specs=VMEM,
        compiler_params=params(16),
        name="finish",
    )(place, *mine, *others, combine)
    experts, units = expert_out.shape[:2]
    hidden, send = pl.pallas_call(
        expert_kernel,
        out_shape=(
            jax.ShapeDtypeStruct((experts, rows, units), BF16),
            jax.ShapeDtypeStruct((rows, half), BF16),
        ),
        in_specs=[SMEM, VMEM, VMEM, VMEM],
        out_specs=(VMEM, VMEM),
        compiler_params=params(8),
        name="experts",
    )(place, slot_in, expert_in, expert_out)
    received = swap_pair(send)
    keep = pl.pallas_call(
        own_kernel,
        out_shape=jax.ShapeDtypeStruct((rows, half), F32),
        in_specs=[SMEM, VMEM, VMEM, any_space],
        out_specs=VMEM,
        cost_estimate=cost(2 * rows * units * half * experts, 2 * experts * units * half),
        compiler_params=params(8),
        name="own",
    )(place, hidden, expert_out, send)
    partial = (keep + received.astype(F32)).astype(BF16)
    partials = jnp.broadcast_to(partial, (groups * rest, rows, half))
    partials = lax.all_to_all(partials, ("wide", "rest"), split_axis=0, concat_axis=0, tiled=True)
    slot_out = jnp.sum(partials.reshape(groups, rest, rows, half).astype(F32), axis=1)
    slot_out = slot_out.astype(BF16).reshape(slots, half)
    other = swap_pair(slot_out)
    done, blocks = count // 2, 8
    mixed, left = pl.pallas_call(
        mix_kernel,
        out_shape=(
            pltpu.HBM((count, model), BF16),
            jax.ShapeDtypeStruct((count - done, half), BF16),
        ),
        in_specs=[SMEM, VMEM, VMEM],
        out_specs=(HBM, VMEM),
        scratch_shapes=[pltpu.VMEM((done, half), BF16), pltpu.SemaphoreType.DMA((blocks // 2,))],
        cost_estimate=cost(2 * count * slots * half, 2 * count * (half + slots)),
        compiler_params=params(16),
        name="mix",
    )(place, combine, slot_out)
    return pl.pallas_call(
        mix_other_kernel,
        out_shape=jax.ShapeDtypeStruct((count, model), BF16),
        in_specs=[SMEM, VMEM, VMEM, VMEM, HBM],
        out_specs=HBM,
        scratch_shapes=[pltpu.VMEM((count, half), BF16), pltpu.SemaphoreType.DMA((blocks + 1,))],
        input_output_aliases={4: 0},
        cost_estimate=cost(2 * count * slots * half, 2 * count * (half + slots)),
        compiler_params=params(16),
        name="mix_other",
    )(place, combine, other, left, mixed)


def solution(mesh):
    wide, narrow = mesh.shape["wide"], mesh.shape["narrow"]
    cut = Mesh(mesh.devices.reshape(wide, narrow // 2, 2), ("wide", "rest", "pair"))
    narrow_axes = ("rest", "pair")
    return jax.shard_map(
        shards,
        mesh=cut,
        in_specs=(
            P(("wide",) + narrow_axes, None),
            P(),
            P("wide", None, narrow_axes),
            P("wide", narrow_axes, None),
        ),
        out_specs=P(("wide",) + narrow_axes, None),
        check_vma=False,
    )
```

```python
import math

import jax
import jax.numpy as jnp
from jax import lax
from jax.experimental import pallas as pl
from jax.experimental.pallas import tpu as pltpu
from jax.sharding import Mesh, PartitionSpec as P

SLOT_PER = 4
SIDE = 128
CHUNK = 256
F32 = jnp.float32
BF16 = jnp.bfloat16
VMEM = pl.BlockSpec(memory_space=pltpu.VMEM)
SMEM = pl.BlockSpec(memory_space=pltpu.SMEM)
HBM = pl.BlockSpec(memory_space=pltpu.HBM)
MIB = 1024 * 1024


def params(mib):
    return pltpu.CompilerParams(vmem_limit_bytes=mib * MIB)


def cost(flops, moved, transcendentals=0):
    return pl.CostEstimate(flops=flops, bytes_accessed=moved, transcendentals=transcendentals)


def in_hbm(value):
    return pltpu.with_memory_space_constraint(value, pltpu.HBM)


def dot(lhs, rhs):
    return jnp.dot(lhs, rhs, preferred_element_type=F32)


def side_state(peak, total):
    lane = lax.broadcasted_iota(jnp.int32, (peak.shape[0], SIDE), 1)
    return jnp.where(lane == 0, peak, jnp.where(lane == 1, total, 0.0))


def side_message(peak, total):
    lane = lax.broadcasted_iota(jnp.int32, (peak.shape[0], SIDE), 1)
    out = jnp.zeros((peak.shape[0], SIDE), F32)
    for index, value in enumerate((peak, total)):
        for piece in range(3):
            part = value.astype(BF16).astype(F32)
            out = jnp.where(lane == 3 * index + piece, part, out)
            value = value - part
    return out.astype(BF16)


def read_message(side):
    value = side.astype(F32)
    return (
        value[:, 0:1] + value[:, 1:2] + value[:, 2:3],
        value[:, 3:4] + value[:, 4:5] + value[:, 5:6],
    )


def column_half(side, half):
    return pl.ds(pl.multiple_of(side * half, half), half)


def gather_kernel(place, tokens, slot_params, logits, turned, held, side, send, table, sems):
    chunks = tokens.shape[0] // CHUNK
    slots = slot_params.shape[1]
    middle = slot_params.shape[0] // 2
    spans = [pl.ds(i * CHUNK, CHUNK) for i in range(chunks)]
    table_copy = pltpu.make_async_copy(slot_params, table, sems.at[chunks])
    table_copy.start()
    copies = [pltpu.make_async_copy(tokens.at[span], held.at[span], sems.at[i]) for i, span in enumerate(spans)]
    for copy in copies:
        copy.start()
    high = jnp.full((8, slots), -jnp.inf, F32)
    table_copy.wait()
    for copy, span in zip(copies, spans):
        copy.wait()
        part = dot(held[span, :middle], table[:middle, :]) + dot(held[span, middle:], table[middle:, :])
        logits[span, :] = part
        high = jnp.maximum(high, jnp.max(part.reshape(CHUNK // 8, 8, slots), axis=0))
    peak = jnp.max(high, axis=0, keepdims=True)
    total = jnp.zeros((8, slots), F32)
    columns = []
    for span in spans:
        weights = jnp.exp(logits[span, :] - peak)
        total = total + jnp.sum(weights.reshape(CHUNK // 8, 8, slots), axis=0)
        columns.append(weights.astype(BF16).T)
    weights = jnp.concatenate(columns, axis=1)
    turned[...] = weights
    half = held.shape[1] // 2
    send[:, :half] = dot(weights, held[:, column_half(1 - place[0], half)]).astype(BF16)
    total = jnp.sum(total, axis=0, keepdims=True)
    peak = jnp.broadcast_to(peak, (8, slots)).T[:, 0:1]
    total = jnp.broadcast_to(total, (8, slots)).T[:, 0:1]
    side[...] = side_state(peak, total)
    send[:, half:] = side_message(peak, total)


def own_sums_kernel(place, turned, held, after, keep):
    keep[...] = dot(turned[...], held[:, column_half(place[0], keep.shape[1])])


def pair_kernel(keep, side, received, send):
    width = keep.shape[1]
    peak_mine, total_mine = side[:, 0:1], side[:, 1:2]
    peak_other, total_other = read_message(received[:, width:])
    peak = jnp.maximum(peak_mine, peak_other)
    scale_mine, scale_other = jnp.exp(peak_mine - peak), jnp.exp(peak_other - peak)
    total = total_mine * scale_mine + total_other * scale_other
    sums = keep[...] * scale_mine + received[:, :width].astype(F32) * scale_other
    send[:, :width] = sums.astype(BF16)
    send[:, width:] = side_message(peak, total)


def add_parts(parts, width):
    states = [read_message(part[:, width:]) for part in parts]
    peak = states[0][0]
    for other, _ in states[1:]:
        peak = jnp.maximum(peak, other)
    total = jnp.zeros_like(peak)
    sums = jnp.zeros((parts[0].shape[0], width), F32)
    for part, (peak_other, total_other) in zip(parts, states):
        scale = jnp.exp(peak_other - peak)
        total = total + total_other * scale
        sums = sums + part[:, :width].astype(F32) * scale
    return sums, peak, total


def merge_kernel(received, send):
    width = send.shape[1] - SIDE
    sums, peak, total = add_parts([received[g] for g in range(received.shape[0])], width)
    send[:, :width] = sums.astype(BF16)
    send[:, width:] = side_message(peak, total)


def finish_kernel(place, *refs):
    slot_in = refs[-1]
    half = slot_in.shape[1] // 2
    parts = (len(refs) - 2) // 2
    means = []
    for side in range(2):
        sums, _, total = add_parts([ref[...] for ref in refs[side * parts : (side + 1) * parts]], half)
        means.append((sums / total).astype(BF16))
    first = place[0] == 0
    slot_in[:, :half] = jnp.where(first, means[0], means[1])
    slot_in[:, half:] = jnp.where(first, means[1], means[0])


def second_product(hidden, weights, columns):
    row = lax.broadcasted_iota(jnp.int32, (hidden[0].shape[0], 1), 0)
    result = 0.0
    for e, value in enumerate(hidden):
        result = jnp.where(row // SLOT_PER == e, dot(value, weights[e, :, columns]), result)
    return result


def expert_kernel(place, slot_in, expert_in, expert_out, hidden, send):
    values = []
    for e in range(expert_in.shape[0]):
        values.append(jax.nn.gelu(dot(slot_in[...], expert_in[e])).astype(BF16))
        hidden[e] = values[e]
    send[...] = second_product(values, expert_out, column_half(1 - place[0], send.shape[1])).astype(BF16)


def own_kernel(place, hidden, expert_out, after, keep):
    values = [hidden[e] for e in range(hidden.shape[0])]
    keep[...] = second_product(values, expert_out, column_half(place[0], keep.shape[1]))


def combine_kernel(logits, after, combine):
    value = logits[...]
    weights = jnp.exp(value - jnp.max(value, axis=1, keepdims=True))
    combine[...] = (weights / jnp.sum(weights, axis=1, keepdims=True)).astype(BF16)


def mix_kernel(place, combine, slot_out, mixed, rest, held, sems):
    width = slot_out.shape[1]
    tokens, done = combine.shape[0], held.shape[0]
    block = done // sems.shape[0]
    columns = pl.ds(pl.multiple_of(place[0] * width, width), width)
    copies = []
    for i in range(tokens // block):
        rows = pl.ds(i * block, block)
        value = dot(combine[rows, :], slot_out[...]).astype(BF16)
        if i < sems.shape[0]:
            held[rows, :] = value
            copies.append(pltpu.make_async_copy(held.at[rows], mixed.at[rows, columns], sems.at[i]))
            copies[-1].start()
        else:
            rest[pl.ds(i * block - done, block), :] = value
    for copy in copies:
        copy.wait()


def mix_other_kernel(place, combine, slot_out, rest, before, mixed, held, sems):
    width = slot_out.shape[1]
    blocks = sems.shape[0] - 1
    tokens = combine.shape[0]
    done = tokens - rest.shape[0]
    mine = pl.ds(pl.multiple_of(place[0] * width, width), width)
    other = pl.ds(pl.multiple_of((1 - place[0]) * width, width), width)
    copies = [pltpu.make_async_copy(rest, mixed.at[pl.ds(done, tokens - done), mine], sems.at[blocks])]
    copies[0].start()
    block = tokens // blocks
    for i in range(blocks):
        rows = pl.ds(i * block, block)
        held[rows, :] = dot(combine[rows, :], slot_out[...]).astype(BF16)
        copies.append(pltpu.make_async_copy(held.at[rows], mixed.at[rows, other], sems.at[i]))
        copies[-1].start()
    for copy in copies:
        copy.wait()


def move(value, axes, offsets):
    sizes = [lax.axis_size(axis) for axis in axes]
    moves = []
    for index in range(math.prod(sizes)):
        source, target, stride = index, 0, 1
        for size, offset in zip(reversed(sizes), reversed(offsets)):
            target += (source % size + offset) % size * stride
            source //= size
            stride *= size
        moves.append((index, target))
    return lax.ppermute(value, axes, moves)


def swap_pair(value):
    return move(value, ("pair",), (1,))


def shards(tokens, slot_params, expert_in, expert_out):
    count, model = tokens.shape
    slots = slot_params.shape[1]
    groups, rest = lax.axis_size("wide"), lax.axis_size("rest")
    rows = slots // groups
    half = model // 2
    place = lax.axis_index("pair").astype(jnp.int32).reshape(1)
    any_space = pl.BlockSpec(memory_space=pl.ANY)

    logits, turned, held, side, send = pl.pallas_call(
        gather_kernel,
        out_shape=(
            jax.ShapeDtypeStruct((count, slots), F32),
            jax.ShapeDtypeStruct((slots, count), BF16),
            jax.ShapeDtypeStruct((count, model), BF16),
            jax.ShapeDtypeStruct((slots, SIDE), F32),
            jax.ShapeDtypeStruct((slots, half + SIDE), BF16),
        ),
        in_specs=[SMEM, HBM, HBM],
        out_specs=(VMEM,) * 5,
        scratch_shapes=[pltpu.VMEM((model, slots), BF16), pltpu.SemaphoreType.DMA((count // CHUNK + 1,))],
        compiler_params=params(24),
        name="gather",
    )(place, in_hbm(tokens), in_hbm(slot_params))
    received = swap_pair(send)
    keep = pl.pallas_call(
        own_sums_kernel,
        out_shape=jax.ShapeDtypeStruct((slots, half), F32),
        in_specs=[SMEM, VMEM, VMEM, any_space],
        out_specs=VMEM,
        cost_estimate=cost(2 * slots * count * half, 2 * count * (half + slots)),
        compiler_params=params(16),
        name="own_sums",
    )(place, turned, held, send)
    send = pl.pallas_call(
        pair_kernel,
        out_shape=jax.ShapeDtypeStruct((slots, half + SIDE), BF16),
        in_specs=[VMEM] * 3,
        out_specs=VMEM,
        cost_estimate=cost(0, 6 * slots * model, 128 * slots * model),
        compiler_params=params(16),
        name="pair",
    )(keep, side, received)
    received = lax.all_to_all(send.reshape(groups, rows, -1), "wide", split_axis=0, concat_axis=0, tiled=True)
    send = pl.pallas_call(
        merge_kernel,
        out_shape=jax.ShapeDtypeStruct((rows, half + SIDE), BF16),
        in_specs=[VMEM],
        out_specs=VMEM,
        compiler_params=params(16),
        name="merge",
    )(received)
    axes = ("rest", "pair")
    mine = [send] + [move(send, axes, (r, 0)) for r in range(1, rest)]
    others = [move(send, axes, (r, 1)) for r in reversed(range(rest))]
    combine = pl.pallas_call(
        combine_kernel,
        out_shape=jax.ShapeDtypeStruct((count, slots), BF16),
        in_specs=[VMEM, any_space],
        out_specs=VMEM,
        cost_estimate=cost(8 * count * slots, 6 * count * slots, count * slots),
        compiler_params=params(16),
        name="combine",
    )(logits, send)
    slot_in = pl.pallas_call(
        finish_kernel,
        out_shape=jax.ShapeDtypeStruct((rows, model), BF16),
        in_specs=[SMEM] + [VMEM] * (2 * rest) + [any_space],
        out_specs=VMEM,
        compiler_params=params(16),
        name="finish",
    )(place, *mine, *others, combine)
    experts, units = expert_out.shape[:2]
    hidden, send = pl.pallas_call(
        expert_kernel,
        out_shape=(
            jax.ShapeDtypeStruct((experts, rows, units), BF16),
            jax.ShapeDtypeStruct((rows, half), BF16),
        ),
        in_specs=[SMEM, VMEM, VMEM, VMEM],
        out_specs=(VMEM, VMEM),
        compiler_params=params(8),
        name="experts",
    )(place, slot_in, expert_in, expert_out)
    received = swap_pair(send)
    keep = pl.pallas_call(
        own_kernel,
        out_shape=jax.ShapeDtypeStruct((rows, half), F32),
        in_specs=[SMEM, VMEM, VMEM, any_space],
        out_specs=VMEM,
        cost_estimate=cost(2 * rows * units * half * experts, 2 * experts * units * half),
        compiler_params=params(8),
        name="own",
    )(place, hidden, expert_out, send)
    partial = (keep + received.astype(F32)).astype(BF16)
    partials = jnp.broadcast_to(partial, (groups * rest, rows, half))
    partials = lax.all_to_all(partials, ("wide", "rest"), split_axis=0, concat_axis=0, tiled=True)
    slot_out = jnp.sum(partials.reshape(groups, rest, rows, half).astype(F32), axis=1)
    slot_out = slot_out.astype(BF16).reshape(slots, half)
    other = swap_pair(slot_out)
    done, blocks = count * 5 // 8, 16
    mixed, left = pl.pallas_call(
        mix_kernel,
        out_shape=(
            pltpu.HBM((count, model), BF16),
            jax.ShapeDtypeStruct((count - done, half), BF16),
        ),
        in_specs=[SMEM, VMEM, VMEM],
        out_specs=(HBM, VMEM),
        scratch_shapes=[pltpu.VMEM((done, half), BF16), pltpu.SemaphoreType.DMA((blocks * 5 // 8,))],
        cost_estimate=cost(2 * count * slots * half, 2 * count * (half + slots)),
        compiler_params=params(16),
        name="mix",
    )(place, combine, slot_out)
    return pl.pallas_call(
        mix_other_kernel,
        out_shape=jax.ShapeDtypeStruct((count, model), BF16),
        in_specs=[SMEM, VMEM, VMEM, VMEM, HBM],
        out_specs=HBM,
        scratch_shapes=[pltpu.VMEM((count, half), BF16), pltpu.SemaphoreType.DMA((blocks + 1,))],
        input_output_aliases={4: 0},
        cost_estimate=cost(2 * count * slots * half, 2 * count * (half + slots)),
        compiler_params=params(16),
        name="mix_other",
    )(place, combine, other, left, mixed)


def solution(mesh):
    wide, narrow = mesh.shape["wide"], mesh.shape["narrow"]
    cut = Mesh(mesh.devices.reshape(wide, narrow // 2, 2), ("wide", "rest", "pair"))
    narrow_axes = ("rest", "pair")
    return jax.shard_map(
        shards,
        mesh=cut,
        in_specs=(
            P(("wide",) + narrow_axes, None),
            P(),
            P("wide", None, narrow_axes),
            P("wide", narrow_axes, None),
        ),
        out_specs=P(("wide",) + narrow_axes, None),
        check_vma=False,
    )
```

```python
import math

import jax
import jax.numpy as jnp
from jax import lax
from jax.experimental import pallas as pl
from jax.experimental.pallas import tpu as pltpu
from jax.sharding import Mesh, PartitionSpec as P

SLOT_PER = 4
SIDE = 128
CHUNK = 512
F32 = jnp.float32
BF16 = jnp.bfloat16
VMEM = pl.BlockSpec(memory_space=pltpu.VMEM)
SMEM = pl.BlockSpec(memory_space=pltpu.SMEM)
HBM = pl.BlockSpec(memory_space=pltpu.HBM)
MIB = 1024 * 1024


def params(mib):
    return pltpu.CompilerParams(vmem_limit_bytes=mib * MIB)


def cost(flops, moved, transcendentals=0):
    return pl.CostEstimate(flops=flops, bytes_accessed=moved, transcendentals=transcendentals)


def in_hbm(value):
    return pltpu.with_memory_space_constraint(value, pltpu.HBM)


def dot(lhs, rhs):
    return jnp.dot(lhs, rhs, preferred_element_type=F32)


def side_state(peak, total):
    lane = lax.broadcasted_iota(jnp.int32, (peak.shape[0], SIDE), 1)
    return jnp.where(lane == 0, peak, jnp.where(lane == 1, total, 0.0))


def side_message(peak, total):
    lane = lax.broadcasted_iota(jnp.int32, (peak.shape[0], SIDE), 1)
    out = jnp.zeros((peak.shape[0], SIDE), F32)
    for index, value in enumerate((peak, total)):
        for piece in range(3):
            part = value.astype(BF16).astype(F32)
            out = jnp.where(lane == 3 * index + piece, part, out)
            value = value - part
    return out.astype(BF16)


def read_message(side):
    value = side.astype(F32)
    return (
        value[:, 0:1] + value[:, 1:2] + value[:, 2:3],
        value[:, 3:4] + value[:, 4:5] + value[:, 5:6],
    )


def column_half(side, half):
    return pl.ds(pl.multiple_of(side * half, half), half)


def gather_kernel(place, tokens, slot_params, logits, turned, held, side, send, table, sems):
    chunks = tokens.shape[0] // CHUNK
    slots = slot_params.shape[1]
    spans = [pl.ds(i * CHUNK, CHUNK) for i in range(chunks)]
    table_copy = pltpu.make_async_copy(slot_params, table, sems.at[chunks])
    table_copy.start()
    copies = [pltpu.make_async_copy(tokens.at[span], held.at[span], sems.at[i]) for i, span in enumerate(spans)]
    for copy in copies:
        copy.start()
    high = jnp.full((8, slots), -jnp.inf, F32)
    table_copy.wait()
    for copy, span in zip(copies, spans):
        copy.wait()
        part = dot(held[span, :], table[...])
        logits[span, :] = part
        high = jnp.maximum(high, jnp.max(part.reshape(CHUNK // 8, 8, slots), axis=0))
    peak = jnp.max(high, axis=0, keepdims=True)
    total = jnp.zeros((8, slots), F32)
    columns = []
    for span in spans:
        weights = jnp.exp(logits[span, :] - peak)
        total = total + jnp.sum(weights.reshape(CHUNK // 8, 8, slots), axis=0)
        columns.append(weights.astype(BF16).T)
    weights = jnp.concatenate(columns, axis=1)
    turned[...] = weights
    half = held.shape[1] // 2
    send[:, :half] = dot(weights, held[:, column_half(1 - place[0], half)]).astype(BF16)
    total = jnp.sum(total, axis=0, keepdims=True)
    peak = jnp.broadcast_to(peak, (8, slots)).T[:, 0:1]
    total = jnp.broadcast_to(total, (8, slots)).T[:, 0:1]
    side[...] = side_state(peak, total)
    send[:, half:] = side_message(peak, total)


def own_sums_kernel(place, turned, held, after, keep):
    keep[...] = dot(turned[...], held[:, column_half(place[0], keep.shape[1])])


def pair_kernel(keep, side, received, send):
    width = keep.shape[1]
    peak_mine, total_mine = side[:, 0:1], side[:, 1:2]
    peak_other, total_other = read_message(received[:, width:])
    peak = jnp.maximum(peak_mine, peak_other)
    scale_mine, scale_other = jnp.exp(peak_mine - peak), jnp.exp(peak_other - peak)
    total = total_mine * scale_mine + total_other * scale_other
    sums = keep[...] * scale_mine + received[:, :width].astype(F32) * scale_other
    send[:, :width] = sums.astype(BF16)
    send[:, width:] = side_message(peak, total)


def add_parts(parts, width):
    states = [read_message(part[:, width:]) for part in parts]
    peak = states[0][0]
    for other, _ in states[1:]:
        peak = jnp.maximum(peak, other)
    total = jnp.zeros_like(peak)
    sums = jnp.zeros((parts[0].shape[0], width), F32)
    for part, (peak_other, total_other) in zip(parts, states):
        scale = jnp.exp(peak_other - peak)
        total = total + total_other * scale
        sums = sums + part[:, :width].astype(F32) * scale
    return sums, peak, total


def merge_kernel(received, send):
    width = send.shape[1] - SIDE
    sums, peak, total = add_parts([received[g] for g in range(received.shape[0])], width)
    send[:, :width] = sums.astype(BF16)
    send[:, width:] = side_message(peak, total)


def find_slot_in(place, mine, others):
    half = mine[0].shape[1] - SIDE
    means = []
    for parts in (mine, others):
        sums, _, total = add_parts([part[...] for part in parts], half)
        means.append((sums / total).astype(BF16))
    first = place[0] == 0
    return jnp.concatenate(
        [jnp.where(first, means[0], means[1]), jnp.where(first, means[1], means[0])], axis=1
    )


def second_product(hidden, weights, columns):
    row = lax.broadcasted_iota(jnp.int32, (hidden[0].shape[0], 1), 0)
    result = 0.0
    for e, value in enumerate(hidden):
        result = jnp.where(row // SLOT_PER == e, dot(value, weights[e, :, columns]), result)
    return result


def expert_kernel(place, expert_in, expert_out, after, *refs):
    parts, hidden, send = refs[:-2], refs[-2], refs[-1]
    count = len(parts) // 2
    slot_in = find_slot_in(place, parts[:count], parts[count:])
    values = []
    for e in range(expert_in.shape[0]):
        values.append(jax.nn.gelu(dot(slot_in, expert_in[e])).astype(BF16))
        hidden[e] = values[e]
    send[...] = second_product(values, expert_out, column_half(1 - place[0], send.shape[1])).astype(BF16)


def own_kernel(place, hidden, expert_out, after, keep):
    values = [hidden[e] for e in range(hidden.shape[0])]
    keep[...] = second_product(values, expert_out, column_half(place[0], keep.shape[1]))


def combine_kernel(logits, after, combine):
    value = logits[...]
    weights = jnp.exp(value - jnp.max(value, axis=1, keepdims=True))
    combine[...] = (weights / jnp.sum(weights, axis=1, keepdims=True)).astype(BF16)


def mix_kernel(place, combine, slot_out, mixed, rest, held, sems):
    width = slot_out.shape[1]
    tokens, done = combine.shape[0], held.shape[0]
    block = done // sems.shape[0]
    columns = pl.ds(pl.multiple_of(place[0] * width, width), width)
    copies = []
    for i in range(tokens // block):
        rows = pl.ds(i * block, block)
        value = dot(combine[rows, :], slot_out[...]).astype(BF16)
        if i < sems.shape[0]:
            held[rows, :] = value
            copies.append(pltpu.make_async_copy(held.at[rows], mixed.at[rows, columns], sems.at[i]))
            copies[-1].start()
        else:
            rest[pl.ds(i * block - done, block), :] = value
    for copy in copies:
        copy.wait()


def mix_other_kernel(place, combine, slot_out, rest, before, mixed, held, sems):
    width = slot_out.shape[1]
    blocks = sems.shape[0] - 1
    tokens = combine.shape[0]
    done = tokens - rest.shape[0]
    mine = pl.ds(pl.multiple_of(place[0] * width, width), width)
    other = pl.ds(pl.multiple_of((1 - place[0]) * width, width), width)
    copies = [pltpu.make_async_copy(rest, mixed.at[pl.ds(done, tokens - done), mine], sems.at[blocks])]
    copies[0].start()
    block = tokens // blocks
    for i in range(blocks):
        rows = pl.ds(i * block, block)
        held[rows, :] = dot(combine[rows, :], slot_out[...]).astype(BF16)
        copies.append(pltpu.make_async_copy(held.at[rows], mixed.at[rows, other], sems.at[i]))
        copies[-1].start()
    for copy in copies:
        copy.wait()


def move(value, axes, offsets):
    sizes = [lax.axis_size(axis) for axis in axes]
    moves = []
    for index in range(math.prod(sizes)):
        source, target, stride = index, 0, 1
        for size, offset in zip(reversed(sizes), reversed(offsets)):
            target += (source % size + offset) % size * stride
            source //= size
            stride *= size
        moves.append((index, target))
    return lax.ppermute(value, axes, moves)


def swap_pair(value):
    return move(value, ("pair",), (1,))


def shards(tokens, slot_params, expert_in, expert_out):
    count, model = tokens.shape
    slots = slot_params.shape[1]
    groups, rest = lax.axis_size("wide"), lax.axis_size("rest")
    rows = slots // groups
    half = model // 2
    place = lax.axis_index("pair").astype(jnp.int32).reshape(1)
    any_space = pl.BlockSpec(memory_space=pl.ANY)

    logits, turned, held, side, send = pl.pallas_call(
        gather_kernel,
        out_shape=(
            jax.ShapeDtypeStruct((count, slots), F32),
            jax.ShapeDtypeStruct((slots, count), BF16),
            jax.ShapeDtypeStruct((count, model), BF16),
            jax.ShapeDtypeStruct((slots, SIDE), F32),
            jax.ShapeDtypeStruct((slots, half + SIDE), BF16),
        ),
        in_specs=[SMEM, HBM, HBM],
        out_specs=(VMEM,) * 5,
        scratch_shapes=[pltpu.VMEM((model, slots), BF16), pltpu.SemaphoreType.DMA((count // CHUNK + 1,))],
        compiler_params=params(24),
        name="gather",
    )(place, in_hbm(tokens), in_hbm(slot_params))
    received = swap_pair(send)
    keep = pl.pallas_call(
        own_sums_kernel,
        out_shape=jax.ShapeDtypeStruct((slots, half), F32),
        in_specs=[SMEM, VMEM, VMEM, any_space],
        out_specs=VMEM,
        cost_estimate=cost(2 * slots * count * half, 2 * count * (half + slots)),
        compiler_params=params(16),
        name="own_sums",
    )(place, turned, held, send)
    send = pl.pallas_call(
        pair_kernel,
        out_shape=jax.ShapeDtypeStruct((slots, half + SIDE), BF16),
        in_specs=[VMEM] * 3,
        out_specs=VMEM,
        cost_estimate=cost(0, 6 * slots * model, 128 * slots * model),
        compiler_params=params(16),
        name="pair",
    )(keep, side, received)
    received = lax.all_to_all(send.reshape(groups, rows, -1), "wide", split_axis=0, concat_axis=0, tiled=True)
    send = pl.pallas_call(
        merge_kernel,
        out_shape=jax.ShapeDtypeStruct((rows, half + SIDE), BF16),
        in_specs=[VMEM],
        out_specs=VMEM,
        compiler_params=params(16),
        name="merge",
    )(received)
    axes = ("rest", "pair")
    mine = [send] + [move(send, axes, (r, 0)) for r in range(1, rest)]
    others = [move(send, axes, (r, 1)) for r in reversed(range(rest))]
    combine = pl.pallas_call(
        combine_kernel,
        out_shape=jax.ShapeDtypeStruct((count, slots), BF16),
        in_specs=[VMEM, any_space],
        out_specs=VMEM,
        cost_estimate=cost(8 * count * slots, 6 * count * slots, count * slots),
        compiler_params=params(16),
        name="combine",
    )(logits, send)
    experts, units = expert_out.shape[:2]
    hidden, send = pl.pallas_call(
        expert_kernel,
        out_shape=(
            jax.ShapeDtypeStruct((experts, rows, units), BF16),
            jax.ShapeDtypeStruct((rows, half), BF16),
        ),
        in_specs=[SMEM, VMEM, VMEM, any_space] + [VMEM] * (2 * rest),
        out_specs=(VMEM, VMEM),
        compiler_params=params(8),
        name="experts",
    )(place, expert_in, expert_out, combine, *mine, *others)
    received = swap_pair(send)
    keep = pl.pallas_call(
        own_kernel,
        out_shape=jax.ShapeDtypeStruct((rows, half), F32),
        in_specs=[SMEM, VMEM, VMEM, any_space],
        out_specs=VMEM,
        cost_estimate=cost(2 * rows * units * half * experts, 2 * experts * units * half),
        compiler_params=params(8),
        name="own",
    )(place, hidden, expert_out, send)
    partial = (keep + received.astype(F32)).astype(BF16)
    partials = jnp.broadcast_to(partial, (groups * rest, rows, half))
    partials = lax.all_to_all(partials, ("rest", "wide"), split_axis=0, concat_axis=0, tiled=True)
    slot_out = jnp.sum(partials.reshape(rest, groups, rows, half).astype(F32), axis=0)
    slot_out = slot_out.astype(BF16).reshape(slots, half)
    other = swap_pair(slot_out)
    done, blocks = count // 2, 8
    mixed, left = pl.pallas_call(
        mix_kernel,
        out_shape=(
            pltpu.HBM((count, model), BF16),
            jax.ShapeDtypeStruct((count - done, half), BF16),
        ),
        in_specs=[SMEM, VMEM, VMEM],
        out_specs=(HBM, VMEM),
        scratch_shapes=[pltpu.VMEM((done, half), BF16), pltpu.SemaphoreType.DMA((blocks // 2,))],
        cost_estimate=cost(2 * count * slots * half, 2 * count * (half + slots)),
        compiler_params=params(16),
        name="mix",
    )(place, combine, slot_out)
    return pl.pallas_call(
        mix_other_kernel,
        out_shape=jax.ShapeDtypeStruct((count, model), BF16),
        in_specs=[SMEM, VMEM, VMEM, VMEM, HBM],
        out_specs=HBM,
        scratch_shapes=[pltpu.VMEM((count, half), BF16), pltpu.SemaphoreType.DMA((blocks + 1,))],
        input_output_aliases={4: 0},
        cost_estimate=cost(2 * count * slots * half, 2 * count * (half + slots)),
        compiler_params=params(16),
        name="mix_other",
    )(place, combine, other, left, mixed)


def solution(mesh):
    wide, narrow = mesh.shape["wide"], mesh.shape["narrow"]
    cut = Mesh(mesh.devices.reshape(wide, narrow // 2, 2), ("wide", "rest", "pair"))
    narrow_axes = ("rest", "pair")
    return jax.shard_map(
        shards,
        mesh=cut,
        in_specs=(
            P(("wide",) + narrow_axes, None),
            P(),
            P("wide", None, narrow_axes),
            P("wide", narrow_axes, None),
        ),
        out_specs=P(("wide",) + narrow_axes, None),
        check_vma=False,
    )
```

```python
import math

import jax
import jax.numpy as jnp
from jax import lax
from jax.experimental import pallas as pl
from jax.experimental.pallas import tpu as pltpu
from jax.sharding import Mesh, PartitionSpec as P

SLOT_PER = 4
SIDE = 128
CHUNK = 128
ROWS, COLUMNS = 128, 256
F32 = jnp.float32
BF16 = jnp.bfloat16
VMEM = pl.BlockSpec(memory_space=pltpu.VMEM)
SMEM = pl.BlockSpec(memory_space=pltpu.SMEM)
HBM = pl.BlockSpec(memory_space=pltpu.HBM)
MIB = 1024 * 1024


def params(mib):
    return pltpu.CompilerParams(vmem_limit_bytes=mib * MIB)


def cost(flops, moved, transcendentals=0):
    return pl.CostEstimate(flops=flops, bytes_accessed=moved, transcendentals=transcendentals)


def in_hbm(value):
    return pltpu.with_memory_space_constraint(value, pltpu.HBM)


def dot(lhs, rhs):
    return jnp.dot(lhs, rhs, preferred_element_type=F32)


def side_state(peak, total):
    lane = lax.broadcasted_iota(jnp.int32, (peak.shape[0], SIDE), 1)
    return jnp.where(lane == 0, peak, jnp.where(lane == 1, total, 0.0))


def side_message(peak, total):
    lane = lax.broadcasted_iota(jnp.int32, (peak.shape[0], SIDE), 1)
    out = jnp.zeros((peak.shape[0], SIDE), F32)
    for index, value in enumerate((peak, total)):
        for piece in range(3):
            part = value.astype(BF16).astype(F32)
            out = jnp.where(lane == 3 * index + piece, part, out)
            value = value - part
    return out.astype(BF16)


def read_message(side):
    value = side.astype(F32)
    return (
        value[:, 0:1] + value[:, 1:2] + value[:, 2:3],
        value[:, 3:4] + value[:, 4:5] + value[:, 5:6],
    )


def column_half(side, half):
    return pl.ds(pl.multiple_of(side * half, half), half)


def gather_kernel(place, tokens, slot_params, logits, turned, held, side, send, table, sems):
    chunks = tokens.shape[0] // CHUNK
    slots = slot_params.shape[1]
    spans = [pl.ds(i * CHUNK, CHUNK) for i in range(chunks)]
    table_copy = pltpu.make_async_copy(slot_params, table, sems.at[chunks])
    table_copy.start()
    copies = [pltpu.make_async_copy(tokens.at[span], held.at[span], sems.at[i]) for i, span in enumerate(spans)]
    for copy in copies:
        copy.start()
    high = jnp.full((8, slots), -jnp.inf, F32)
    table_copy.wait()
    for copy, span in zip(copies, spans):
        copy.wait()
        part = dot(held[span, :], table[...])
        logits[span, :] = part
        high = jnp.maximum(high, jnp.max(part.reshape(CHUNK // 8, 8, slots), axis=0))
    peak = jnp.max(high, axis=0, keepdims=True)
    total = jnp.zeros((8, slots), F32)
    columns = []
    for span in spans:
        weights = jnp.exp(logits[span, :] - peak)
        total = total + jnp.sum(weights.reshape(CHUNK // 8, 8, slots), axis=0)
        columns.append(weights.astype(BF16).T)
    weights = jnp.concatenate(columns, axis=1)
    turned[...] = weights
    half = held.shape[1] // 2
    send[:, :half] = dot(weights, held[:, column_half(1 - place[0], half)]).astype(BF16)
    total = jnp.sum(total, axis=0, keepdims=True)
    peak = jnp.broadcast_to(peak, (8, slots)).T[:, 0:1]
    total = jnp.broadcast_to(total, (8, slots)).T[:, 0:1]
    side[...] = side_state(peak, total)
    send[:, half:] = side_message(peak, total)


def own_sums_kernel(place, turned, held, after, keep):
    keep[...] = dot(turned[...], held[:, column_half(place[0], keep.shape[1])])


def pair_kernel(keep, side, received, send):
    width = keep.shape[1]
    peak_mine, total_mine = side[:, 0:1], side[:, 1:2]
    peak_other, total_other = read_message(received[:, width:])
    peak = jnp.maximum(peak_mine, peak_other)
    scale_mine, scale_other = jnp.exp(peak_mine - peak), jnp.exp(peak_other - peak)
    total = total_mine * scale_mine + total_other * scale_other
    sums = keep[...] * scale_mine + received[:, :width].astype(F32) * scale_other
    send[:, :width] = sums.astype(BF16)
    send[:, width:] = side_message(peak, total)


def add_parts(parts, width):
    states = [read_message(part[:, width:]) for part in parts]
    peak = states[0][0]
    for other, _ in states[1:]:
        peak = jnp.maximum(peak, other)
    total = jnp.zeros_like(peak)
    sums = jnp.zeros((parts[0].shape[0], width), F32)
    for part, (peak_other, total_other) in zip(parts, states):
        scale = jnp.exp(peak_other - peak)
        total = total + total_other * scale
        sums = sums + part[:, :width].astype(F32) * scale
    return sums, peak, total


def merge_kernel(received, send):
    width = send.shape[1] - SIDE
    sums, peak, total = add_parts([received[g] for g in range(received.shape[0])], width)
    send[:, :width] = sums.astype(BF16)
    send[:, width:] = side_message(peak, total)


def find_slot_in(place, mine, others):
    half = mine[0].shape[1] - SIDE
    means = []
    for parts in (mine, others):
        sums, _, total = add_parts([part[...] for part in parts], half)
        means.append((sums / total).astype(BF16))
    first = place[0] == 0
    return jnp.concatenate(
        [jnp.where(first, means[0], means[1]), jnp.where(first, means[1], means[0])], axis=1
    )


def second_product(hidden, weights, columns):
    row = lax.broadcasted_iota(jnp.int32, (hidden[0].shape[0], 1), 0)
    result = 0.0
    for e, value in enumerate(hidden):
        result = jnp.where(row // SLOT_PER == e, dot(value, weights[e, :, columns]), result)
    return result


def expert_kernel(place, expert_in, expert_out, after, *refs):
    parts, hidden, send = refs[:-2], refs[-2], refs[-1]
    count = len(parts) // 2
    slot_in = find_slot_in(place, parts[:count], parts[count:])
    values = []
    for e in range(expert_in.shape[0]):
        values.append(jax.nn.gelu(dot(slot_in, expert_in[e])).astype(BF16))
        hidden[e] = values[e]
    send[...] = second_product(values, expert_out, column_half(1 - place[0], send.shape[1])).astype(BF16)


def own_kernel(place, hidden, expert_out, after, keep):
    values = [hidden[e] for e in range(hidden.shape[0])]
    keep[...] = second_product(values, expert_out, column_half(place[0], keep.shape[1]))


def combine_kernel(logits, after, combine):
    value = logits[...]
    weights = jnp.exp(value - jnp.max(value, axis=1, keepdims=True))
    combine[...] = (weights / jnp.sum(weights, axis=1, keepdims=True)).astype(BF16)


def mix_block(combine, slot_out, start, size, target, offset):
    for row in range(start, start + size, ROWS):
        for column in range(0, slot_out.shape[1], COLUMNS):
            columns = pl.ds(column, COLUMNS)
            value = dot(combine[pl.ds(row, ROWS), :], slot_out[:, columns])
            target[pl.ds(row - offset, ROWS), columns] = value.astype(BF16)


def mix_kernel(place, combine, slot_out, mixed, rest, held, sems):
    columns = column_half(place[0], slot_out.shape[1])
    tokens, done = combine.shape[0], held.shape[0]
    block = done // sems.shape[0]
    copies = []
    for i in range(tokens // block):
        if i < sems.shape[0]:
            rows = pl.ds(i * block, block)
            mix_block(combine, slot_out, i * block, block, held, 0)
            copies.append(pltpu.make_async_copy(held.at[rows], mixed.at[rows, columns], sems.at[i]))
            copies[-1].start()
        else:
            mix_block(combine, slot_out, i * block, block, rest, done)
    for copy in copies:
        copy.wait()


def mix_other_kernel(place, combine, slot_out, rest, before, mixed, held, sems):
    half = slot_out.shape[1]
    blocks = sems.shape[0] - 1
    tokens = combine.shape[0]
    done = tokens - rest.shape[0]
    target = mixed.at[pl.ds(done, tokens - done), column_half(place[0], half)]
    copies = [pltpu.make_async_copy(rest, target, sems.at[blocks])]
    copies[0].start()
    block = tokens // blocks
    for i in range(blocks):
        rows = pl.ds(i * block, block)
        mix_block(combine, slot_out, i * block, block, held, 0)
        target = mixed.at[rows, column_half(1 - place[0], half)]
        copies.append(pltpu.make_async_copy(held.at[rows], target, sems.at[i]))
        copies[-1].start()
    for copy in copies:
        copy.wait()


def move(value, axes, offsets):
    sizes = [lax.axis_size(axis) for axis in axes]
    moves = []
    for index in range(math.prod(sizes)):
        source, target, stride = index, 0, 1
        for size, offset in zip(reversed(sizes), reversed(offsets)):
            target += (source % size + offset) % size * stride
            source //= size
            stride *= size
        moves.append((index, target))
    return lax.ppermute(value, axes, moves)


def swap_pair(value):
    return move(value, ("pair",), (1,))


def shards(tokens, slot_params, expert_in, expert_out):
    count, model = tokens.shape
    slots = slot_params.shape[1]
    groups, rest = lax.axis_size("wide"), lax.axis_size("rest")
    rows = slots // groups
    half = model // 2
    place = lax.axis_index("pair").astype(jnp.int32).reshape(1)
    any_space = pl.BlockSpec(memory_space=pl.ANY)

    logits, turned, held, side, send = pl.pallas_call(
        gather_kernel,
        out_shape=(
            jax.ShapeDtypeStruct((count, slots), F32),
            jax.ShapeDtypeStruct((slots, count), BF16),
            jax.ShapeDtypeStruct((count, model), BF16),
            jax.ShapeDtypeStruct((slots, SIDE), F32),
            jax.ShapeDtypeStruct((slots, half + SIDE), BF16),
        ),
        in_specs=[SMEM, HBM, HBM],
        out_specs=(VMEM,) * 5,
        scratch_shapes=[pltpu.VMEM((model, slots), BF16), pltpu.SemaphoreType.DMA((count // CHUNK + 1,))],
        compiler_params=params(24),
        name="gather",
    )(place, in_hbm(tokens), in_hbm(slot_params))
    received = swap_pair(send)
    keep = pl.pallas_call(
        own_sums_kernel,
        out_shape=jax.ShapeDtypeStruct((slots, half), F32),
        in_specs=[SMEM, VMEM, VMEM, any_space],
        out_specs=VMEM,
        cost_estimate=cost(2 * slots * count * half, 2 * count * (half + slots)),
        compiler_params=params(16),
        name="own_sums",
    )(place, turned, held, send)
    send = pl.pallas_call(
        pair_kernel,
        out_shape=jax.ShapeDtypeStruct((slots, half + SIDE), BF16),
        in_specs=[VMEM] * 3,
        out_specs=VMEM,
        cost_estimate=cost(0, 6 * slots * model, 128 * slots * model),
        compiler_params=params(16),
        name="pair",
    )(keep, side, received)
    received = lax.all_to_all(send.reshape(groups, rows, -1), "wide", split_axis=0, concat_axis=0, tiled=True)
    send = pl.pallas_call(
        merge_kernel,
        out_shape=jax.ShapeDtypeStruct((rows, half + SIDE), BF16),
        in_specs=[VMEM],
        out_specs=VMEM,
        compiler_params=params(16),
        name="merge",
    )(received)
    axes = ("rest", "pair")
    mine = [send] + [move(send, axes, (r, 0)) for r in range(1, rest)]
    others = [move(send, axes, (r, 1)) for r in reversed(range(rest))]
    combine = pl.pallas_call(
        combine_kernel,
        out_shape=jax.ShapeDtypeStruct((count, slots), BF16),
        in_specs=[VMEM, any_space],
        out_specs=VMEM,
        cost_estimate=cost(8 * count * slots, 6 * count * slots, count * slots),
        compiler_params=params(16),
        name="combine",
    )(logits, send)
    experts, units = expert_out.shape[:2]
    hidden, send = pl.pallas_call(
        expert_kernel,
        out_shape=(
            jax.ShapeDtypeStruct((experts, rows, units), BF16),
            jax.ShapeDtypeStruct((rows, half), BF16),
        ),
        in_specs=[SMEM, VMEM, VMEM, any_space] + [VMEM] * (2 * rest),
        out_specs=(VMEM, VMEM),
        compiler_params=params(8),
        name="experts",
    )(place, expert_in, expert_out, combine, *mine, *others)
    received = swap_pair(send)
    keep = pl.pallas_call(
        own_kernel,
        out_shape=jax.ShapeDtypeStruct((rows, half), F32),
        in_specs=[SMEM, VMEM, VMEM, any_space],
        out_specs=VMEM,
        cost_estimate=cost(2 * rows * units * half * experts, 2 * experts * units * half),
        compiler_params=params(8),
        name="own",
    )(place, hidden, expert_out, send)
    partial = (keep + received.astype(F32)).astype(BF16)
    partials = jnp.broadcast_to(partial, (groups * rest, rows, half))
    partials = lax.all_to_all(partials, ("rest", "wide"), split_axis=0, concat_axis=0, tiled=True)
    slot_out = jnp.sum(partials.reshape(rest, groups, rows, half).astype(F32), axis=0)
    slot_out = slot_out.astype(BF16).reshape(slots, half)
    other = swap_pair(slot_out)
    done, blocks = count // 2, 8
    mixed, left = pl.pallas_call(
        mix_kernel,
        out_shape=(
            pltpu.HBM((count, model), BF16),
            jax.ShapeDtypeStruct((count - done, half), BF16),
        ),
        in_specs=[SMEM, VMEM, VMEM],
        out_specs=(HBM, VMEM),
        scratch_shapes=[pltpu.VMEM((done, half), BF16), pltpu.SemaphoreType.DMA((blocks // 2,))],
        cost_estimate=cost(2 * count * slots * half, 2 * count * (half + slots)),
        compiler_params=params(16),
        name="mix",
    )(place, combine, slot_out)
    return pl.pallas_call(
        mix_other_kernel,
        out_shape=jax.ShapeDtypeStruct((count, model), BF16),
        in_specs=[SMEM, VMEM, VMEM, VMEM, HBM],
        out_specs=HBM,
        scratch_shapes=[pltpu.VMEM((count, half), BF16), pltpu.SemaphoreType.DMA((blocks + 1,))],
        input_output_aliases={4: 0},
        cost_estimate=cost(2 * count * slots * half, 2 * count * (half + slots)),
        compiler_params=params(16),
        name="mix_other",
    )(place, combine, other, left, mixed)


def solution(mesh):
    wide, narrow = mesh.shape["wide"], mesh.shape["narrow"]
    cut = Mesh(mesh.devices.reshape(wide, narrow // 2, 2), ("wide", "rest", "pair"))
    narrow_axes = ("rest", "pair")
    return jax.shard_map(
        shards,
        mesh=cut,
        in_specs=(
            P(("wide",) + narrow_axes, None),
            P(),
            P("wide", None, narrow_axes),
            P("wide", narrow_axes, None),
        ),
        out_specs=P(("wide",) + narrow_axes, None),
        check_vma=False,
    )
```

```python
import math

import jax
import jax.numpy as jnp
from jax import lax
from jax.experimental import pallas as pl
from jax.experimental.pallas import tpu as pltpu
from jax.sharding import Mesh, PartitionSpec as P

SLOT_PER = 4
SIDE = 128
CHUNK, TOGETHER = 256, 2
F32 = jnp.float32
BF16 = jnp.bfloat16
VMEM = pl.BlockSpec(memory_space=pltpu.VMEM)
SMEM = pl.BlockSpec(memory_space=pltpu.SMEM)
HBM = pl.BlockSpec(memory_space=pltpu.HBM)
MIB = 1024 * 1024


def params(mib):
    return pltpu.CompilerParams(vmem_limit_bytes=mib * MIB)


def cost(flops, moved, transcendentals=0):
    return pl.CostEstimate(flops=flops, bytes_accessed=moved, transcendentals=transcendentals)


def in_hbm(value):
    return pltpu.with_memory_space_constraint(value, pltpu.HBM)


def dot(lhs, rhs):
    return jnp.dot(lhs, rhs, preferred_element_type=F32)


def side_state(peak, total):
    lane = lax.broadcasted_iota(jnp.int32, (peak.shape[0], SIDE), 1)
    return jnp.where(lane == 0, peak, jnp.where(lane == 1, total, 0.0))


def side_message(peak, total):
    lane = lax.broadcasted_iota(jnp.int32, (peak.shape[0], SIDE), 1)
    out = jnp.zeros((peak.shape[0], SIDE), F32)
    for index, value in enumerate((peak, total)):
        for piece in range(3):
            part = value.astype(BF16).astype(F32)
            out = jnp.where(lane == 3 * index + piece, part, out)
            value = value - part
    return out.astype(BF16)


def read_message(side):
    value = side.astype(F32)
    return (
        value[:, 0:1] + value[:, 1:2] + value[:, 2:3],
        value[:, 3:4] + value[:, 4:5] + value[:, 5:6],
    )


def column_half(side, half):
    return pl.ds(pl.multiple_of(side * half, half), half)


def gather_kernel(place, tokens, slot_params, logits, turned, held, side, send, table, sems):
    chunks = tokens.shape[0] // CHUNK
    slots = slot_params.shape[1]
    spans = [pl.ds(i * CHUNK, CHUNK) for i in range(chunks)]
    table_copy = pltpu.make_async_copy(slot_params, table, sems.at[chunks])
    table_copy.start()
    copies = [pltpu.make_async_copy(tokens.at[span], held.at[span], sems.at[i]) for i, span in enumerate(spans)]
    for copy in copies:
        copy.start()
    high = jnp.full((8, slots), -jnp.inf, F32)
    table_copy.wait()
    for first in range(0, chunks, TOGETHER):
        for copy in copies[first : first + TOGETHER]:
            copy.wait()
        parts = [dot(held[span, :], table[...]) for span in spans[first : first + TOGETHER]]
        for part, span in zip(parts, spans[first:]):
            logits[span, :] = part
            high = jnp.maximum(high, jnp.max(part.reshape(CHUNK // 8, 8, slots), axis=0))
    peak = jnp.max(high, axis=0, keepdims=True)
    total = jnp.zeros((8, slots), F32)
    columns = []
    for span in spans:
        weights = jnp.exp(logits[span, :] - peak)
        total = total + jnp.sum(weights.reshape(CHUNK // 8, 8, slots), axis=0)
        columns.append(weights.astype(BF16).T)
    weights = jnp.concatenate(columns, axis=1)
    turned[...] = weights
    half = held.shape[1] // 2
    send[:, :half] = dot(weights, held[:, column_half(1 - place[0], half)]).astype(BF16)
    total = jnp.sum(total, axis=0, keepdims=True)
    peak = jnp.broadcast_to(peak, (8, slots)).T[:, 0:1]
    total = jnp.broadcast_to(total, (8, slots)).T[:, 0:1]
    side[...] = side_state(peak, total)
    send[:, half:] = side_message(peak, total)


def own_sums_kernel(place, turned, held, after, keep):
    keep[...] = dot(turned[...], held[:, column_half(place[0], keep.shape[1])])


def pair_kernel(keep, side, received, send):
    width = keep.shape[1]
    peak_mine, total_mine = side[:, 0:1], side[:, 1:2]
    peak_other, total_other = read_message(received[:, width:])
    peak = jnp.maximum(peak_mine, peak_other)
    scale_mine, scale_other = jnp.exp(peak_mine - peak), jnp.exp(peak_other - peak)
    total = total_mine * scale_mine + total_other * scale_other
    sums = keep[...] * scale_mine + received[:, :width].astype(F32) * scale_other
    send[:, :width] = sums.astype(BF16)
    send[:, width:] = side_message(peak, total)


def add_parts(parts, width):
    states = [read_message(part[:, width:]) for part in parts]
    peak = states[0][0]
    for other, _ in states[1:]:
        peak = jnp.maximum(peak, other)
    total = jnp.zeros_like(peak)
    sums = jnp.zeros((parts[0].shape[0], width), F32)
    for part, (peak_other, total_other) in zip(parts, states):
        scale = jnp.exp(peak_other - peak)
        total = total + total_other * scale
        sums = sums + part[:, :width].astype(F32) * scale
    return sums, peak, total


def merge_kernel(received, send):
    width = send.shape[1] - SIDE
    sums, peak, total = add_parts([received[g] for g in range(received.shape[0])], width)
    send[:, :width] = sums.astype(BF16)
    send[:, width:] = side_message(peak, total)


def find_slot_in(place, mine, others):
    half = mine[0].shape[1] - SIDE
    means = []
    for parts in (mine, others):
        sums, _, total = add_parts([part[...] for part in parts], half)
        means.append((sums / total).astype(BF16))
    first = place[0] == 0
    return jnp.concatenate(
        [jnp.where(first, means[0], means[1]), jnp.where(first, means[1], means[0])], axis=1
    )


def second_product(hidden, weights, columns):
    row = lax.broadcasted_iota(jnp.int32, (hidden[0].shape[0], 1), 0)
    result = 0.0
    for e, value in enumerate(hidden):
        result = jnp.where(row // SLOT_PER == e, dot(value, weights[e, :, columns]), result)
    return result


def expert_kernel(place, expert_in, expert_out, after, *refs):
    parts, hidden, send = refs[:-2], refs[-2], refs[-1]
    count = len(parts) // 2
    slot_in = find_slot_in(place, parts[:count], parts[count:])
    values = []
    for e in range(expert_in.shape[0]):
        values.append(jax.nn.gelu(dot(slot_in, expert_in[e])).astype(BF16))
        hidden[e] = values[e]
    send[...] = second_product(values, expert_out, column_half(1 - place[0], send.shape[1])).astype(BF16)


def own_kernel(place, hidden, expert_out, after, keep):
    values = [hidden[e] for e in range(hidden.shape[0])]
    keep[...] = second_product(values, expert_out, column_half(place[0], keep.shape[1]))


def combine_kernel(logits, after, combine):
    value = logits[...]
    weights = jnp.exp(value - jnp.max(value, axis=1, keepdims=True))
    combine[...] = (weights / jnp.sum(weights, axis=1, keepdims=True)).astype(BF16)


def mix_kernel(place, combine, slot_out, mixed, rest, held, sems):
    width = slot_out.shape[1]
    tokens, done = combine.shape[0], held.shape[0]
    block = done // sems.shape[0]
    columns = pl.ds(pl.multiple_of(place[0] * width, width), width)
    copies = []
    for i in range(tokens // block):
        rows = pl.ds(i * block, block)
        value = dot(combine[rows, :], slot_out[...]).astype(BF16)
        if i < sems.shape[0]:
            held[rows, :] = value
            copies.append(pltpu.make_async_copy(held.at[rows], mixed.at[rows, columns], sems.at[i]))
            copies[-1].start()
        else:
            rest[pl.ds(i * block - done, block), :] = value
    for copy in copies:
        copy.wait()


def mix_other_kernel(place, combine, slot_out, rest, before, mixed, held, sems):
    width = slot_out.shape[1]
    blocks = sems.shape[0] - 1
    tokens = combine.shape[0]
    done = tokens - rest.shape[0]
    mine = pl.ds(pl.multiple_of(place[0] * width, width), width)
    other = pl.ds(pl.multiple_of((1 - place[0]) * width, width), width)
    copies = [pltpu.make_async_copy(rest, mixed.at[pl.ds(done, tokens - done), mine], sems.at[blocks])]
    copies[0].start()
    block = tokens // blocks
    for i in range(blocks):
        rows = pl.ds(i * block, block)
        held[rows, :] = dot(combine[rows, :], slot_out[...]).astype(BF16)
        copies.append(pltpu.make_async_copy(held.at[rows], mixed.at[rows, other], sems.at[i]))
        copies[-1].start()
    for copy in copies:
        copy.wait()


def move(value, axes, offsets):
    sizes = [lax.axis_size(axis) for axis in axes]
    moves = []
    for index in range(math.prod(sizes)):
        source, target, stride = index, 0, 1
        for size, offset in zip(reversed(sizes), reversed(offsets)):
            target += (source % size + offset) % size * stride
            source //= size
            stride *= size
        moves.append((index, target))
    return lax.ppermute(value, axes, moves)


def swap_pair(value):
    return move(value, ("pair",), (1,))


def shards(tokens, slot_params, expert_in, expert_out):
    count, model = tokens.shape
    slots = slot_params.shape[1]
    groups, rest = lax.axis_size("wide"), lax.axis_size("rest")
    rows = slots // groups
    half = model // 2
    place = lax.axis_index("pair").astype(jnp.int32).reshape(1)
    any_space = pl.BlockSpec(memory_space=pl.ANY)

    logits, turned, held, side, send = pl.pallas_call(
        gather_kernel,
        out_shape=(
            jax.ShapeDtypeStruct((count, slots), F32),
            jax.ShapeDtypeStruct((slots, count), BF16),
            jax.ShapeDtypeStruct((count, model), BF16),
            jax.ShapeDtypeStruct((slots, SIDE), F32),
            jax.ShapeDtypeStruct((slots, half + SIDE), BF16),
        ),
        in_specs=[SMEM, HBM, HBM],
        out_specs=(VMEM,) * 5,
        scratch_shapes=[pltpu.VMEM((model, slots), BF16), pltpu.SemaphoreType.DMA((count // CHUNK + 1,))],
        compiler_params=params(24),
        name="gather",
    )(place, in_hbm(tokens), in_hbm(slot_params))
    received = swap_pair(send)
    keep = pl.pallas_call(
        own_sums_kernel,
        out_shape=jax.ShapeDtypeStruct((slots, half), F32),
        in_specs=[SMEM, VMEM, VMEM, any_space],
        out_specs=VMEM,
        cost_estimate=cost(2 * slots * count * half, 2 * count * (half + slots)),
        compiler_params=params(16),
        name="own_sums",
    )(place, turned, held, send)
    send = pl.pallas_call(
        pair_kernel,
        out_shape=jax.ShapeDtypeStruct((slots, half + SIDE), BF16),
        in_specs=[VMEM] * 3,
        out_specs=VMEM,
        cost_estimate=cost(0, 6 * slots * model, 128 * slots * model),
        compiler_params=params(16),
        name="pair",
    )(keep, side, received)
    received = lax.all_to_all(send.reshape(groups, rows, -1), "wide", split_axis=0, concat_axis=0, tiled=True)
    send = pl.pallas_call(
        merge_kernel,
        out_shape=jax.ShapeDtypeStruct((rows, half + SIDE), BF16),
        in_specs=[VMEM],
        out_specs=VMEM,
        compiler_params=params(16),
        name="merge",
    )(received)
    axes = ("rest", "pair")
    mine = [send] + [move(send, axes, (r, 0)) for r in range(1, rest)]
    others = [move(send, axes, (r, 1)) for r in reversed(range(rest))]
    combine = pl.pallas_call(
        combine_kernel,
        out_shape=jax.ShapeDtypeStruct((count, slots), BF16),
        in_specs=[VMEM, any_space],
        out_specs=VMEM,
        cost_estimate=cost(8 * count * slots, 6 * count * slots, count * slots),
        compiler_params=params(16),
        name="combine",
    )(logits, send)
    experts, units = expert_out.shape[:2]
    hidden, send = pl.pallas_call(
        expert_kernel,
        out_shape=(
            jax.ShapeDtypeStruct((experts, rows, units), BF16),
            jax.ShapeDtypeStruct((rows, half), BF16),
        ),
        in_specs=[SMEM, VMEM, VMEM, any_space] + [VMEM] * (2 * rest),
        out_specs=(VMEM, VMEM),
        compiler_params=params(8),
        name="experts",
    )(place, expert_in, expert_out, combine, *mine, *others)
    received = swap_pair(send)
    keep = pl.pallas_call(
        own_kernel,
        out_shape=jax.ShapeDtypeStruct((rows, half), F32),
        in_specs=[SMEM, VMEM, VMEM, any_space],
        out_specs=VMEM,
        cost_estimate=cost(2 * rows * units * half * experts, 2 * experts * units * half),
        compiler_params=params(8),
        name="own",
    )(place, hidden, expert_out, send)
    partial = (keep + received.astype(F32)).astype(BF16)
    partials = jnp.broadcast_to(partial, (groups * rest, rows, half))
    partials = lax.all_to_all(partials, ("rest", "wide"), split_axis=0, concat_axis=0, tiled=True)
    slot_out = jnp.sum(partials.reshape(rest, groups, rows, half).astype(F32), axis=0)
    slot_out = slot_out.astype(BF16).reshape(slots, half)
    other = swap_pair(slot_out)
    done, blocks = count // 2, 8
    mixed, left = pl.pallas_call(
        mix_kernel,
        out_shape=(
            pltpu.HBM((count, model), BF16),
            jax.ShapeDtypeStruct((count - done, half), BF16),
        ),
        in_specs=[SMEM, VMEM, VMEM],
        out_specs=(HBM, VMEM),
        scratch_shapes=[pltpu.VMEM((done, half), BF16), pltpu.SemaphoreType.DMA((blocks // 2,))],
        cost_estimate=cost(2 * count * slots * half, 2 * count * (half + slots)),
        compiler_params=params(16),
        name="mix",
    )(place, combine, slot_out)
    return pl.pallas_call(
        mix_other_kernel,
        out_shape=jax.ShapeDtypeStruct((count, model), BF16),
        in_specs=[SMEM, VMEM, VMEM, VMEM, HBM],
        out_specs=HBM,
        scratch_shapes=[pltpu.VMEM((count, half), BF16), pltpu.SemaphoreType.DMA((blocks + 1,))],
        input_output_aliases={4: 0},
        cost_estimate=cost(2 * count * slots * half, 2 * count * (half + slots)),
        compiler_params=params(16),
        name="mix_other",
    )(place, combine, other, left, mixed)


def solution(mesh):
    wide, narrow = mesh.shape["wide"], mesh.shape["narrow"]
    cut = Mesh(mesh.devices.reshape(wide, narrow // 2, 2), ("wide", "rest", "pair"))
    narrow_axes = ("rest", "pair")
    return jax.shard_map(
        shards,
        mesh=cut,
        in_specs=(
            P(("wide",) + narrow_axes, None),
            P(),
            P("wide", None, narrow_axes),
            P("wide", narrow_axes, None),
        ),
        out_specs=P(("wide",) + narrow_axes, None),
        check_vma=False,
    )
```

```python
import math

import jax
import jax.numpy as jnp
from jax import lax
from jax.experimental import pallas as pl
from jax.experimental.pallas import tpu as pltpu
from jax.sharding import Mesh, PartitionSpec as P

SLOT_PER = 4
SIDE = 128
CHUNK, TOGETHER = 256, 2
F32 = jnp.float32
BF16 = jnp.bfloat16
VMEM = pl.BlockSpec(memory_space=pltpu.VMEM)
SMEM = pl.BlockSpec(memory_space=pltpu.SMEM)
HBM = pl.BlockSpec(memory_space=pltpu.HBM)
MIB = 1024 * 1024


def params(mib):
    return pltpu.CompilerParams(vmem_limit_bytes=mib * MIB)


def cost(flops, moved, transcendentals=0):
    return pl.CostEstimate(flops=flops, bytes_accessed=moved, transcendentals=transcendentals)


def in_hbm(value):
    return pltpu.with_memory_space_constraint(value, pltpu.HBM)


def dot(lhs, rhs):
    return jnp.dot(lhs, rhs, preferred_element_type=F32)


def side_state(*columns):
    lane = lax.broadcasted_iota(jnp.int32, (columns[0].shape[0], SIDE), 1)
    out = jnp.zeros((columns[0].shape[0], SIDE), F32)
    for index, value in enumerate(columns):
        out = jnp.where(lane == index, value, out)
    return out


def side_message(peak, total):
    lane = lax.broadcasted_iota(jnp.int32, (peak.shape[0], SIDE), 1)
    out = jnp.zeros((peak.shape[0], SIDE), F32)
    for index, value in enumerate((peak, total)):
        for piece in range(3):
            part = value.astype(BF16).astype(F32)
            out = jnp.where(lane == 3 * index + piece, part, out)
            value = value - part
    return out.astype(BF16)


def read_message(side):
    value = side.astype(F32)
    return (
        value[:, 0:1] + value[:, 1:2] + value[:, 2:3],
        value[:, 3:4] + value[:, 4:5] + value[:, 5:6],
    )


def column_half(side, half):
    return pl.ds(pl.multiple_of(side * half, half), half)


def gather_kernel(place, tokens, slot_params, logits, turned, held, side, send, table, sems):
    chunks = tokens.shape[0] // CHUNK
    slots = slot_params.shape[1]
    half = held.shape[1] // 2
    spans = [pl.ds(i * CHUNK, CHUNK) for i in range(chunks)]
    table_copy = pltpu.make_async_copy(slot_params, table, sems.at[chunks])
    table_copy.start()
    copies = [pltpu.make_async_copy(tokens.at[span], held.at[span], sems.at[i]) for i, span in enumerate(spans)]
    for copy in copies:
        copy.start()

    def find_peak(parts, high=None):
        for part in parts:
            top = jnp.max(part.reshape(CHUNK // 8, 8, slots), axis=0)
            high = top if high is None else jnp.maximum(high, top)
        return high

    def weigh(first, parts, peak):
        total = jnp.zeros((8, slots), F32)
        columns = []
        for part in parts:
            weights = jnp.exp(part - peak)
            total = total + jnp.sum(weights.reshape(CHUNK // 8, 8, slots), axis=0)
            columns.append(weights.astype(BF16).T)
        weights = jnp.concatenate(columns, axis=1)
        span = pl.ds(first * CHUNK, len(parts) * CHUNK)
        turned[:, span] = weights
        sums = dot(weights, held[span, column_half(1 - place[0], half)])
        return sums, jnp.sum(total, axis=0, keepdims=True)

    table_copy.wait()
    high = None
    for first in range(0, chunks, TOGETHER):
        for copy in copies[first : first + TOGETHER]:
            copy.wait()
        parts = [dot(held[span, :], table[...]) for span in spans[first : first + TOGETHER]]
        for part, span in zip(parts, spans[first:]):
            logits[span, :] = part
        if first + TOGETHER < chunks:
            high = find_peak(parts, high)
    early_peak = jnp.max(high, axis=0, keepdims=True)
    early, early_total = weigh(0, [logits[span, :] for span in spans[:first]], early_peak)
    late_peak = jnp.max(find_peak(parts), axis=0, keepdims=True)
    late, late_total = weigh(first, parts, late_peak)
    peak = jnp.maximum(early_peak, late_peak)
    early_scale, late_scale = jnp.exp(early_peak - peak), jnp.exp(late_peak - peak)
    total = early_total * early_scale + late_total * late_scale
    row = lax.broadcasted_iota(jnp.int32, (8, slots), 0)
    columns = jnp.zeros((8, slots), F32)
    for index, value in enumerate((peak, total, early_scale, late_scale)):
        columns = jnp.where(row == index, value, columns)
    columns = columns.T
    peak, total, early_scale, late_scale = [columns[:, i : i + 1] for i in range(4)]
    send[:, :half] = (early * early_scale + late * late_scale).astype(BF16)
    side[...] = side_state(peak, total, early_scale, late_scale)
    send[:, half:] = side_message(peak, total)


def own_sums_kernel(place, turned, held, side, after, keep):
    columns = column_half(place[0], keep.shape[1])
    early = held.shape[0] - TOGETHER * CHUNK
    spans = (pl.ds(0, early), pl.ds(early, TOGETHER * CHUNK))
    early, late = [dot(turned[:, span], held[span, columns]) for span in spans]
    keep[...] = early * side[:, 2:3] + late * side[:, 3:4]


def pair_kernel(keep, side, received, send):
    width = keep.shape[1]
    peak_mine, total_mine = side[:, 0:1], side[:, 1:2]
    peak_other, total_other = read_message(received[:, width:])
    peak = jnp.maximum(peak_mine, peak_other)
    scale_mine, scale_other = jnp.exp(peak_mine - peak), jnp.exp(peak_other - peak)
    total = total_mine * scale_mine + total_other * scale_other
    sums = keep[...] * scale_mine + received[:, :width].astype(F32) * scale_other
    send[:, :width] = sums.astype(BF16)
    send[:, width:] = side_message(peak, total)


def add_parts(parts, width):
    states = [read_message(part[:, width:]) for part in parts]
    peak = states[0][0]
    for other, _ in states[1:]:
        peak = jnp.maximum(peak, other)
    total = jnp.zeros_like(peak)
    sums = jnp.zeros((parts[0].shape[0], width), F32)
    for part, (peak_other, total_other) in zip(parts, states):
        scale = jnp.exp(peak_other - peak)
        total = total + total_other * scale
        sums = sums + part[:, :width].astype(F32) * scale
    return sums, peak, total


def merge_kernel(received, send):
    width = send.shape[1] - SIDE
    sums, peak, total = add_parts([received[g] for g in range(received.shape[0])], width)
    send[:, :width] = sums.astype(BF16)
    send[:, width:] = side_message(peak, total)


def find_slot_in(place, mine, others):
    half = mine[0].shape[1] - SIDE
    means = []
    for parts in (mine, others):
        sums, _, total = add_parts([part[...] for part in parts], half)
        means.append((sums / total).astype(BF16))
    first = place[0] == 0
    return jnp.concatenate(
        [jnp.where(first, means[0], means[1]), jnp.where(first, means[1], means[0])], axis=1
    )


def second_product(hidden, weights, columns):
    row = lax.broadcasted_iota(jnp.int32, (hidden[0].shape[0], 1), 0)
    result = 0.0
    for e, value in enumerate(hidden):
        result = jnp.where(row // SLOT_PER == e, dot(value, weights[e, :, columns]), result)
    return result


def expert_kernel(place, expert_in, expert_out, after, *refs):
    parts, hidden, send = refs[:-2], refs[-2], refs[-1]
    count = len(parts) // 2
    slot_in = find_slot_in(place, parts[:count], parts[count:])
    values = []
    for e in range(expert_in.shape[0]):
        values.append(jax.nn.gelu(dot(slot_in, expert_in[e])).astype(BF16))
        hidden[e] = values[e]
    send[...] = second_product(values, expert_out, column_half(1 - place[0], send.shape[1])).astype(BF16)


def own_kernel(place, hidden, expert_out, after, keep):
    values = [hidden[e] for e in range(hidden.shape[0])]
    keep[...] = second_product(values, expert_out, column_half(place[0], keep.shape[1]))


def combine_kernel(logits, after, combine):
    value = logits[...]
    weights = jnp.exp(value - jnp.max(value, axis=1, keepdims=True))
    combine[...] = (weights / jnp.sum(weights, axis=1, keepdims=True)).astype(BF16)


def mix_kernel(place, combine, slot_out, mixed, rest, held, sems):
    width = slot_out.shape[1]
    tokens, done = combine.shape[0], held.shape[0]
    block = done // sems.shape[0]
    columns = pl.ds(pl.multiple_of(place[0] * width, width), width)
    copies = []
    for i in range(tokens // block):
        rows = pl.ds(i * block, block)
        value = dot(combine[rows, :], slot_out[...]).astype(BF16)
        if i < sems.shape[0]:
            held[rows, :] = value
            copies.append(pltpu.make_async_copy(held.at[rows], mixed.at[rows, columns], sems.at[i]))
            copies[-1].start()
        else:
            rest[pl.ds(i * block - done, block), :] = value
    for copy in copies:
        copy.wait()


def mix_other_kernel(place, combine, slot_out, rest, before, mixed, held, sems):
    width = slot_out.shape[1]
    blocks = sems.shape[0] - 1
    tokens = combine.shape[0]
    done = tokens - rest.shape[0]
    mine = pl.ds(pl.multiple_of(place[0] * width, width), width)
    other = pl.ds(pl.multiple_of((1 - place[0]) * width, width), width)
    copies = [pltpu.make_async_copy(rest, mixed.at[pl.ds(done, tokens - done), mine], sems.at[blocks])]
    copies[0].start()
    block = tokens // blocks
    for i in range(blocks):
        rows = pl.ds(i * block, block)
        held[rows, :] = dot(combine[rows, :], slot_out[...]).astype(BF16)
        copies.append(pltpu.make_async_copy(held.at[rows], mixed.at[rows, other], sems.at[i]))
        copies[-1].start()
    for copy in copies:
        copy.wait()


def move(value, axes, offsets):
    sizes = [lax.axis_size(axis) for axis in axes]
    moves = []
    for index in range(math.prod(sizes)):
        source, target, stride = index, 0, 1
        for size, offset in zip(reversed(sizes), reversed(offsets)):
            target += (source % size + offset) % size * stride
            source //= size
            stride *= size
        moves.append((index, target))
    return lax.ppermute(value, axes, moves)


def swap_pair(value):
    return move(value, ("pair",), (1,))


def shards(tokens, slot_params, expert_in, expert_out):
    count, model = tokens.shape
    slots = slot_params.shape[1]
    groups, rest = lax.axis_size("wide"), lax.axis_size("rest")
    rows = slots // groups
    half = model // 2
    place = lax.axis_index("pair").astype(jnp.int32).reshape(1)
    any_space = pl.BlockSpec(memory_space=pl.ANY)

    logits, turned, held, side, send = pl.pallas_call(
        gather_kernel,
        out_shape=(
            jax.ShapeDtypeStruct((count, slots), F32),
            jax.ShapeDtypeStruct((slots, count), BF16),
            jax.ShapeDtypeStruct((count, model), BF16),
            jax.ShapeDtypeStruct((slots, SIDE), F32),
            jax.ShapeDtypeStruct((slots, half + SIDE), BF16),
        ),
        in_specs=[SMEM, HBM, HBM],
        out_specs=(VMEM,) * 5,
        scratch_shapes=[pltpu.VMEM((model, slots), BF16), pltpu.SemaphoreType.DMA((count // CHUNK + 1,))],
        compiler_params=params(24),
        name="gather",
    )(place, in_hbm(tokens), in_hbm(slot_params))
    received = swap_pair(send)
    keep = pl.pallas_call(
        own_sums_kernel,
        out_shape=jax.ShapeDtypeStruct((slots, half), F32),
        in_specs=[SMEM, VMEM, VMEM, VMEM, any_space],
        out_specs=VMEM,
        cost_estimate=cost(2 * slots * count * half, 2 * count * (half + slots)),
        compiler_params=params(16),
        name="own_sums",
    )(place, turned, held, side, send)
    send = pl.pallas_call(
        pair_kernel,
        out_shape=jax.ShapeDtypeStruct((slots, half + SIDE), BF16),
        in_specs=[VMEM] * 3,
        out_specs=VMEM,
        cost_estimate=cost(0, 6 * slots * model, 128 * slots * model),
        compiler_params=params(16),
        name="pair",
    )(keep, side, received)
    received = lax.all_to_all(send.reshape(groups, rows, -1), "wide", split_axis=0, concat_axis=0, tiled=True)
    send = pl.pallas_call(
        merge_kernel,
        out_shape=jax.ShapeDtypeStruct((rows, half + SIDE), BF16),
        in_specs=[VMEM],
        out_specs=VMEM,
        compiler_params=params(16),
        name="merge",
    )(received)
    axes = ("rest", "pair")
    mine = [send] + [move(send, axes, (r, 0)) for r in range(1, rest)]
    others = [move(send, axes, (r, 1)) for r in reversed(range(rest))]
    combine = pl.pallas_call(
        combine_kernel,
        out_shape=jax.ShapeDtypeStruct((count, slots), BF16),
        in_specs=[VMEM, any_space],
        out_specs=VMEM,
        cost_estimate=cost(8 * count * slots, 6 * count * slots, count * slots),
        compiler_params=params(16),
        name="combine",
    )(logits, send)
    experts, units = expert_out.shape[:2]
    hidden, send = pl.pallas_call(
        expert_kernel,
        out_shape=(
            jax.ShapeDtypeStruct((experts, rows, units), BF16),
            jax.ShapeDtypeStruct((rows, half), BF16),
        ),
        in_specs=[SMEM, VMEM, VMEM, any_space] + [VMEM] * (2 * rest),
        out_specs=(VMEM, VMEM),
        compiler_params=params(8),
        name="experts",
    )(place, expert_in, expert_out, combine, *mine, *others)
    received = swap_pair(send)
    keep = pl.pallas_call(
        own_kernel,
        out_shape=jax.ShapeDtypeStruct((rows, half), F32),
        in_specs=[SMEM, VMEM, VMEM, any_space],
        out_specs=VMEM,
        cost_estimate=cost(2 * rows * units * half * experts, 2 * experts * units * half),
        compiler_params=params(8),
        name="own",
    )(place, hidden, expert_out, send)
    partial = (keep + received.astype(F32)).astype(BF16)
    partials = jnp.broadcast_to(partial, (groups * rest, rows, half))
    partials = lax.all_to_all(partials, ("rest", "wide"), split_axis=0, concat_axis=0, tiled=True)
    slot_out = jnp.sum(partials.reshape(rest, groups, rows, half).astype(F32), axis=0)
    slot_out = slot_out.astype(BF16).reshape(slots, half)
    other = swap_pair(slot_out)
    done, blocks = count // 2, 8
    mixed, left = pl.pallas_call(
        mix_kernel,
        out_shape=(
            pltpu.HBM((count, model), BF16),
            jax.ShapeDtypeStruct((count - done, half), BF16),
        ),
        in_specs=[SMEM, VMEM, VMEM],
        out_specs=(HBM, VMEM),
        scratch_shapes=[pltpu.VMEM((done, half), BF16), pltpu.SemaphoreType.DMA((blocks // 2,))],
        cost_estimate=cost(2 * count * slots * half, 2 * count * (half + slots)),
        compiler_params=params(16),
        name="mix",
    )(place, combine, slot_out)
    return pl.pallas_call(
        mix_other_kernel,
        out_shape=jax.ShapeDtypeStruct((count, model), BF16),
        in_specs=[SMEM, VMEM, VMEM, VMEM, HBM],
        out_specs=HBM,
        scratch_shapes=[pltpu.VMEM((count, half), BF16), pltpu.SemaphoreType.DMA((blocks + 1,))],
        input_output_aliases={4: 0},
        cost_estimate=cost(2 * count * slots * half, 2 * count * (half + slots)),
        compiler_params=params(16),
        name="mix_other",
    )(place, combine, other, left, mixed)


def solution(mesh):
    wide, narrow = mesh.shape["wide"], mesh.shape["narrow"]
    cut = Mesh(mesh.devices.reshape(wide, narrow // 2, 2), ("wide", "rest", "pair"))
    narrow_axes = ("rest", "pair")
    return jax.shard_map(
        shards,
        mesh=cut,
        in_specs=(
            P(("wide",) + narrow_axes, None),
            P(),
            P("wide", None, narrow_axes),
            P("wide", narrow_axes, None),
        ),
        out_specs=P(("wide",) + narrow_axes, None),
        check_vma=False,
    )
```

```python
import math

import jax
import jax.numpy as jnp
from jax import lax
from jax.experimental import pallas as pl
from jax.experimental.pallas import tpu as pltpu
from jax.sharding import Mesh, PartitionSpec as P

SLOT_PER = 4
SIDE = 128
CHUNK, TOGETHER = 256, 2
F32 = jnp.float32
BF16 = jnp.bfloat16
VMEM = pl.BlockSpec(memory_space=pltpu.VMEM)
SMEM = pl.BlockSpec(memory_space=pltpu.SMEM)
HBM = pl.BlockSpec(memory_space=pltpu.HBM)
MIB = 1024 * 1024


def params(mib):
    return pltpu.CompilerParams(vmem_limit_bytes=mib * MIB)


def cost(flops, moved, transcendentals=0):
    return pl.CostEstimate(flops=flops, bytes_accessed=moved, transcendentals=transcendentals)


def in_hbm(value):
    return pltpu.with_memory_space_constraint(value, pltpu.HBM)


def dot(lhs, rhs):
    return jnp.dot(lhs, rhs, preferred_element_type=F32)


def side_state(*columns):
    lane = lax.broadcasted_iota(jnp.int32, (columns[0].shape[0], SIDE), 1)
    out = jnp.zeros((columns[0].shape[0], SIDE), F32)
    for index, value in enumerate(columns):
        out = jnp.where(lane == index, value, out)
    return out


def side_message(peak, total):
    lane = lax.broadcasted_iota(jnp.int32, (peak.shape[0], SIDE), 1)
    out = jnp.zeros((peak.shape[0], SIDE), F32)
    for index, value in enumerate((peak, total)):
        for piece in range(3):
            part = value.astype(BF16).astype(F32)
            out = jnp.where(lane == 3 * index + piece, part, out)
            value = value - part
    return out.astype(BF16)


def read_message(side):
    value = side.astype(F32)
    return (
        value[:, 0:1] + value[:, 1:2] + value[:, 2:3],
        value[:, 3:4] + value[:, 4:5] + value[:, 5:6],
    )


def column_half(side, half):
    return pl.ds(pl.multiple_of(side * half, half), half)


def gather_kernel(place, tokens, slot_params, logits, turned, held, side, send, table, sems):
    chunks = tokens.shape[0] // CHUNK
    slots = slot_params.shape[1]
    half = held.shape[1] // 2
    spans = [pl.ds(i * CHUNK, CHUNK) for i in range(chunks)]
    table_copy = pltpu.make_async_copy(slot_params, table, sems.at[chunks])
    table_copy.start()
    copies = [pltpu.make_async_copy(tokens.at[span], held.at[span], sems.at[i]) for i, span in enumerate(spans)]
    for copy in copies:
        copy.start()

    def find_peak(parts, high=None):
        for part in parts:
            top = jnp.max(part.reshape(CHUNK // 8, 8, slots), axis=0)
            high = top if high is None else jnp.maximum(high, top)
        return high

    def weigh(first, parts, peak):
        total = jnp.zeros((8, slots), F32)
        columns = []
        for part in parts:
            weights = jnp.exp(part - peak)
            total = total + jnp.sum(weights.reshape(CHUNK // 8, 8, slots), axis=0)
            columns.append(weights.astype(BF16).T)
        weights = jnp.concatenate(columns, axis=1)
        span = pl.ds(first * CHUNK, len(parts) * CHUNK)
        turned[:, span] = weights
        sums = dot(weights, held[span, column_half(1 - place[0], half)])
        return sums, jnp.sum(total, axis=0, keepdims=True)

    table_copy.wait()
    high = None
    for first in range(0, chunks, TOGETHER):
        for copy in copies[first : first + TOGETHER]:
            copy.wait()
        parts = [dot(held[span, :], table[...]) for span in spans[first : first + TOGETHER]]
        for part, span in zip(parts, spans[first:]):
            logits[span, :] = part
        if first + TOGETHER < chunks:
            high = find_peak(parts, high)
    early_peak = jnp.max(high, axis=0, keepdims=True)
    early, early_total = weigh(0, [logits[span, :] for span in spans[:first]], early_peak)
    late_peak = jnp.max(find_peak(parts), axis=0, keepdims=True)
    late, late_total = weigh(first, parts, late_peak)
    peak = jnp.maximum(early_peak, late_peak)
    early_scale, late_scale = jnp.exp(early_peak - peak), jnp.exp(late_peak - peak)
    total = early_total * early_scale + late_total * late_scale
    row = lax.broadcasted_iota(jnp.int32, (8, slots), 0)
    columns = jnp.zeros((8, slots), F32)
    for index, value in enumerate((peak, total, early_scale, late_scale)):
        columns = jnp.where(row == index, value, columns)
    columns = columns.T
    peak, total, early_scale, late_scale = [columns[:, i : i + 1] for i in range(4)]
    send[:, :half] = (early * early_scale + late * late_scale).astype(BF16)
    side[...] = side_state(peak, total, early_scale, late_scale)
    send[:, half:] = side_message(peak, total)


def own_sums_kernel(place, turned, held, side, after, keep):
    columns = column_half(place[0], keep.shape[1])
    early = held.shape[0] - TOGETHER * CHUNK
    spans = (pl.ds(0, early), pl.ds(early, TOGETHER * CHUNK))
    early, late = [dot(turned[:, span], held[span, columns]) for span in spans]
    keep[...] = early * side[:, 2:3] + late * side[:, 3:4]


def pair_kernel(keep, side, received, send):
    width = keep.shape[1]
    peak_mine, total_mine = side[:, 0:1], side[:, 1:2]
    peak_other, total_other = read_message(received[:, width:])
    peak = jnp.maximum(peak_mine, peak_other)
    scale_mine, scale_other = jnp.exp(peak_mine - peak), jnp.exp(peak_other - peak)
    total = total_mine * scale_mine + total_other * scale_other
    sums = keep[...] * scale_mine + received[:, :width].astype(F32) * scale_other
    send[:, :width] = sums.astype(BF16)
    send[:, width:] = side_message(peak, total)


def add_parts(parts, width):
    states = [read_message(part[:, width:]) for part in parts]
    peak = states[0][0]
    for other, _ in states[1:]:
        peak = jnp.maximum(peak, other)
    total = jnp.zeros_like(peak)
    sums = jnp.zeros((parts[0].shape[0], width), F32)
    for part, (peak_other, total_other) in zip(parts, states):
        scale = jnp.exp(peak_other - peak)
        total = total + total_other * scale
        sums = sums + part[:, :width].astype(F32) * scale
    return sums, peak, total


def merge_kernel(received, send):
    width = send.shape[1] - SIDE
    sums, peak, total = add_parts([received[g] for g in range(received.shape[0])], width)
    send[:, :width] = sums.astype(BF16)
    send[:, width:] = side_message(peak, total)


def finish_kernel(combine, *refs):
    slot_in = refs[-1]
    sums, _, total = add_parts([ref[...] for ref in refs[:-1]], slot_in.shape[1])
    slot_in[...] = (sums / total).astype(BF16)


def first_product_kernel(place, slot_in, expert_in, result):
    half = slot_in.shape[1]
    for e in range(expert_in.shape[0]):
        result[e] = dot(slot_in[...], expert_in[e, column_half(place[0], half), :])


def second_product(hidden, weights, columns):
    row = lax.broadcasted_iota(jnp.int32, (hidden[0].shape[0], 1), 0)
    result = 0.0
    for e, value in enumerate(hidden):
        result = jnp.where(row // SLOT_PER == e, dot(value, weights[e, :, columns]), result)
    return result


def expert_kernel(place, slot_in, first, expert_in, expert_out, hidden, send):
    half = slot_in.shape[1]
    values = []
    for e in range(expert_in.shape[0]):
        product = first[e] + dot(slot_in[...], expert_in[e, column_half(1 - place[0], half), :])
        values.append(jax.nn.gelu(product).astype(BF16))
        hidden[e] = values[e]
    send[...] = second_product(values, expert_out, column_half(1 - place[0], half)).astype(BF16)


def own_kernel(place, hidden, expert_out, after, keep):
    values = [hidden[e] for e in range(hidden.shape[0])]
    keep[...] = second_product(values, expert_out, column_half(place[0], keep.shape[1]))


def combine_kernel(logits, after, combine):
    value = logits[...]
    weights = jnp.exp(value - jnp.max(value, axis=1, keepdims=True))
    combine[...] = (weights / jnp.sum(weights, axis=1, keepdims=True)).astype(BF16)


def mix_kernel(place, combine, slot_out, mixed, rest, held, sems):
    width = slot_out.shape[1]
    tokens, done = combine.shape[0], held.shape[0]
    block = done // sems.shape[0]
    columns = pl.ds(pl.multiple_of(place[0] * width, width), width)
    copies = []
    for i in range(tokens // block):
        rows = pl.ds(i * block, block)
        value = dot(combine[rows, :], slot_out[...]).astype(BF16)
        if i < sems.shape[0]:
            held[rows, :] = value
            copies.append(pltpu.make_async_copy(held.at[rows], mixed.at[rows, columns], sems.at[i]))
            copies[-1].start()
        else:
            rest[pl.ds(i * block - done, block), :] = value
    for copy in copies:
        copy.wait()


def mix_other_kernel(place, combine, slot_out, rest, before, mixed, held, sems):
    width = slot_out.shape[1]
    blocks = sems.shape[0] - 1
    tokens = combine.shape[0]
    done = tokens - rest.shape[0]
    mine = pl.ds(pl.multiple_of(place[0] * width, width), width)
    other = pl.ds(pl.multiple_of((1 - place[0]) * width, width), width)
    copies = [pltpu.make_async_copy(rest, mixed.at[pl.ds(done, tokens - done), mine], sems.at[blocks])]
    copies[0].start()
    block = tokens // blocks
    for i in range(blocks):
        rows = pl.ds(i * block, block)
        held[rows, :] = dot(combine[rows, :], slot_out[...]).astype(BF16)
        copies.append(pltpu.make_async_copy(held.at[rows], mixed.at[rows, other], sems.at[i]))
        copies[-1].start()
    for copy in copies:
        copy.wait()


def move(value, axes, offsets):
    sizes = [lax.axis_size(axis) for axis in axes]
    moves = []
    for index in range(math.prod(sizes)):
        source, target, stride = index, 0, 1
        for size, offset in zip(reversed(sizes), reversed(offsets)):
            target += (source % size + offset) % size * stride
            source //= size
            stride *= size
        moves.append((index, target))
    return lax.ppermute(value, axes, moves)


def swap_pair(value):
    return move(value, ("pair",), (1,))


def shards(tokens, slot_params, expert_in, expert_out):
    count, model = tokens.shape
    slots = slot_params.shape[1]
    groups, rest = lax.axis_size("wide"), lax.axis_size("rest")
    rows = slots // groups
    half = model // 2
    place = lax.axis_index("pair").astype(jnp.int32).reshape(1)
    any_space = pl.BlockSpec(memory_space=pl.ANY)

    logits, turned, held, side, send = pl.pallas_call(
        gather_kernel,
        out_shape=(
            jax.ShapeDtypeStruct((count, slots), F32),
            jax.ShapeDtypeStruct((slots, count), BF16),
            jax.ShapeDtypeStruct((count, model), BF16),
            jax.ShapeDtypeStruct((slots, SIDE), F32),
            jax.ShapeDtypeStruct((slots, half + SIDE), BF16),
        ),
        in_specs=[SMEM, HBM, HBM],
        out_specs=(VMEM,) * 5,
        scratch_shapes=[pltpu.VMEM((model, slots), BF16), pltpu.SemaphoreType.DMA((count // CHUNK + 1,))],
        compiler_params=params(24),
        name="gather",
    )(place, in_hbm(tokens), in_hbm(slot_params))
    received = swap_pair(send)
    keep = pl.pallas_call(
        own_sums_kernel,
        out_shape=jax.ShapeDtypeStruct((slots, half), F32),
        in_specs=[SMEM, VMEM, VMEM, VMEM, any_space],
        out_specs=VMEM,
        cost_estimate=cost(2 * slots * count * half, 2 * count * (half + slots)),
        compiler_params=params(16),
        name="own_sums",
    )(place, turned, held, side, send)
    send = pl.pallas_call(
        pair_kernel,
        out_shape=jax.ShapeDtypeStruct((slots, half + SIDE), BF16),
        in_specs=[VMEM] * 3,
        out_specs=VMEM,
        cost_estimate=cost(0, 6 * slots * model, 128 * slots * model),
        compiler_params=params(16),
        name="pair",
    )(keep, side, received)
    received = lax.all_to_all(send.reshape(groups, rows, -1), "wide", split_axis=0, concat_axis=0, tiled=True)
    send = pl.pallas_call(
        merge_kernel,
        out_shape=jax.ShapeDtypeStruct((rows, half + SIDE), BF16),
        in_specs=[VMEM],
        out_specs=VMEM,
        compiler_params=params(16),
        name="merge",
    )(received)
    mine = [send] + [move(send, ("rest",), (r,)) for r in range(1, rest)]
    combine = pl.pallas_call(
        combine_kernel,
        out_shape=jax.ShapeDtypeStruct((count, slots), BF16),
        in_specs=[VMEM, any_space],
        out_specs=VMEM,
        cost_estimate=cost(8 * count * slots, 6 * count * slots, count * slots),
        compiler_params=params(16),
        name="combine",
    )(logits, send)
    experts, units = expert_out.shape[:2]
    slot_in = pl.pallas_call(
        finish_kernel,
        out_shape=jax.ShapeDtypeStruct((rows, half), BF16),
        in_specs=[any_space] + [VMEM] * rest,
        out_specs=VMEM,
        compiler_params=params(16),
        name="finish",
    )(combine, *mine)
    other = swap_pair(slot_in)
    first = pl.pallas_call(
        first_product_kernel,
        out_shape=jax.ShapeDtypeStruct((experts, rows, units), F32),
        in_specs=[SMEM, VMEM, VMEM],
        out_specs=VMEM,
        cost_estimate=cost(2 * rows * units * half * experts, 2 * experts * units * half),
        compiler_params=params(8),
        name="first_product",
    )(place, slot_in, expert_in)
    hidden, send = pl.pallas_call(
        expert_kernel,
        out_shape=(
            jax.ShapeDtypeStruct((experts, rows, units), BF16),
            jax.ShapeDtypeStruct((rows, half), BF16),
        ),
        in_specs=[SMEM, VMEM, VMEM, VMEM, VMEM],
        out_specs=(VMEM, VMEM),
        compiler_params=params(8),
        name="experts",
    )(place, other, first, expert_in, expert_out)
    received = swap_pair(send)
    keep = pl.pallas_call(
        own_kernel,
        out_shape=jax.ShapeDtypeStruct((rows, half), F32),
        in_specs=[SMEM, VMEM, VMEM, any_space],
        out_specs=VMEM,
        cost_estimate=cost(2 * rows * units * half * experts, 2 * experts * units * half),
        compiler_params=params(8),
        name="own",
    )(place, hidden, expert_out, send)
    partial = (keep + received.astype(F32)).astype(BF16)
    partials = jnp.broadcast_to(partial, (groups * rest, rows, half))
    partials = lax.all_to_all(partials, ("rest", "wide"), split_axis=0, concat_axis=0, tiled=True)
    slot_out = jnp.sum(partials.reshape(rest, groups, rows, half).astype(F32), axis=0)
    slot_out = slot_out.astype(BF16).reshape(slots, half)
    other = swap_pair(slot_out)
    done, blocks = count // 2, 8
    mixed, left = pl.pallas_call(
        mix_kernel,
        out_shape=(
            pltpu.HBM((count, model), BF16),
            jax.ShapeDtypeStruct((count - done, half), BF16),
        ),
        in_specs=[SMEM, VMEM, VMEM],
        out_specs=(HBM, VMEM),
        scratch_shapes=[pltpu.VMEM((done, half), BF16), pltpu.SemaphoreType.DMA((blocks // 2,))],
        cost_estimate=cost(2 * count * slots * half, 2 * count * (half + slots)),
        compiler_params=params(16),
        name="mix",
    )(place, combine, slot_out)
    return pl.pallas_call(
        mix_other_kernel,
        out_shape=jax.ShapeDtypeStruct((count, model), BF16),
        in_specs=[SMEM, VMEM, VMEM, VMEM, HBM],
        out_specs=HBM,
        scratch_shapes=[pltpu.VMEM((count, half), BF16), pltpu.SemaphoreType.DMA((blocks + 1,))],
        input_output_aliases={4: 0},
        cost_estimate=cost(2 * count * slots * half, 2 * count * (half + slots)),
        compiler_params=params(16),
        name="mix_other",
    )(place, combine, other, left, mixed)


def solution(mesh):
    wide, narrow = mesh.shape["wide"], mesh.shape["narrow"]
    cut = Mesh(mesh.devices.reshape(wide, narrow // 2, 2), ("wide", "rest", "pair"))
    narrow_axes = ("rest", "pair")
    return jax.shard_map(
        shards,
        mesh=cut,
        in_specs=(
            P(("wide",) + narrow_axes, None),
            P(),
            P("wide", None, narrow_axes),
            P("wide", narrow_axes, None),
        ),
        out_specs=P(("wide",) + narrow_axes, None),
        check_vma=False,
    )
```

```python
import math

import jax
import jax.numpy as jnp
from jax import lax
from jax.experimental import pallas as pl
from jax.experimental.pallas import tpu as pltpu
from jax.sharding import Mesh, PartitionSpec as P

SLOT_PER = 4
SIDE = 128
CHUNK, TOGETHER = 256, 2
F32 = jnp.float32
BF16 = jnp.bfloat16
VMEM = pl.BlockSpec(memory_space=pltpu.VMEM)
SMEM = pl.BlockSpec(memory_space=pltpu.SMEM)
HBM = pl.BlockSpec(memory_space=pltpu.HBM)
MIB = 1024 * 1024


def params(mib):
    return pltpu.CompilerParams(vmem_limit_bytes=mib * MIB)


def cost(flops, moved, transcendentals=0):
    return pl.CostEstimate(flops=flops, bytes_accessed=moved, transcendentals=transcendentals)


def in_hbm(value):
    return pltpu.with_memory_space_constraint(value, pltpu.HBM)


def dot(lhs, rhs):
    return jnp.dot(lhs, rhs, preferred_element_type=F32)


def side_state(*columns):
    lane = lax.broadcasted_iota(jnp.int32, (columns[0].shape[0], SIDE), 1)
    out = jnp.zeros((columns[0].shape[0], SIDE), F32)
    for index, value in enumerate(columns):
        out = jnp.where(lane == index, value, out)
    return out


def side_message(peak, total):
    lane = lax.broadcasted_iota(jnp.int32, (peak.shape[0], SIDE), 1)
    out = jnp.zeros((peak.shape[0], SIDE), F32)
    for index, value in enumerate((peak, total)):
        for piece in range(3):
            part = value.astype(BF16).astype(F32)
            out = jnp.where(lane == 3 * index + piece, part, out)
            value = value - part
    return out.astype(BF16)


def read_message(side):
    value = side.astype(F32)
    return (
        value[:, 0:1] + value[:, 1:2] + value[:, 2:3],
        value[:, 3:4] + value[:, 4:5] + value[:, 5:6],
    )


def column_half(side, half):
    return pl.ds(pl.multiple_of(side * half, half), half)


def gather_kernel(place, tokens, slot_params, logits, turned, held, side, send, table, sems):
    chunks = tokens.shape[0] // CHUNK
    slots = slot_params.shape[1]
    half = held.shape[1] // 2
    spans = [pl.ds(i * CHUNK, CHUNK) for i in range(chunks)]
    table_copy = pltpu.make_async_copy(slot_params, table, sems.at[chunks])
    table_copy.start()
    copies = [pltpu.make_async_copy(tokens.at[span], held.at[span], sems.at[i]) for i, span in enumerate(spans)]
    for copy in copies:
        copy.start()

    def find_peak(parts, high=None):
        for part in parts:
            top = jnp.max(part.reshape(CHUNK // 8, 8, slots), axis=0)
            high = top if high is None else jnp.maximum(high, top)
        return high

    def weigh(first, parts, peak):
        total = jnp.zeros((8, slots), F32)
        columns = []
        for part in parts:
            weights = jnp.exp(part - peak)
            total = total + jnp.sum(weights.reshape(CHUNK // 8, 8, slots), axis=0)
            columns.append(weights.astype(BF16).T)
        weights = jnp.concatenate(columns, axis=1)
        span = pl.ds(first * CHUNK, len(parts) * CHUNK)
        turned[:, span] = weights
        sums = dot(weights, held[span, column_half(1 - place[0], half)])
        return sums, jnp.sum(total, axis=0, keepdims=True)

    table_copy.wait()
    high = None
    for first in range(0, chunks, TOGETHER):
        for copy in copies[first : first + TOGETHER]:
            copy.wait()
        parts = [dot(held[span, :], table[...]) for span in spans[first : first + TOGETHER]]
        for part, span in zip(parts, spans[first:]):
            logits[span, :] = part
        if first + TOGETHER < chunks:
            high = find_peak(parts, high)
    early_peak = jnp.max(high, axis=0, keepdims=True)
    early, early_total = weigh(0, [logits[span, :] for span in spans[:first]], early_peak)
    late_peak = jnp.max(find_peak(parts), axis=0, keepdims=True)
    late, late_total = weigh(first, parts, late_peak)
    peak = jnp.maximum(early_peak, late_peak)
    early_scale, late_scale = jnp.exp(early_peak - peak), jnp.exp(late_peak - peak)
    total = early_total * early_scale + late_total * late_scale
    row = lax.broadcasted_iota(jnp.int32, (8, slots), 0)
    columns = jnp.zeros((8, slots), F32)
    for index, value in enumerate((peak, total, early_scale, late_scale)):
        columns = jnp.where(row == index, value, columns)
    columns = columns.T
    peak, total, early_scale, late_scale = [columns[:, i : i + 1] for i in range(4)]
    send[:, :half] = (early * early_scale + late * late_scale).astype(BF16)
    side[...] = side_state(peak, total, early_scale, late_scale)
    send[:, half:] = side_message(peak, total)


def own_sums_kernel(place, turned, held, side, after, keep):
    columns = column_half(place[0], keep.shape[1])
    early = held.shape[0] - TOGETHER * CHUNK
    spans = (pl.ds(0, early), pl.ds(early, TOGETHER * CHUNK))
    early, late = [dot(turned[:, span], held[span, columns]) for span in spans]
    keep[...] = early * side[:, 2:3] + late * side[:, 3:4]


def pair_kernel(place, keep, side, received, *sends):
    width = keep.shape[1]
    for r, send in enumerate(sends):
        rows = send.shape[0]
        span = pl.ds(pl.multiple_of((place[1] ^ r) * rows, rows), rows)
        peak_mine, total_mine = side[span, 0:1], side[span, 1:2]
        peak_other, total_other = read_message(received[span, width:])
        peak = jnp.maximum(peak_mine, peak_other)
        scale_mine, scale_other = jnp.exp(peak_mine - peak), jnp.exp(peak_other - peak)
        total = total_mine * scale_mine + total_other * scale_other
        sums = keep[span, :] * scale_mine + received[span, :width].astype(F32) * scale_other
        send[:, :width] = sums.astype(BF16)
        send[:, width:] = side_message(peak, total)


def add_parts(parts, width):
    states = [read_message(part[:, width:]) for part in parts]
    peak = states[0][0]
    for other, _ in states[1:]:
        peak = jnp.maximum(peak, other)
    total = jnp.zeros_like(peak)
    sums = jnp.zeros((parts[0].shape[0], width), F32)
    for part, (peak_other, total_other) in zip(parts, states):
        scale = jnp.exp(peak_other - peak)
        total = total + total_other * scale
        sums = sums + part[:, :width].astype(F32) * scale
    return sums, peak, total


def merge_kernel(place, *refs):
    for n, send in enumerate(refs[-2:]):
        rows, width = send.shape[0], send.shape[1] - SIDE
        span = pl.ds(pl.multiple_of((place[2] ^ n) * rows, rows), rows)
        sums, peak, total = add_parts([ref[span, :] for ref in refs[:-2]], width)
        send[:, :width] = sums.astype(BF16)
        send[:, width:] = side_message(peak, total)


def finish_kernel(combine, *refs):
    slot_in = refs[-1]
    sums, _, total = add_parts([ref[...] for ref in refs[:-1]], slot_in.shape[1])
    slot_in[...] = (sums / total).astype(BF16)


def first_product_kernel(place, slot_in, expert_in, result):
    half = slot_in.shape[1]
    for e in range(expert_in.shape[0]):
        result[e] = dot(slot_in[...], expert_in[e, column_half(place[0], half), :])


def second_product(hidden, weights, columns):
    row = lax.broadcasted_iota(jnp.int32, (hidden[0].shape[0], 1), 0)
    result = 0.0
    for e, value in enumerate(hidden):
        result = jnp.where(row // SLOT_PER == e, dot(value, weights[e, :, columns]), result)
    return result


def expert_kernel(place, slot_in, first, expert_in, expert_out, hidden, send):
    half = slot_in.shape[1]
    values = []
    for e in range(expert_in.shape[0]):
        product = first[e] + dot(slot_in[...], expert_in[e, column_half(1 - place[0], half), :])
        values.append(jax.nn.gelu(product).astype(BF16))
        hidden[e] = values[e]
    send[...] = second_product(values, expert_out, column_half(1 - place[0], half)).astype(BF16)


def own_kernel(place, hidden, expert_out, after, keep):
    values = [hidden[e] for e in range(hidden.shape[0])]
    keep[...] = second_product(values, expert_out, column_half(place[0], keep.shape[1]))


def combine_kernel(place, logits, after, combine):
    value = logits[...]
    slots = value.shape[1]
    weights = jnp.exp(value - jnp.max(value, axis=1, keepdims=True))
    weights = (weights / jnp.sum(weights, axis=1, keepdims=True)).astype(BF16)
    row = lax.broadcasted_iota(jnp.int32, (slots, slots), 0)
    column = lax.broadcasted_iota(jnp.int32, (slots, slots), 1)
    swap = jnp.where(row == (column ^ place[3]), 1.0, 0.0).astype(BF16)
    combine[...] = dot(weights, swap).astype(BF16)


def mix_kernel(place, combine, slot_out, mixed, rest, held, sems):
    width = slot_out.shape[1]
    tokens, done = combine.shape[0], held.shape[0]
    block = done // sems.shape[0]
    columns = pl.ds(pl.multiple_of(place[0] * width, width), width)
    copies = []
    for i in range(tokens // block):
        rows = pl.ds(i * block, block)
        value = dot(combine[rows, :], slot_out[...]).astype(BF16)
        if i < sems.shape[0]:
            held[rows, :] = value
            copies.append(pltpu.make_async_copy(held.at[rows], mixed.at[rows, columns], sems.at[i]))
            copies[-1].start()
        else:
            rest[pl.ds(i * block - done, block), :] = value
    for copy in copies:
        copy.wait()


def mix_other_kernel(place, combine, slot_out, rest, before, mixed, held, sems):
    width = slot_out.shape[1]
    blocks = sems.shape[0] - 1
    tokens = combine.shape[0]
    done = tokens - rest.shape[0]
    mine = pl.ds(pl.multiple_of(place[0] * width, width), width)
    other = pl.ds(pl.multiple_of((1 - place[0]) * width, width), width)
    copies = [pltpu.make_async_copy(rest, mixed.at[pl.ds(done, tokens - done), mine], sems.at[blocks])]
    copies[0].start()
    block = tokens // blocks
    for i in range(blocks):
        rows = pl.ds(i * block, block)
        held[rows, :] = dot(combine[rows, :], slot_out[...]).astype(BF16)
        copies.append(pltpu.make_async_copy(held.at[rows], mixed.at[rows, other], sems.at[i]))
        copies[-1].start()
    for copy in copies:
        copy.wait()


def move(value, axes, offsets):
    sizes = [lax.axis_size(axis) for axis in axes]
    moves = []
    for index in range(math.prod(sizes)):
        source, target, stride = index, 0, 1
        for size, offset in zip(reversed(sizes), reversed(offsets)):
            target += (source % size ^ offset) * stride
            source //= size
            stride *= size
        moves.append((index, target))
    return lax.ppermute(value, axes, moves)


def swap_pair(value):
    return move(value, ("pair",), (1,))


def shards(tokens, slot_params, expert_in, expert_out):
    count, model = tokens.shape
    slots = slot_params.shape[1]
    far, near, rest = [lax.axis_size(axis) for axis in ("far", "near", "rest")]
    rows = slots // (far * near)
    half = model // 2
    far_at, near_at = lax.axis_index("far"), lax.axis_index("near")
    place = [lax.axis_index("pair"), far_at, near_at, (far_at * near + near_at) * rows]
    place = jnp.stack(place).astype(jnp.int32)
    any_space = pl.BlockSpec(memory_space=pl.ANY)

    logits, turned, held, side, send = pl.pallas_call(
        gather_kernel,
        out_shape=(
            jax.ShapeDtypeStruct((count, slots), F32),
            jax.ShapeDtypeStruct((slots, count), BF16),
            jax.ShapeDtypeStruct((count, model), BF16),
            jax.ShapeDtypeStruct((slots, SIDE), F32),
            jax.ShapeDtypeStruct((slots, half + SIDE), BF16),
        ),
        in_specs=[SMEM, HBM, HBM],
        out_specs=(VMEM,) * 5,
        scratch_shapes=[pltpu.VMEM((model, slots), BF16), pltpu.SemaphoreType.DMA((count // CHUNK + 1,))],
        compiler_params=params(24),
        name="gather",
    )(place, in_hbm(tokens), in_hbm(slot_params))
    received = swap_pair(send)
    keep = pl.pallas_call(
        own_sums_kernel,
        out_shape=jax.ShapeDtypeStruct((slots, half), F32),
        in_specs=[SMEM, VMEM, VMEM, VMEM, any_space],
        out_specs=VMEM,
        cost_estimate=cost(2 * slots * count * half, 2 * count * (half + slots)),
        compiler_params=params(16),
        name="own_sums",
    )(place, turned, held, side, send)
    sends = pl.pallas_call(
        pair_kernel,
        out_shape=(jax.ShapeDtypeStruct((near * rows, half + SIDE), BF16),) * far,
        in_specs=[SMEM] + [VMEM] * 3,
        out_specs=(VMEM,) * far,
        cost_estimate=cost(0, 6 * slots * model, 128 * slots * model),
        compiler_params=params(16),
        name="pair",
    )(place, keep, side, received)
    parts = [sends[0]] + [move(sends[r], ("far",), (r,)) for r in range(1, far)]
    send, their = pl.pallas_call(
        merge_kernel,
        out_shape=(jax.ShapeDtypeStruct((rows, half + SIDE), BF16),) * 2,
        in_specs=[SMEM] + [VMEM] * far,
        out_specs=(VMEM, VMEM),
        compiler_params=params(16),
        name="merge",
    )(place, *parts)
    plane = ("near", "rest")
    mine = [send] + [move(send, plane, (0, r)) for r in range(1, rest)]
    mine += [move(their, plane, (1, r)) for r in range(rest)]
    combine = pl.pallas_call(
        combine_kernel,
        out_shape=jax.ShapeDtypeStruct((count, slots), BF16),
        in_specs=[SMEM, VMEM, any_space],
        out_specs=VMEM,
        cost_estimate=cost(8 * count * slots, 6 * count * slots, count * slots),
        compiler_params=params(16),
        name="combine",
    )(place, logits, send)
    experts, units = expert_out.shape[:2]
    slot_in = pl.pallas_call(
        finish_kernel,
        out_shape=jax.ShapeDtypeStruct((rows, half), BF16),
        in_specs=[any_space] + [VMEM] * len(mine),
        out_specs=VMEM,
        compiler_params=params(16),
        name="finish",
    )(combine, *mine)
    other = swap_pair(slot_in)
    first = pl.pallas_call(
        first_product_kernel,
        out_shape=jax.ShapeDtypeStruct((experts, rows, units), F32),
        in_specs=[SMEM, VMEM, VMEM],
        out_specs=VMEM,
        cost_estimate=cost(2 * rows * units * half * experts, 2 * experts * units * half),
        compiler_params=params(8),
        name="first_product",
    )(place, slot_in, expert_in)
    hidden, send = pl.pallas_call(
        expert_kernel,
        out_shape=(
            jax.ShapeDtypeStruct((experts, rows, units), BF16),
            jax.ShapeDtypeStruct((rows, half), BF16),
        ),
        in_specs=[SMEM, VMEM, VMEM, VMEM, VMEM],
        out_specs=(VMEM, VMEM),
        compiler_params=params(8),
        name="experts",
    )(place, other, first, expert_in, expert_out)
    received = swap_pair(send)
    keep = pl.pallas_call(
        own_kernel,
        out_shape=jax.ShapeDtypeStruct((rows, half), F32),
        in_specs=[SMEM, VMEM, VMEM, any_space],
        out_specs=VMEM,
        cost_estimate=cost(2 * rows * units * half * experts, 2 * experts * units * half),
        compiler_params=params(8),
        name="own",
    )(place, hidden, expert_out, send)
    partial = (keep + received.astype(F32)).astype(BF16)
    own = partial.astype(F32)
    for r in range(1, rest):
        own = own + move(partial, plane, (0, r)).astype(F32)
    their = jnp.zeros_like(own)
    for r in range(rest):
        their = their + move(partial, plane, (1, r)).astype(F32)
    block = jnp.concatenate([own, their], axis=0).astype(BF16)
    slot_out = jnp.concatenate([block] + [move(block, ("far",), (r,)) for r in range(1, far)], axis=0)
    other = swap_pair(slot_out)
    done, blocks = count // 2, 8
    mixed, left = pl.pallas_call(
        mix_kernel,
        out_shape=(
            pltpu.HBM((count, model), BF16),
            jax.ShapeDtypeStruct((count - done, half), BF16),
        ),
        in_specs=[SMEM, VMEM, VMEM],
        out_specs=(HBM, VMEM),
        scratch_shapes=[pltpu.VMEM((done, half), BF16), pltpu.SemaphoreType.DMA((blocks // 2,))],
        cost_estimate=cost(2 * count * slots * half, 2 * count * (half + slots)),
        compiler_params=params(16),
        name="mix",
    )(place, combine, slot_out)
    return pl.pallas_call(
        mix_other_kernel,
        out_shape=jax.ShapeDtypeStruct((count, model), BF16),
        in_specs=[SMEM, VMEM, VMEM, VMEM, HBM],
        out_specs=HBM,
        scratch_shapes=[pltpu.VMEM((count, half), BF16), pltpu.SemaphoreType.DMA((blocks + 1,))],
        input_output_aliases={4: 0},
        cost_estimate=cost(2 * count * slots * half, 2 * count * (half + slots)),
        compiler_params=params(16),
        name="mix_other",
    )(place, combine, other, left, mixed)


def solution(mesh):
    wide, narrow = mesh.shape["wide"], mesh.shape["narrow"]
    cut = Mesh(mesh.devices.reshape(wide // 2, 2, narrow // 2, 2), ("far", "near", "rest", "pair"))
    wide_axes, narrow_axes = ("far", "near"), ("rest", "pair")
    return jax.shard_map(
        shards,
        mesh=cut,
        in_specs=(
            P(wide_axes + narrow_axes, None),
            P(),
            P(wide_axes, None, narrow_axes),
            P(wide_axes, narrow_axes, None),
        ),
        out_specs=P(wide_axes + narrow_axes, None),
        check_vma=False,
    )
```

```python
import math

import jax
import jax.numpy as jnp
from jax import lax
from jax.experimental import pallas as pl
from jax.experimental.pallas import tpu as pltpu
from jax.sharding import Mesh, PartitionSpec as P

SLOT_PER = 4
SIDE = 128
CHUNK, TOGETHER = 256, 2
F32 = jnp.float32
BF16 = jnp.bfloat16
VMEM = pl.BlockSpec(memory_space=pltpu.VMEM)
SMEM = pl.BlockSpec(memory_space=pltpu.SMEM)
HBM = pl.BlockSpec(memory_space=pltpu.HBM)
MIB = 1024 * 1024


def params(mib):
    return pltpu.CompilerParams(vmem_limit_bytes=mib * MIB)


def cost(flops, moved, transcendentals=0):
    return pl.CostEstimate(flops=flops, bytes_accessed=moved, transcendentals=transcendentals)


def in_hbm(value):
    return pltpu.with_memory_space_constraint(value, pltpu.HBM)


def dot(lhs, rhs):
    return jnp.dot(lhs, rhs, preferred_element_type=F32)


def side_state(*columns):
    lane = lax.broadcasted_iota(jnp.int32, (columns[0].shape[0], SIDE), 1)
    out = jnp.zeros((columns[0].shape[0], SIDE), F32)
    for index, value in enumerate(columns):
        out = jnp.where(lane == index, value, out)
    return out


def side_message(peak, total):
    lane = lax.broadcasted_iota(jnp.int32, (peak.shape[0], SIDE), 1)
    out = jnp.zeros((peak.shape[0], SIDE), F32)
    for index, value in enumerate((peak, total)):
        for piece in range(3):
            part = value.astype(BF16).astype(F32)
            out = jnp.where(lane == 3 * index + piece, part, out)
            value = value - part
    return out.astype(BF16)


def read_message(side):
    value = side.astype(F32)
    return (
        value[:, 0:1] + value[:, 1:2] + value[:, 2:3],
        value[:, 3:4] + value[:, 4:5] + value[:, 5:6],
    )


def column_half(side, half):
    return pl.ds(pl.multiple_of(side * half, half), half)


def gather_kernel(place, tokens, slot_params, logits, turned, held, side, send, table, sems):
    chunks = tokens.shape[0] // CHUNK
    slots = slot_params.shape[1]
    half = held.shape[1] // 2
    spans = [pl.ds(i * CHUNK, CHUNK) for i in range(chunks)]
    table_copy = pltpu.make_async_copy(slot_params, table, sems.at[chunks])
    table_copy.start()
    copies = [pltpu.make_async_copy(tokens.at[span], held.at[span], sems.at[i]) for i, span in enumerate(spans)]
    for copy in copies:
        copy.start()

    def find_peak(parts, high=None):
        for part in parts:
            top = jnp.max(part.reshape(CHUNK // 8, 8, slots), axis=0)
            high = top if high is None else jnp.maximum(high, top)
        return high

    def weigh(first, parts, peak):
        total = jnp.zeros((8, slots), F32)
        columns = []
        for part in parts:
            weights = jnp.exp(part - peak)
            total = total + jnp.sum(weights.reshape(CHUNK // 8, 8, slots), axis=0)
            columns.append(weights.astype(BF16).T)
        weights = jnp.concatenate(columns, axis=1)
        span = pl.ds(first * CHUNK, len(parts) * CHUNK)
        turned[:, span] = weights
        sums = dot(weights, held[span, column_half(1 - place[0], half)])
        return sums, jnp.sum(total, axis=0, keepdims=True)

    table_copy.wait()
    high = None
    for first in range(0, chunks, TOGETHER):
        for copy in copies[first : first + TOGETHER]:
            copy.wait()
        parts = [dot(held[span, :], table[...]) for span in spans[first : first + TOGETHER]]
        for part, span in zip(parts, spans[first:]):
            logits[span, :] = part
        if first + TOGETHER < chunks:
            high = find_peak(parts, high)
    early_peak = jnp.max(high, axis=0, keepdims=True)
    early, early_total = weigh(0, [logits[span, :] for span in spans[:first]], early_peak)
    late_peak = jnp.max(find_peak(parts), axis=0, keepdims=True)
    late, late_total = weigh(first, parts, late_peak)
    peak = jnp.maximum(early_peak, late_peak)
    early_scale, late_scale = jnp.exp(early_peak - peak), jnp.exp(late_peak - peak)
    total = early_total * early_scale + late_total * late_scale
    row = lax.broadcasted_iota(jnp.int32, (8, slots), 0)
    columns = jnp.zeros((8, slots), F32)
    for index, value in enumerate((peak, total, early_scale, late_scale)):
        columns = jnp.where(row == index, value, columns)
    columns = columns.T
    peak, total, early_scale, late_scale = [columns[:, i : i + 1] for i in range(4)]
    send[:, :half] = (early * early_scale + late * late_scale).astype(BF16)
    side[...] = side_state(peak, total, early_scale, late_scale)
    send[:, half:] = side_message(peak, total)


def own_sums_kernel(place, turned, held, side, after, keep):
    columns = column_half(place[0], keep.shape[1])
    early = held.shape[0] - TOGETHER * CHUNK
    spans = (pl.ds(0, early), pl.ds(early, TOGETHER * CHUNK))
    early, late = [dot(turned[:, span], held[span, columns]) for span in spans]
    keep[...] = early * side[:, 2:3] + late * side[:, 3:4]


def pair_kernel(far_at, keep, side, received, *sends):
    width = keep.shape[1]
    for r, send in enumerate(sends):
        rows = send.shape[0]
        span = pl.ds(pl.multiple_of((far_at[0] ^ r) * rows, rows), rows)
        peak_mine, total_mine = side[span, 0:1], side[span, 1:2]
        peak_other, total_other = read_message(received[span, width:])
        peak = jnp.maximum(peak_mine, peak_other)
        scale_mine, scale_other = jnp.exp(peak_mine - peak), jnp.exp(peak_other - peak)
        total = total_mine * scale_mine + total_other * scale_other
        sums = keep[span, :] * scale_mine + received[span, :width].astype(F32) * scale_other
        send[:, :width] = sums.astype(BF16)
        send[:, width:] = side_message(peak, total)


def add_parts(parts, width):
    states = [read_message(part[:, width:]) for part in parts]
    peak = states[0][0]
    for other, _ in states[1:]:
        peak = jnp.maximum(peak, other)
    total = jnp.zeros_like(peak)
    sums = jnp.zeros((parts[0].shape[0], width), F32)
    for part, (peak_other, total_other) in zip(parts, states):
        scale = jnp.exp(peak_other - peak)
        total = total + total_other * scale
        sums = sums + part[:, :width].astype(F32) * scale
    return sums, peak, total


def merge_kernel(near_at, *refs):
    for n, send in enumerate(refs[-2:]):
        rows, width = send.shape[0], send.shape[1] - SIDE
        span = pl.ds(pl.multiple_of((near_at[0] ^ n) * rows, rows), rows)
        sums, peak, total = add_parts([ref[span, :] for ref in refs[:-2]], width)
        send[:, :width] = sums.astype(BF16)
        send[:, width:] = side_message(peak, total)


def finish_kernel(combine, *refs):
    slot_in = refs[-1]
    sums, _, total = add_parts([ref[...] for ref in refs[:-1]], slot_in.shape[1])
    slot_in[...] = (sums / total).astype(BF16)


def first_product_kernel(place, slot_in, expert_in, result):
    half = slot_in.shape[1]
    for e in range(expert_in.shape[0]):
        result[e] = dot(slot_in[...], expert_in[e, column_half(place[0], half), :])


def second_product(hidden, weights, columns):
    row = lax.broadcasted_iota(jnp.int32, (hidden[0].shape[0], 1), 0)
    result = 0.0
    for e, value in enumerate(hidden):
        result = jnp.where(row // SLOT_PER == e, dot(value, weights[e, :, columns]), result)
    return result


def expert_kernel(place, slot_in, first, expert_in, expert_out, hidden, send):
    half = slot_in.shape[1]
    values = []
    for e in range(expert_in.shape[0]):
        product = first[e] + dot(slot_in[...], expert_in[e, column_half(1 - place[0], half), :])
        values.append(jax.nn.gelu(product).astype(BF16))
        hidden[e] = values[e]
    send[...] = second_product(values, expert_out, column_half(1 - place[0], half)).astype(BF16)


def own_kernel(place, hidden, expert_out, after, keep):
    values = [hidden[e] for e in range(hidden.shape[0])]
    keep[...] = second_product(values, expert_out, column_half(place[0], keep.shape[1]))


def combine_kernel(logits, after, combine):
    value = logits[...]
    weights = jnp.exp(value - jnp.max(value, axis=1, keepdims=True))
    combine[...] = (weights / jnp.sum(weights, axis=1, keepdims=True)).astype(BF16)


def mix_kernel(place, combine, slot_out, mixed, rest, held, sems):
    width = slot_out.shape[1]
    tokens, done = combine.shape[0], held.shape[0]
    block = done // sems.shape[0]
    columns = pl.ds(pl.multiple_of(place[0] * width, width), width)
    copies = []
    for i in range(tokens // block):
        rows = pl.ds(i * block, block)
        value = dot(combine[rows, :], slot_out[...]).astype(BF16)
        if i < sems.shape[0]:
            held[rows, :] = value
            copies.append(pltpu.make_async_copy(held.at[rows], mixed.at[rows, columns], sems.at[i]))
            copies[-1].start()
        else:
            rest[pl.ds(i * block - done, block), :] = value
    for copy in copies:
        copy.wait()


def mix_other_kernel(place, combine, slot_out, rest, before, mixed, held, sems):
    width = slot_out.shape[1]
    blocks = sems.shape[0] - 1
    tokens = combine.shape[0]
    done = tokens - rest.shape[0]
    mine = pl.ds(pl.multiple_of(place[0] * width, width), width)
    other = pl.ds(pl.multiple_of((1 - place[0]) * width, width), width)
    copies = [pltpu.make_async_copy(rest, mixed.at[pl.ds(done, tokens - done), mine], sems.at[blocks])]
    copies[0].start()
    block = tokens // blocks
    for i in range(blocks):
        rows = pl.ds(i * block, block)
        held[rows, :] = dot(combine[rows, :], slot_out[...]).astype(BF16)
        copies.append(pltpu.make_async_copy(held.at[rows], mixed.at[rows, other], sems.at[i]))
        copies[-1].start()
    for copy in copies:
        copy.wait()


def move(value, axes, offsets):
    sizes = [lax.axis_size(axis) for axis in axes]
    moves = []
    for index in range(math.prod(sizes)):
        source, target, stride = index, 0, 1
        for size, offset in zip(reversed(sizes), reversed(offsets)):
            target += (source % size ^ offset) * stride
            source //= size
            stride *= size
        moves.append((index, target))
    return lax.ppermute(value, axes, moves)


def swap_pair(value):
    return move(value, ("pair",), (1,))


def shards(tokens, slot_params, expert_in, expert_out):
    count, model = tokens.shape
    slots = slot_params.shape[1]
    far, near, rest = [lax.axis_size(axis) for axis in ("far", "near", "rest")]
    rows = slots // (far * near)
    half = model // 2
    place, far_at, near_at = [
        lax.axis_index(axis).astype(jnp.int32).reshape(1) for axis in ("pair", "far", "near")
    ]
    any_space = pl.BlockSpec(memory_space=pl.ANY)

    logits, turned, held, side, send = pl.pallas_call(
        gather_kernel,
        out_shape=(
            jax.ShapeDtypeStruct((count, slots), F32),
            jax.ShapeDtypeStruct((slots, count), BF16),
            jax.ShapeDtypeStruct((count, model), BF16),
            jax.ShapeDtypeStruct((slots, SIDE), F32),
            jax.ShapeDtypeStruct((slots, half + SIDE), BF16),
        ),
        in_specs=[SMEM, HBM, HBM],
        out_specs=(VMEM,) * 5,
        scratch_shapes=[pltpu.VMEM((model, slots), BF16), pltpu.SemaphoreType.DMA((count // CHUNK + 1,))],
        compiler_params=params(24),
        name="gather",
    )(place, in_hbm(tokens), in_hbm(slot_params))
    received = swap_pair(send)
    keep = pl.pallas_call(
        own_sums_kernel,
        out_shape=jax.ShapeDtypeStruct((slots, half), F32),
        in_specs=[SMEM, VMEM, VMEM, VMEM, any_space],
        out_specs=VMEM,
        cost_estimate=cost(2 * slots * count * half, 2 * count * (half + slots)),
        compiler_params=params(16),
        name="own_sums",
    )(place, turned, held, side, send)
    sends = pl.pallas_call(
        pair_kernel,
        out_shape=(jax.ShapeDtypeStruct((near * rows, half + SIDE), BF16),) * far,
        in_specs=[SMEM] + [VMEM] * 3,
        out_specs=(VMEM,) * far,
        cost_estimate=cost(0, 6 * slots * model, 128 * slots * model),
        compiler_params=params(16),
        name="pair",
    )(far_at, keep, side, received)
    parts = [sends[0]] + [move(sends[r], ("far",), (r,)) for r in range(1, far)]
    send, their = pl.pallas_call(
        merge_kernel,
        out_shape=(jax.ShapeDtypeStruct((rows, half + SIDE), BF16),) * 2,
        in_specs=[SMEM] + [VMEM] * far,
        out_specs=(VMEM, VMEM),
        compiler_params=params(16),
        name="merge",
    )(near_at, *parts)
    plane = ("near", "rest")
    mine = [send] + [move(send, plane, (0, r)) for r in range(1, rest)]
    mine += [move(their, plane, (1, r)) for r in range(rest)]
    combine = pl.pallas_call(
        combine_kernel,
        out_shape=jax.ShapeDtypeStruct((count, slots), BF16),
        in_specs=[VMEM, any_space],
        out_specs=VMEM,
        cost_estimate=cost(8 * count * slots, 6 * count * slots, count * slots),
        compiler_params=params(16),
        name="combine",
    )(logits, send)
    experts, units = expert_out.shape[:2]
    slot_in = pl.pallas_call(
        finish_kernel,
        out_shape=jax.ShapeDtypeStruct((rows, half), BF16),
        in_specs=[any_space] + [VMEM] * len(mine),
        out_specs=VMEM,
        compiler_params=params(16),
        name="finish",
    )(combine, *mine)
    other = swap_pair(slot_in)
    first = pl.pallas_call(
        first_product_kernel,
        out_shape=jax.ShapeDtypeStruct((experts, rows, units), F32),
        in_specs=[SMEM, VMEM, VMEM],
        out_specs=VMEM,
        cost_estimate=cost(2 * rows * units * half * experts, 2 * experts * units * half),
        compiler_params=params(8),
        name="first_product",
    )(place, slot_in, expert_in)
    hidden, send = pl.pallas_call(
        expert_kernel,
        out_shape=(
            jax.ShapeDtypeStruct((experts, rows, units), BF16),
            jax.ShapeDtypeStruct((rows, half), BF16),
        ),
        in_specs=[SMEM, VMEM, VMEM, VMEM, VMEM],
        out_specs=(VMEM, VMEM),
        compiler_params=params(8),
        name="experts",
    )(place, other, first, expert_in, expert_out)
    received = swap_pair(send)
    keep = pl.pallas_call(
        own_kernel,
        out_shape=jax.ShapeDtypeStruct((rows, half), F32),
        in_specs=[SMEM, VMEM, VMEM, any_space],
        out_specs=VMEM,
        cost_estimate=cost(2 * rows * units * half * experts, 2 * experts * units * half),
        compiler_params=params(8),
        name="own",
    )(place, hidden, expert_out, send)
    partial = (keep + received.astype(F32)).astype(BF16)
    groups = far * near
    partials = jnp.broadcast_to(partial, (groups * rest, rows, half))
    partials = lax.all_to_all(partials, ("rest", "far", "near"), split_axis=0, concat_axis=0, tiled=True)
    slot_out = jnp.sum(partials.reshape(rest, groups, rows, half).astype(F32), axis=0)
    slot_out = slot_out.astype(BF16).reshape(slots, half)
    other = swap_pair(slot_out)
    done, blocks = count // 2, 8
    mixed, left = pl.pallas_call(
        mix_kernel,
        out_shape=(
            pltpu.HBM((count, model), BF16),
            jax.ShapeDtypeStruct((count - done, half), BF16),
        ),
        in_specs=[SMEM, VMEM, VMEM],
        out_specs=(HBM, VMEM),
        scratch_shapes=[pltpu.VMEM((done, half), BF16), pltpu.SemaphoreType.DMA((blocks // 2,))],
        cost_estimate=cost(2 * count * slots * half, 2 * count * (half + slots)),
        compiler_params=params(16),
        name="mix",
    )(place, combine, slot_out)
    return pl.pallas_call(
        mix_other_kernel,
        out_shape=jax.ShapeDtypeStruct((count, model), BF16),
        in_specs=[SMEM, VMEM, VMEM, VMEM, HBM],
        out_specs=HBM,
        scratch_shapes=[pltpu.VMEM((count, half), BF16), pltpu.SemaphoreType.DMA((blocks + 1,))],
        input_output_aliases={4: 0},
        cost_estimate=cost(2 * count * slots * half, 2 * count * (half + slots)),
        compiler_params=params(16),
        name="mix_other",
    )(place, combine, other, left, mixed)


def solution(mesh):
    wide, narrow = mesh.shape["wide"], mesh.shape["narrow"]
    cut = Mesh(mesh.devices.reshape(wide // 2, 2, narrow // 2, 2), ("far", "near", "rest", "pair"))
    wide_axes, narrow_axes = ("far", "near"), ("rest", "pair")
    return jax.shard_map(
        shards,
        mesh=cut,
        in_specs=(
            P(wide_axes + narrow_axes, None),
            P(),
            P(wide_axes, None, narrow_axes),
            P(wide_axes, narrow_axes, None),
        ),
        out_specs=P(wide_axes + narrow_axes, None),
        check_vma=False,
    )
```

```python
import functools
import math

import jax
import jax.numpy as jnp
from jax import lax
from jax.experimental import pallas as pl
from jax.experimental.pallas import tpu as pltpu
from jax.sharding import Mesh, PartitionSpec as P

SLOT_PER = 4
SIDE = 128
CHUNK, TOGETHER = 256, 2
F32 = jnp.float32
BF16 = jnp.bfloat16
VMEM = pl.BlockSpec(memory_space=pltpu.VMEM)
SMEM = pl.BlockSpec(memory_space=pltpu.SMEM)
HBM = pl.BlockSpec(memory_space=pltpu.HBM)
MIB = 1024 * 1024


def params(mib):
    return pltpu.CompilerParams(vmem_limit_bytes=mib * MIB)


def cost(flops, moved, transcendentals=0):
    return pl.CostEstimate(flops=flops, bytes_accessed=moved, transcendentals=transcendentals)


def in_hbm(value):
    return pltpu.with_memory_space_constraint(value, pltpu.HBM)


def dot(lhs, rhs):
    return jnp.dot(lhs, rhs, preferred_element_type=F32)


def side_state(*columns):
    lane = lax.broadcasted_iota(jnp.int32, (columns[0].shape[0], SIDE), 1)
    out = jnp.zeros((columns[0].shape[0], SIDE), F32)
    for index, value in enumerate(columns):
        out = jnp.where(lane == index, value, out)
    return out


def side_message(peak, total):
    lane = lax.broadcasted_iota(jnp.int32, (peak.shape[0], SIDE), 1)
    out = jnp.zeros((peak.shape[0], SIDE), F32)
    for index, value in enumerate((peak, total)):
        for piece in range(3):
            part = value.astype(BF16).astype(F32)
            out = jnp.where(lane == 3 * index + piece, part, out)
            value = value - part
    return out.astype(BF16)


def read_message(side):
    value = side.astype(F32)
    return (
        value[:, 0:1] + value[:, 1:2] + value[:, 2:3],
        value[:, 3:4] + value[:, 4:5] + value[:, 5:6],
    )


def column_half(side, half):
    return pl.ds(pl.multiple_of(side * half, half), half)


def gather_kernel(place, tokens, slot_params, logits, turned, held, side, send, table, sems):
    chunks = tokens.shape[0] // CHUNK
    slots = slot_params.shape[1]
    half = held.shape[1] // 2
    spans = [pl.ds(i * CHUNK, CHUNK) for i in range(chunks)]
    table_copy = pltpu.make_async_copy(slot_params, table, sems.at[chunks])
    table_copy.start()
    copies = [pltpu.make_async_copy(tokens.at[span], held.at[span], sems.at[i]) for i, span in enumerate(spans)]
    for copy in copies:
        copy.start()

    def find_peak(parts, high=None):
        for part in parts:
            top = jnp.max(part.reshape(CHUNK // 8, 8, slots), axis=0)
            high = top if high is None else jnp.maximum(high, top)
        return high

    def weigh(first, parts, peak):
        total = jnp.zeros((8, slots), F32)
        columns = []
        for part in parts:
            weights = jnp.exp(part - peak)
            total = total + jnp.sum(weights.reshape(CHUNK // 8, 8, slots), axis=0)
            columns.append(weights.astype(BF16).T)
        weights = jnp.concatenate(columns, axis=1)
        span = pl.ds(first * CHUNK, len(parts) * CHUNK)
        turned[:, span] = weights
        sums = dot(weights, held[span, column_half(1 - place[0], half)])
        return sums, jnp.sum(total, axis=0, keepdims=True)

    table_copy.wait()
    high = None
    for first in range(0, chunks, TOGETHER):
        for copy in copies[first : first + TOGETHER]:
            copy.wait()
        parts = [dot(held[span, :], table[...]) for span in spans[first : first + TOGETHER]]
        for part, span in zip(parts, spans[first:]):
            logits[span, :] = part
        if first + TOGETHER < chunks:
            high = find_peak(parts, high)
    early_peak = jnp.max(high, axis=0, keepdims=True)
    early, early_total = weigh(0, [logits[span, :] for span in spans[:first]], early_peak)
    late_peak = jnp.max(find_peak(parts), axis=0, keepdims=True)
    late, late_total = weigh(first, parts, late_peak)
    peak = jnp.maximum(early_peak, late_peak)
    early_scale, late_scale = jnp.exp(early_peak - peak), jnp.exp(late_peak - peak)
    total = early_total * early_scale + late_total * late_scale
    row = lax.broadcasted_iota(jnp.int32, (8, slots), 0)
    columns = jnp.zeros((8, slots), F32)
    for index, value in enumerate((peak, total, early_scale, late_scale)):
        columns = jnp.where(row == index, value, columns)
    columns = columns.T
    peak, total, early_scale, late_scale = [columns[:, i : i + 1] for i in range(4)]
    send[:, :half] = (early * early_scale + late * late_scale).astype(BF16)
    side[...] = side_state(peak, total, early_scale, late_scale)
    send[:, half:] = side_message(peak, total)


def own_sums_kernel(place, turned, held, side, after, keep):
    columns = column_half(place[0], keep.shape[1])
    early = held.shape[0] - TOGETHER * CHUNK
    spans = (pl.ds(0, early), pl.ds(early, TOGETHER * CHUNK))
    early, late = [dot(turned[:, span], held[span, columns]) for span in spans]
    keep[...] = early * side[:, 2:3] + late * side[:, 3:4]


def pair_kernel(far_at, keep, side, received, *sends):
    width = keep.shape[1]
    for r, send in enumerate(sends):
        rows = send.shape[0]
        span = pl.ds(pl.multiple_of((far_at[0] ^ r) * rows, rows), rows)
        peak_mine, total_mine = side[span, 0:1], side[span, 1:2]
        peak_other, total_other = read_message(received[span, width:])
        peak = jnp.maximum(peak_mine, peak_other)
        scale_mine, scale_other = jnp.exp(peak_mine - peak), jnp.exp(peak_other - peak)
        total = total_mine * scale_mine + total_other * scale_other
        sums = keep[span, :] * scale_mine + received[span, :width].astype(F32) * scale_other
        send[:, :width] = sums.astype(BF16)
        send[:, width:] = side_message(peak, total)


def add_parts(parts, width):
    states = [read_message(part[:, width:]) for part in parts]
    peak = states[0][0]
    for other, _ in states[1:]:
        peak = jnp.maximum(peak, other)
    total = jnp.zeros_like(peak)
    sums = jnp.zeros((parts[0].shape[0], width), F32)
    for part, (peak_other, total_other) in zip(parts, states):
        scale = jnp.exp(peak_other - peak)
        total = total + total_other * scale
        sums = sums + part[:, :width].astype(F32) * scale
    return sums, peak, total


def merge_kernel(near_at, *refs):
    for n, send in enumerate(refs[-2:]):
        rows, width = send.shape[0], send.shape[1] - SIDE
        span = pl.ds(pl.multiple_of((near_at[0] ^ n) * rows, rows), rows)
        sums, peak, total = add_parts([ref[span, :] for ref in refs[:-2]], width)
        send[:, :width] = sums.astype(BF16)
        send[:, width:] = side_message(peak, total)


def finish_kernel(combine, *refs):
    slot_in = refs[-1]
    sums, _, total = add_parts([ref[...] for ref in refs[:-1]], slot_in.shape[1])
    slot_in[...] = (sums / total).astype(BF16)


def first_product_kernel(place, slot_in, expert_in, result):
    half = slot_in.shape[1]
    for e in range(expert_in.shape[0]):
        result[e] = dot(slot_in[...], expert_in[e, column_half(place[0], half), :])


def second_product(hidden, weights, columns):
    row = lax.broadcasted_iota(jnp.int32, (hidden[0].shape[0], 1), 0)
    result = 0.0
    for e, value in enumerate(hidden):
        result = jnp.where(row // SLOT_PER == e, dot(value, weights[e, :, columns]), result)
    return result


def expert_kernel(place, slot_in, first, expert_in, expert_out, hidden, send):
    half = slot_in.shape[1]
    values = []
    for e in range(expert_in.shape[0]):
        product = first[e] + dot(slot_in[...], expert_in[e, column_half(1 - place[0], half), :])
        values.append(jax.nn.gelu(product).astype(BF16))
        hidden[e] = values[e]
    send[...] = second_product(values, expert_out, column_half(1 - place[0], half)).astype(BF16)


def own_kernel(place, hidden, expert_out, after, keep):
    values = [hidden[e] for e in range(hidden.shape[0])]
    keep[...] = second_product(values, expert_out, column_half(place[0], keep.shape[1]))


def combine_kernel(rows, far_at, near_at, logits, after, combine):
    value = logits[...]
    slots = value.shape[1]
    weights = jnp.exp(value - jnp.max(value, axis=1, keepdims=True))
    weights = (weights / jnp.sum(weights, axis=1, keepdims=True)).astype(BF16)
    row = lax.broadcasted_iota(jnp.int32, (slots, slots), 0)
    column = lax.broadcasted_iota(jnp.int32, (slots, slots), 1)
    swap = jnp.where(row == (column ^ ((far_at[0] * 2 + near_at[0]) * rows)), 1.0, 0.0).astype(BF16)
    combine[...] = dot(weights, swap).astype(BF16)


def mix_kernel(place, combine, slot_out, mixed, rest, held, sems):
    width = slot_out.shape[1]
    tokens, done = combine.shape[0], held.shape[0]
    block = done // sems.shape[0]
    columns = pl.ds(pl.multiple_of(place[0] * width, width), width)
    copies = []
    for i in range(tokens // block):
        rows = pl.ds(i * block, block)
        value = dot(combine[rows, :], slot_out[...]).astype(BF16)
        if i < sems.shape[0]:
            held[rows, :] = value
            copies.append(pltpu.make_async_copy(held.at[rows], mixed.at[rows, columns], sems.at[i]))
            copies[-1].start()
        else:
            rest[pl.ds(i * block - done, block), :] = value
    for copy in copies:
        copy.wait()


def mix_other_kernel(place, combine, slot_out, rest, before, mixed, held, sems):
    width = slot_out.shape[1]
    blocks = sems.shape[0] - 1
    tokens = combine.shape[0]
    done = tokens - rest.shape[0]
    mine = pl.ds(pl.multiple_of(place[0] * width, width), width)
    other = pl.ds(pl.multiple_of((1 - place[0]) * width, width), width)
    copies = [pltpu.make_async_copy(rest, mixed.at[pl.ds(done, tokens - done), mine], sems.at[blocks])]
    copies[0].start()
    block = tokens // blocks
    for i in range(blocks):
        rows = pl.ds(i * block, block)
        held[rows, :] = dot(combine[rows, :], slot_out[...]).astype(BF16)
        copies.append(pltpu.make_async_copy(held.at[rows], mixed.at[rows, other], sems.at[i]))
        copies[-1].start()
    for copy in copies:
        copy.wait()


def move(value, axes, offsets):
    sizes = [lax.axis_size(axis) for axis in axes]
    moves = []
    for index in range(math.prod(sizes)):
        source, target, stride = index, 0, 1
        for size, offset in zip(reversed(sizes), reversed(offsets)):
            target += (source % size ^ offset) * stride
            source //= size
            stride *= size
        moves.append((index, target))
    return lax.ppermute(value, axes, moves)


def swap_pair(value):
    return move(value, ("pair",), (1,))


def shards(tokens, slot_params, expert_in, expert_out):
    count, model = tokens.shape
    slots = slot_params.shape[1]
    far, near, rest = [lax.axis_size(axis) for axis in ("far", "near", "rest")]
    rows = slots // (far * near)
    half = model // 2
    place, far_at, near_at = [
        lax.axis_index(axis).astype(jnp.int32).reshape(1) for axis in ("pair", "far", "near")
    ]
    any_space = pl.BlockSpec(memory_space=pl.ANY)

    logits, turned, held, side, send = pl.pallas_call(
        gather_kernel,
        out_shape=(
            jax.ShapeDtypeStruct((count, slots), F32),
            jax.ShapeDtypeStruct((slots, count), BF16),
            jax.ShapeDtypeStruct((count, model), BF16),
            jax.ShapeDtypeStruct((slots, SIDE), F32),
            jax.ShapeDtypeStruct((slots, half + SIDE), BF16),
        ),
        in_specs=[SMEM, HBM, HBM],
        out_specs=(VMEM,) * 5,
        scratch_shapes=[pltpu.VMEM((model, slots), BF16), pltpu.SemaphoreType.DMA((count // CHUNK + 1,))],
        compiler_params=params(24),
        name="gather",
    )(place, in_hbm(tokens), in_hbm(slot_params))
    received = swap_pair(send)
    keep = pl.pallas_call(
        own_sums_kernel,
        out_shape=jax.ShapeDtypeStruct((slots, half), F32),
        in_specs=[SMEM, VMEM, VMEM, VMEM, any_space],
        out_specs=VMEM,
        cost_estimate=cost(2 * slots * count * half, 2 * count * (half + slots)),
        compiler_params=params(16),
        name="own_sums",
    )(place, turned, held, side, send)
    sends = pl.pallas_call(
        pair_kernel,
        out_shape=(jax.ShapeDtypeStruct((near * rows, half + SIDE), BF16),) * far,
        in_specs=[SMEM] + [VMEM] * 3,
        out_specs=(VMEM,) * far,
        cost_estimate=cost(0, 6 * slots * model, 128 * slots * model),
        compiler_params=params(16),
        name="pair",
    )(far_at, keep, side, received)
    parts = [sends[0]] + [move(sends[r], ("far",), (r,)) for r in range(1, far)]
    send, their = pl.pallas_call(
        merge_kernel,
        out_shape=(jax.ShapeDtypeStruct((rows, half + SIDE), BF16),) * 2,
        in_specs=[SMEM] + [VMEM] * far,
        out_specs=(VMEM, VMEM),
        compiler_params=params(16),
        name="merge",
    )(near_at, *parts)
    plane = ("near", "rest")
    mine = [send] + [move(send, plane, (0, r)) for r in range(1, rest)]
    mine += [move(their, plane, (1, r)) for r in range(rest)]
    combine = pl.pallas_call(
        functools.partial(combine_kernel, rows),
        out_shape=jax.ShapeDtypeStruct((count, slots), BF16),
        in_specs=[SMEM, SMEM, VMEM, any_space],
        out_specs=VMEM,
        cost_estimate=cost(8 * count * slots, 6 * count * slots, count * slots),
        compiler_params=params(16),
        name="combine",
    )(far_at, near_at, logits, send)
    experts, units = expert_out.shape[:2]
    slot_in = pl.pallas_call(
        finish_kernel,
        out_shape=jax.ShapeDtypeStruct((rows, half), BF16),
        in_specs=[any_space] + [VMEM] * len(mine),
        out_specs=VMEM,
        compiler_params=params(16),
        name="finish",
    )(combine, *mine)
    other = swap_pair(slot_in)
    first = pl.pallas_call(
        first_product_kernel,
        out_shape=jax.ShapeDtypeStruct((experts, rows, units), F32),
        in_specs=[SMEM, VMEM, VMEM],
        out_specs=VMEM,
        cost_estimate=cost(2 * rows * units * half * experts, 2 * experts * units * half),
        compiler_params=params(8),
        name="first_product",
    )(place, slot_in, expert_in)
    hidden, send = pl.pallas_call(
        expert_kernel,
        out_shape=(
            jax.ShapeDtypeStruct((experts, rows, units), BF16),
            jax.ShapeDtypeStruct((rows, half), BF16),
        ),
        in_specs=[SMEM, VMEM, VMEM, VMEM, VMEM],
        out_specs=(VMEM, VMEM),
        compiler_params=params(8),
        name="experts",
    )(place, other, first, expert_in, expert_out)
    received = swap_pair(send)
    keep = pl.pallas_call(
        own_kernel,
        out_shape=jax.ShapeDtypeStruct((rows, half), F32),
        in_specs=[SMEM, VMEM, VMEM, any_space],
        out_specs=VMEM,
        cost_estimate=cost(2 * rows * units * half * experts, 2 * experts * units * half),
        compiler_params=params(8),
        name="own",
    )(place, hidden, expert_out, send)
    partial = (keep + received.astype(F32)).astype(BF16)
    own = partial.astype(F32)
    for r in range(1, rest):
        own = own + move(partial, plane, (0, r)).astype(F32)
    their = jnp.zeros_like(own)
    for r in range(rest):
        their = their + move(partial, plane, (1, r)).astype(F32)
    block = jnp.concatenate([own, their], axis=0).astype(BF16)
    slot_out = jnp.concatenate([block] + [move(block, ("far",), (r,)) for r in range(1, far)], axis=0)
    other = swap_pair(slot_out)
    done, blocks = count // 2, 8
    mixed, left = pl.pallas_call(
        mix_kernel,
        out_shape=(
            pltpu.HBM((count, model), BF16),
            jax.ShapeDtypeStruct((count - done, half), BF16),
        ),
        in_specs=[SMEM, VMEM, VMEM],
        out_specs=(HBM, VMEM),
        scratch_shapes=[pltpu.VMEM((done, half), BF16), pltpu.SemaphoreType.DMA((blocks // 2,))],
        cost_estimate=cost(2 * count * slots * half, 2 * count * (half + slots)),
        compiler_params=params(16),
        name="mix",
    )(place, combine, slot_out)
    return pl.pallas_call(
        mix_other_kernel,
        out_shape=jax.ShapeDtypeStruct((count, model), BF16),
        in_specs=[SMEM, VMEM, VMEM, VMEM, HBM],
        out_specs=HBM,
        scratch_shapes=[pltpu.VMEM((count, half), BF16), pltpu.SemaphoreType.DMA((blocks + 1,))],
        input_output_aliases={4: 0},
        cost_estimate=cost(2 * count * slots * half, 2 * count * (half + slots)),
        compiler_params=params(16),
        name="mix_other",
    )(place, combine, other, left, mixed)


def solution(mesh):
    wide, narrow = mesh.shape["wide"], mesh.shape["narrow"]
    cut = Mesh(mesh.devices.reshape(wide // 2, 2, narrow // 2, 2), ("far", "near", "rest", "pair"))
    wide_axes, narrow_axes = ("far", "near"), ("rest", "pair")
    return jax.shard_map(
        shards,
        mesh=cut,
        in_specs=(
            P(wide_axes + narrow_axes, None),
            P(),
            P(wide_axes, None, narrow_axes),
            P(wide_axes, narrow_axes, None),
        ),
        out_specs=P(wide_axes + narrow_axes, None),
        check_vma=False,
    )
```

```python
import functools
import math

import jax
import jax.numpy as jnp
from jax import lax
from jax.experimental import pallas as pl
from jax.experimental.pallas import tpu as pltpu
from jax.sharding import Mesh, PartitionSpec as P

SLOT_PER = 4
SIDE = 128
CHUNK, TOGETHER = 256, 2
F32 = jnp.float32
BF16 = jnp.bfloat16
VMEM = pl.BlockSpec(memory_space=pltpu.VMEM)
SMEM = pl.BlockSpec(memory_space=pltpu.SMEM)
HBM = pl.BlockSpec(memory_space=pltpu.HBM)
MIB = 1024 * 1024


def params(mib):
    return pltpu.CompilerParams(vmem_limit_bytes=mib * MIB)


def cost(flops, moved, transcendentals=0):
    return pl.CostEstimate(flops=flops, bytes_accessed=moved, transcendentals=transcendentals)


def in_hbm(value):
    return pltpu.with_memory_space_constraint(value, pltpu.HBM)


def dot(lhs, rhs):
    return jnp.dot(lhs, rhs, preferred_element_type=F32)


def side_state(*columns):
    lane = lax.broadcasted_iota(jnp.int32, (columns[0].shape[0], SIDE), 1)
    out = jnp.zeros((columns[0].shape[0], SIDE), F32)
    for index, value in enumerate(columns):
        out = jnp.where(lane == index, value, out)
    return out


def side_message(peak, total):
    lane = lax.broadcasted_iota(jnp.int32, (peak.shape[0], SIDE), 1)
    out = jnp.zeros((peak.shape[0], SIDE), F32)
    for index, value in enumerate((peak, total)):
        for piece in range(3):
            part = value.astype(BF16).astype(F32)
            out = jnp.where(lane == 3 * index + piece, part, out)
            value = value - part
    return out.astype(BF16)


def read_message(side):
    value = side.astype(F32)
    return (
        value[:, 0:1] + value[:, 1:2] + value[:, 2:3],
        value[:, 3:4] + value[:, 4:5] + value[:, 5:6],
    )


def pair_at(place):
    return place[0] & 1


def near_at(place, rest):
    return place[0] // (2 * rest) & 1


def far_at(place, rest):
    return place[0] // (4 * rest)


def column_half(side, half):
    return pl.ds(pl.multiple_of(side * half, half), half)


def gather_kernel(place, tokens, slot_params, logits, turned, held, side, send, table, sems):
    chunks = tokens.shape[0] // CHUNK
    slots = slot_params.shape[1]
    half = held.shape[1] // 2
    spans = [pl.ds(i * CHUNK, CHUNK) for i in range(chunks)]
    table_copy = pltpu.make_async_copy(slot_params, table, sems.at[chunks])
    table_copy.start()
    copies = [pltpu.make_async_copy(tokens.at[span], held.at[span], sems.at[i]) for i, span in enumerate(spans)]
    for copy in copies:
        copy.start()

    def find_peak(parts, high=None):
        for part in parts:
            top = jnp.max(part.reshape(CHUNK // 8, 8, slots), axis=0)
            high = top if high is None else jnp.maximum(high, top)
        return high

    def weigh(first, parts, peak):
        total = jnp.zeros((8, slots), F32)
        columns = []
        for part in parts:
            weights = jnp.exp(part - peak)
            total = total + jnp.sum(weights.reshape(CHUNK // 8, 8, slots), axis=0)
            columns.append(weights.astype(BF16).T)
        weights = jnp.concatenate(columns, axis=1)
        span = pl.ds(first * CHUNK, len(parts) * CHUNK)
        turned[:, span] = weights
        sums = dot(weights, held[span, column_half(1 - pair_at(place), half)])
        return sums, jnp.sum(total, axis=0, keepdims=True)

    table_copy.wait()
    high = None
    for first in range(0, chunks, TOGETHER):
        for copy in copies[first : first + TOGETHER]:
            copy.wait()
        parts = [dot(held[span, :], table[...]) for span in spans[first : first + TOGETHER]]
        for part, span in zip(parts, spans[first:]):
            logits[span, :] = part
        if first + TOGETHER < chunks:
            high = find_peak(parts, high)
    early_peak = jnp.max(high, axis=0, keepdims=True)
    early, early_total = weigh(0, [logits[span, :] for span in spans[:first]], early_peak)
    late_peak = jnp.max(find_peak(parts), axis=0, keepdims=True)
    late, late_total = weigh(first, parts, late_peak)
    peak = jnp.maximum(early_peak, late_peak)
    early_scale, late_scale = jnp.exp(early_peak - peak), jnp.exp(late_peak - peak)
    total = early_total * early_scale + late_total * late_scale
    row = lax.broadcasted_iota(jnp.int32, (8, slots), 0)
    columns = jnp.zeros((8, slots), F32)
    for index, value in enumerate((peak, total, early_scale, late_scale)):
        columns = jnp.where(row == index, value, columns)
    columns = columns.T
    peak, total, early_scale, late_scale = [columns[:, i : i + 1] for i in range(4)]
    send[:, :half] = (early * early_scale + late * late_scale).astype(BF16)
    side[...] = side_state(peak, total, early_scale, late_scale)
    send[:, half:] = side_message(peak, total)


def own_sums_kernel(place, turned, held, side, after, keep):
    columns = column_half(pair_at(place), keep.shape[1])
    early = held.shape[0] - TOGETHER * CHUNK
    spans = (pl.ds(0, early), pl.ds(early, TOGETHER * CHUNK))
    early, late = [dot(turned[:, span], held[span, columns]) for span in spans]
    keep[...] = early * side[:, 2:3] + late * side[:, 3:4]


def pair_kernel(rest, place, keep, side, received, *sends):
    width = keep.shape[1]
    for r, send in enumerate(sends):
        rows = send.shape[0]
        span = pl.ds(pl.multiple_of((far_at(place, rest) ^ r) * rows, rows), rows)
        peak_mine, total_mine = side[span, 0:1], side[span, 1:2]
        peak_other, total_other = read_message(received[span, width:])
        peak = jnp.maximum(peak_mine, peak_other)
        scale_mine, scale_other = jnp.exp(peak_mine - peak), jnp.exp(peak_other - peak)
        total = total_mine * scale_mine + total_other * scale_other
        sums = keep[span, :] * scale_mine + received[span, :width].astype(F32) * scale_other
        send[:, :width] = sums.astype(BF16)
        send[:, width:] = side_message(peak, total)


def add_parts(parts, width):
    states = [read_message(part[:, width:]) for part in parts]
    peak = states[0][0]
    for other, _ in states[1:]:
        peak = jnp.maximum(peak, other)
    total = jnp.zeros_like(peak)
    sums = jnp.zeros((parts[0].shape[0], width), F32)
    for part, (peak_other, total_other) in zip(parts, states):
        scale = jnp.exp(peak_other - peak)
        total = total + total_other * scale
        sums = sums + part[:, :width].astype(F32) * scale
    return sums, peak, total


def merge_kernel(rest, place, *refs):
    for n, send in enumerate(refs[-2:]):
        rows, width = send.shape[0], send.shape[1] - SIDE
        span = pl.ds(pl.multiple_of((near_at(place, rest) ^ n) * rows, rows), rows)
        sums, peak, total = add_parts([ref[span, :] for ref in refs[:-2]], width)
        send[:, :width] = sums.astype(BF16)
        send[:, width:] = side_message(peak, total)


def finish_kernel(combine, *refs):
    slot_in = refs[-1]
    sums, _, total = add_parts([ref[...] for ref in refs[:-1]], slot_in.shape[1])
    slot_in[...] = (sums / total).astype(BF16)


def first_product_kernel(place, slot_in, expert_in, result):
    half = slot_in.shape[1]
    for e in range(expert_in.shape[0]):
        result[e] = dot(slot_in[...], expert_in[e, column_half(pair_at(place), half), :])


def second_product(hidden, weights, columns):
    row = lax.broadcasted_iota(jnp.int32, (hidden[0].shape[0], 1), 0)
    result = 0.0
    for e, value in enumerate(hidden):
        result = jnp.where(row // SLOT_PER == e, dot(value, weights[e, :, columns]), result)
    return result


def expert_kernel(place, slot_in, first, expert_in, expert_out, hidden, send):
    half = slot_in.shape[1]
    values = []
    for e in range(expert_in.shape[0]):
        product = first[e] + dot(slot_in[...], expert_in[e, column_half(1 - pair_at(place), half), :])
        values.append(jax.nn.gelu(product).astype(BF16))
        hidden[e] = values[e]
    send[...] = second_product(values, expert_out, column_half(1 - pair_at(place), half)).astype(BF16)


def own_kernel(place, hidden, expert_out, after, keep):
    values = [hidden[e] for e in range(hidden.shape[0])]
    keep[...] = second_product(values, expert_out, column_half(pair_at(place), keep.shape[1]))


def combine_kernel(logits, after, combine):
    value = logits[...]
    weights = jnp.exp(value - jnp.max(value, axis=1, keepdims=True))
    combine[...] = (weights / jnp.sum(weights, axis=1, keepdims=True)).astype(BF16)


def mix_kernel(place, combine, slot_out, mixed, rest, held, sems):
    width = slot_out.shape[1]
    tokens, done = combine.shape[0], held.shape[0]
    block = done // sems.shape[0]
    columns = pl.ds(pl.multiple_of(pair_at(place) * width, width), width)
    copies = []
    for i in range(tokens // block):
        rows = pl.ds(i * block, block)
        value = dot(combine[rows, :], slot_out[...]).astype(BF16)
        if i < sems.shape[0]:
            held[rows, :] = value
            copies.append(pltpu.make_async_copy(held.at[rows], mixed.at[rows, columns], sems.at[i]))
            copies[-1].start()
        else:
            rest[pl.ds(i * block - done, block), :] = value
    for copy in copies:
        copy.wait()


def mix_other_kernel(place, combine, slot_out, rest, before, mixed, held, sems):
    width = slot_out.shape[1]
    blocks = sems.shape[0] - 1
    tokens = combine.shape[0]
    done = tokens - rest.shape[0]
    mine = pl.ds(pl.multiple_of(pair_at(place) * width, width), width)
    other = pl.ds(pl.multiple_of((1 - pair_at(place)) * width, width), width)
    copies = [pltpu.make_async_copy(rest, mixed.at[pl.ds(done, tokens - done), mine], sems.at[blocks])]
    copies[0].start()
    block = tokens // blocks
    for i in range(blocks):
        rows = pl.ds(i * block, block)
        held[rows, :] = dot(combine[rows, :], slot_out[...]).astype(BF16)
        copies.append(pltpu.make_async_copy(held.at[rows], mixed.at[rows, other], sems.at[i]))
        copies[-1].start()
    for copy in copies:
        copy.wait()


def move(value, axes, offsets):
    sizes = [lax.axis_size(axis) for axis in axes]
    moves = []
    for index in range(math.prod(sizes)):
        source, target, stride = index, 0, 1
        for size, offset in zip(reversed(sizes), reversed(offsets)):
            target += (source % size ^ offset) * stride
            source //= size
            stride *= size
        moves.append((index, target))
    return lax.ppermute(value, axes, moves)


def swap_pair(value):
    return move(value, ("pair",), (1,))


def shards(tokens, slot_params, expert_in, expert_out):
    count, model = tokens.shape
    slots = slot_params.shape[1]
    far, near, rest = [lax.axis_size(axis) for axis in ("far", "near", "rest")]
    rows = slots // (far * near)
    half = model // 2
    place = lax.axis_index(("far", "near", "rest", "pair")).astype(jnp.int32).reshape(1)
    any_space = pl.BlockSpec(memory_space=pl.ANY)

    logits, turned, held, side, send = pl.pallas_call(
        gather_kernel,
        out_shape=(
            jax.ShapeDtypeStruct((count, slots), F32),
            jax.ShapeDtypeStruct((slots, count), BF16),
            jax.ShapeDtypeStruct((count, model), BF16),
            jax.ShapeDtypeStruct((slots, SIDE), F32),
            jax.ShapeDtypeStruct((slots, half + SIDE), BF16),
        ),
        in_specs=[SMEM, HBM, HBM],
        out_specs=(VMEM,) * 5,
        scratch_shapes=[pltpu.VMEM((model, slots), BF16), pltpu.SemaphoreType.DMA((count // CHUNK + 1,))],
        compiler_params=params(24),
        name="gather",
    )(place, in_hbm(tokens), in_hbm(slot_params))
    received = swap_pair(send)
    keep = pl.pallas_call(
        own_sums_kernel,
        out_shape=jax.ShapeDtypeStruct((slots, half), F32),
        in_specs=[SMEM, VMEM, VMEM, VMEM, any_space],
        out_specs=VMEM,
        cost_estimate=cost(2 * slots * count * half, 2 * count * (half + slots)),
        compiler_params=params(16),
        name="own_sums",
    )(place, turned, held, side, send)
    sends = pl.pallas_call(
        functools.partial(pair_kernel, rest),
        out_shape=(jax.ShapeDtypeStruct((near * rows, half + SIDE), BF16),) * far,
        in_specs=[SMEM] + [VMEM] * 3,
        out_specs=(VMEM,) * far,
        cost_estimate=cost(0, 6 * slots * model, 128 * slots * model),
        compiler_params=params(16),
        name="pair",
    )(place, keep, side, received)
    parts = [sends[0]] + [move(sends[r], ("far",), (r,)) for r in range(1, far)]
    send, their = pl.pallas_call(
        functools.partial(merge_kernel, rest),
        out_shape=(jax.ShapeDtypeStruct((rows, half + SIDE), BF16),) * 2,
        in_specs=[SMEM] + [VMEM] * far,
        out_specs=(VMEM, VMEM),
        compiler_params=params(16),
        name="merge",
    )(place, *parts)
    plane = ("near", "rest")
    mine = [send] + [move(send, plane, (0, r)) for r in range(1, rest)]
    mine += [move(their, plane, (1, r)) for r in range(rest)]
    combine = pl.pallas_call(
        combine_kernel,
        out_shape=jax.ShapeDtypeStruct((count, slots), BF16),
        in_specs=[VMEM, any_space],
        out_specs=VMEM,
        cost_estimate=cost(8 * count * slots, 6 * count * slots, count * slots),
        compiler_params=params(16),
        name="combine",
    )(logits, send)
    experts, units = expert_out.shape[:2]
    slot_in = pl.pallas_call(
        finish_kernel,
        out_shape=jax.ShapeDtypeStruct((rows, half), BF16),
        in_specs=[any_space] + [VMEM] * len(mine),
        out_specs=VMEM,
        compiler_params=params(16),
        name="finish",
    )(combine, *mine)
    other = swap_pair(slot_in)
    first = pl.pallas_call(
        first_product_kernel,
        out_shape=jax.ShapeDtypeStruct((experts, rows, units), F32),
        in_specs=[SMEM, VMEM, VMEM],
        out_specs=VMEM,
        cost_estimate=cost(2 * rows * units * half * experts, 2 * experts * units * half),
        compiler_params=params(8),
        name="first_product",
    )(place, slot_in, expert_in)
    hidden, send = pl.pallas_call(
        expert_kernel,
        out_shape=(
            jax.ShapeDtypeStruct((experts, rows, units), BF16),
            jax.ShapeDtypeStruct((rows, half), BF16),
        ),
        in_specs=[SMEM, VMEM, VMEM, VMEM, VMEM],
        out_specs=(VMEM, VMEM),
        compiler_params=params(8),
        name="experts",
    )(place, other, first, expert_in, expert_out)
    received = swap_pair(send)
    keep = pl.pallas_call(
        own_kernel,
        out_shape=jax.ShapeDtypeStruct((rows, half), F32),
        in_specs=[SMEM, VMEM, VMEM, any_space],
        out_specs=VMEM,
        cost_estimate=cost(2 * rows * units * half * experts, 2 * experts * units * half),
        compiler_params=params(8),
        name="own",
    )(place, hidden, expert_out, send)
    partial = (keep + received.astype(F32)).astype(BF16)
    groups = far * near
    partials = jnp.broadcast_to(partial, (groups * rest, rows, half))
    partials = lax.all_to_all(partials, ("rest", "far", "near"), split_axis=0, concat_axis=0, tiled=True)
    slot_out = jnp.sum(partials.reshape(rest, groups, rows, half).astype(F32), axis=0)
    slot_out = slot_out.astype(BF16).reshape(slots, half)
    other = swap_pair(slot_out)
    done, blocks = count // 2, 8
    mixed, left = pl.pallas_call(
        mix_kernel,
        out_shape=(
            pltpu.HBM((count, model), BF16),
            jax.ShapeDtypeStruct((count - done, half), BF16),
        ),
        in_specs=[SMEM, VMEM, VMEM],
        out_specs=(HBM, VMEM),
        scratch_shapes=[pltpu.VMEM((done, half), BF16), pltpu.SemaphoreType.DMA((blocks // 2,))],
        cost_estimate=cost(2 * count * slots * half, 2 * count * (half + slots)),
        compiler_params=params(16),
        name="mix",
    )(place, combine, slot_out)
    return pl.pallas_call(
        mix_other_kernel,
        out_shape=jax.ShapeDtypeStruct((count, model), BF16),
        in_specs=[SMEM, VMEM, VMEM, VMEM, HBM],
        out_specs=HBM,
        scratch_shapes=[pltpu.VMEM((count, half), BF16), pltpu.SemaphoreType.DMA((blocks + 1,))],
        input_output_aliases={4: 0},
        cost_estimate=cost(2 * count * slots * half, 2 * count * (half + slots)),
        compiler_params=params(16),
        name="mix_other",
    )(place, combine, other, left, mixed)


def solution(mesh):
    wide, narrow = mesh.shape["wide"], mesh.shape["narrow"]
    cut = Mesh(mesh.devices.reshape(wide // 2, 2, narrow // 2, 2), ("far", "near", "rest", "pair"))
    wide_axes, narrow_axes = ("far", "near"), ("rest", "pair")
    return jax.shard_map(
        shards,
        mesh=cut,
        in_specs=(
            P(wide_axes + narrow_axes, None),
            P(),
            P(wide_axes, None, narrow_axes),
            P(wide_axes, narrow_axes, None),
        ),
        out_specs=P(wide_axes + narrow_axes, None),
        check_vma=False,
    )
```

```python
import functools
import math

import jax
import jax.numpy as jnp
from jax import lax
from jax.experimental import pallas as pl
from jax.experimental.pallas import tpu as pltpu
from jax.sharding import Mesh, PartitionSpec as P

SLOT_PER = 4
SIDE = 128
CHUNK = 256
F32 = jnp.float32
BF16 = jnp.bfloat16
VMEM = pl.BlockSpec(memory_space=pltpu.VMEM)
SMEM = pl.BlockSpec(memory_space=pltpu.SMEM)
HBM = pl.BlockSpec(memory_space=pltpu.HBM)
MIB = 1024 * 1024


def params(mib):
    return pltpu.CompilerParams(vmem_limit_bytes=mib * MIB)


def cost(flops, moved, transcendentals=0):
    return pl.CostEstimate(flops=flops, bytes_accessed=moved, transcendentals=transcendentals)


def in_hbm(value):
    return pltpu.with_memory_space_constraint(value, pltpu.HBM)


def dot(lhs, rhs):
    return jnp.dot(lhs, rhs, preferred_element_type=F32)


def side_state(*columns):
    lane = lax.broadcasted_iota(jnp.int32, (columns[0].shape[0], SIDE), 1)
    out = jnp.zeros((columns[0].shape[0], SIDE), F32)
    for index, value in enumerate(columns):
        out = jnp.where(lane == index, value, out)
    return out


def side_message(peak, total):
    lane = lax.broadcasted_iota(jnp.int32, (peak.shape[0], SIDE), 1)
    out = jnp.zeros((peak.shape[0], SIDE), F32)
    for index, value in enumerate((peak, total)):
        for piece in range(3):
            part = value.astype(BF16).astype(F32)
            out = jnp.where(lane == 3 * index + piece, part, out)
            value = value - part
    return out.astype(BF16)


def read_message(side):
    value = side.astype(F32)
    return (
        value[:, 0:1] + value[:, 1:2] + value[:, 2:3],
        value[:, 3:4] + value[:, 4:5] + value[:, 5:6],
    )


def pair_at(place):
    return place[0] & 1


def near_at(place, rest):
    return place[0] // (2 * rest) & 1


def far_at(place, rest):
    return place[0] // (4 * rest)


def column_half(side, half):
    return pl.ds(pl.multiple_of(side * half, half), half)


def gather_kernel(place, tokens, slot_params, logits, turned, held, side, send, table, sems):
    chunks = tokens.shape[0] // CHUNK
    slots = slot_params.shape[1]
    half = held.shape[1] // 2
    spans = [pl.ds(i * CHUNK, CHUNK) for i in range(chunks)]
    table_copy = pltpu.make_async_copy(slot_params, table, sems.at[chunks])
    table_copy.start()
    copies = [pltpu.make_async_copy(tokens.at[span], held.at[span], sems.at[i]) for i, span in enumerate(spans)]
    for copy in copies:
        copy.start()

    def find_peak(parts, high=None):
        for part in parts:
            top = jnp.max(part.reshape(CHUNK // 8, 8, slots), axis=0)
            high = top if high is None else jnp.maximum(high, top)
        return high

    def weigh(first, parts, peak):
        total = jnp.zeros((8, slots), F32)
        columns = []
        for part in parts:
            weights = jnp.exp(part - peak)
            total = total + jnp.sum(weights.reshape(CHUNK // 8, 8, slots), axis=0)
            columns.append(weights.astype(BF16).T)
        weights = jnp.concatenate(columns, axis=1)
        span = pl.ds(first * CHUNK, len(parts) * CHUNK)
        turned[:, span] = weights
        sums = dot(weights, held[span, column_half(1 - pair_at(place), half)])
        return sums, jnp.sum(total, axis=0, keepdims=True)

    table_copy.wait()
    high = None
    starts = [0] + list(range(1, chunks, 2))
    for first, end in zip(starts, starts[1:] + [chunks]):
        for copy in copies[first:end]:
            copy.wait()
        parts = [dot(held[span, :], table[...]) for span in spans[first:end]]
        for part, span in zip(parts, spans[first:end]):
            logits[span, :] = part
        if end < chunks:
            high = find_peak(parts, high)
    early_peak = jnp.max(high, axis=0, keepdims=True)
    early, early_total = weigh(0, [logits[span, :] for span in spans[:first]], early_peak)
    late_peak = jnp.max(find_peak(parts), axis=0, keepdims=True)
    late, late_total = weigh(first, parts, late_peak)
    peak = jnp.maximum(early_peak, late_peak)
    early_scale, late_scale = jnp.exp(early_peak - peak), jnp.exp(late_peak - peak)
    total = early_total * early_scale + late_total * late_scale
    row = lax.broadcasted_iota(jnp.int32, (8, slots), 0)
    columns = jnp.zeros((8, slots), F32)
    for index, value in enumerate((peak, total, early_scale, late_scale)):
        columns = jnp.where(row == index, value, columns)
    columns = columns.T
    peak, total, early_scale, late_scale = [columns[:, i : i + 1] for i in range(4)]
    send[:, :half] = (early * early_scale + late * late_scale).astype(BF16)
    side[...] = side_state(peak, total, early_scale, late_scale)
    send[:, half:] = side_message(peak, total)


def own_sums_kernel(place, turned, held, side, after, keep):
    columns = column_half(pair_at(place), keep.shape[1])
    early = held.shape[0] - CHUNK
    spans = (pl.ds(0, early), pl.ds(early, CHUNK))
    early, late = [dot(turned[:, span], held[span, columns]) for span in spans]
    keep[...] = early * side[:, 2:3] + late * side[:, 3:4]


def pair_kernel(rest, place, keep, side, received, *sends):
    width = keep.shape[1]
    for r, send in enumerate(sends):
        rows = send.shape[0]
        span = pl.ds(pl.multiple_of((far_at(place, rest) ^ r) * rows, rows), rows)
        peak_mine, total_mine = side[span, 0:1], side[span, 1:2]
        peak_other, total_other = read_message(received[span, width:])
        peak = jnp.maximum(peak_mine, peak_other)
        scale_mine, scale_other = jnp.exp(peak_mine - peak), jnp.exp(peak_other - peak)
        total = total_mine * scale_mine + total_other * scale_other
        sums = keep[span, :] * scale_mine + received[span, :width].astype(F32) * scale_other
        send[:, :width] = sums.astype(BF16)
        send[:, width:] = side_message(peak, total)


def add_parts(parts, width):
    states = [read_message(part[:, width:]) for part in parts]
    peak = states[0][0]
    for other, _ in states[1:]:
        peak = jnp.maximum(peak, other)
    total = jnp.zeros_like(peak)
    sums = jnp.zeros((parts[0].shape[0], width), F32)
    for part, (peak_other, total_other) in zip(parts, states):
        scale = jnp.exp(peak_other - peak)
        total = total + total_other * scale
        sums = sums + part[:, :width].astype(F32) * scale
    return sums, peak, total


def merge_kernel(rest, place, *refs):
    for n, send in enumerate(refs[-2:]):
        rows, width = send.shape[0], send.shape[1] - SIDE
        span = pl.ds(pl.multiple_of((near_at(place, rest) ^ n) * rows, rows), rows)
        sums, peak, total = add_parts([ref[span, :] for ref in refs[:-2]], width)
        send[:, :width] = sums.astype(BF16)
        send[:, width:] = side_message(peak, total)


def finish_kernel(combine, *refs):
    slot_in = refs[-1]
    sums, _, total = add_parts([ref[...] for ref in refs[:-1]], slot_in.shape[1])
    slot_in[...] = (sums / total).astype(BF16)


def first_product_kernel(place, slot_in, expert_in, result):
    half = slot_in.shape[1]
    for e in range(expert_in.shape[0]):
        result[e] = dot(slot_in[...], expert_in[e, column_half(pair_at(place), half), :])


def second_product(hidden, weights, columns):
    row = lax.broadcasted_iota(jnp.int32, (hidden[0].shape[0], 1), 0)
    result = 0.0
    for e, value in enumerate(hidden):
        result = jnp.where(row // SLOT_PER == e, dot(value, weights[e, :, columns]), result)
    return result


def expert_kernel(place, slot_in, first, expert_in, expert_out, hidden, send):
    half = slot_in.shape[1]
    values = []
    for e in range(expert_in.shape[0]):
        product = first[e] + dot(slot_in[...], expert_in[e, column_half(1 - pair_at(place), half), :])
        values.append(jax.nn.gelu(product).astype(BF16))
        hidden[e] = values[e]
    send[...] = second_product(values, expert_out, column_half(1 - pair_at(place), half)).astype(BF16)


def own_kernel(place, hidden, expert_out, after, keep):
    values = [hidden[e] for e in range(hidden.shape[0])]
    keep[...] = second_product(values, expert_out, column_half(pair_at(place), keep.shape[1]))


def combine_kernel(logits, after, combine):
    value = logits[...]
    weights = jnp.exp(value - jnp.max(value, axis=1, keepdims=True))
    combine[...] = (weights / jnp.sum(weights, axis=1, keepdims=True)).astype(BF16)


def mix_kernel(place, combine, slot_out, mixed, rest, held, sems):
    width = slot_out.shape[1]
    tokens, done = combine.shape[0], held.shape[0]
    block = done // sems.shape[0]
    columns = pl.ds(pl.multiple_of(pair_at(place) * width, width), width)
    copies = []
    for i in range(tokens // block):
        rows = pl.ds(i * block, block)
        value = dot(combine[rows, :], slot_out[...]).astype(BF16)
        if i < sems.shape[0]:
            held[rows, :] = value
            copies.append(pltpu.make_async_copy(held.at[rows], mixed.at[rows, columns], sems.at[i]))
            copies[-1].start()
        else:
            rest[pl.ds(i * block - done, block), :] = value
    for copy in copies:
        copy.wait()


def mix_other_kernel(place, combine, slot_out, rest, before, mixed, held, sems):
    width = slot_out.shape[1]
    blocks = sems.shape[0] - 1
    tokens = combine.shape[0]
    done = tokens - rest.shape[0]
    mine = pl.ds(pl.multiple_of(pair_at(place) * width, width), width)
    other = pl.ds(pl.multiple_of((1 - pair_at(place)) * width, width), width)
    copies = [pltpu.make_async_copy(rest, mixed.at[pl.ds(done, tokens - done), mine], sems.at[blocks])]
    copies[0].start()
    block = tokens // blocks
    for i in range(blocks):
        rows = pl.ds(i * block, block)
        held[rows, :] = dot(combine[rows, :], slot_out[...]).astype(BF16)
        copies.append(pltpu.make_async_copy(held.at[rows], mixed.at[rows, other], sems.at[i]))
        copies[-1].start()
    for copy in copies:
        copy.wait()


def move(value, axes, offsets):
    sizes = [lax.axis_size(axis) for axis in axes]
    moves = []
    for index in range(math.prod(sizes)):
        source, target, stride = index, 0, 1
        for size, offset in zip(reversed(sizes), reversed(offsets)):
            target += (source % size ^ offset) * stride
            source //= size
            stride *= size
        moves.append((index, target))
    return lax.ppermute(value, axes, moves)


def swap_pair(value):
    return move(value, ("pair",), (1,))


def shards(tokens, slot_params, expert_in, expert_out):
    count, model = tokens.shape
    slots = slot_params.shape[1]
    far, near, rest = [lax.axis_size(axis) for axis in ("far", "near", "rest")]
    rows = slots // (far * near)
    half = model // 2
    place = lax.axis_index(("far", "near", "rest", "pair")).astype(jnp.int32).reshape(1)
    any_space = pl.BlockSpec(memory_space=pl.ANY)

    logits, turned, held, side, send = pl.pallas_call(
        gather_kernel,
        out_shape=(
            jax.ShapeDtypeStruct((count, slots), F32),
            jax.ShapeDtypeStruct((slots, count), BF16),
            jax.ShapeDtypeStruct((count, model), BF16),
            jax.ShapeDtypeStruct((slots, SIDE), F32),
            jax.ShapeDtypeStruct((slots, half + SIDE), BF16),
        ),
        in_specs=[SMEM, HBM, HBM],
        out_specs=(VMEM,) * 5,
        scratch_shapes=[pltpu.VMEM((model, slots), BF16), pltpu.SemaphoreType.DMA((count // CHUNK + 1,))],
        compiler_params=params(24),
        name="gather",
    )(place, in_hbm(tokens), in_hbm(slot_params))
    received = swap_pair(send)
    keep = pl.pallas_call(
        own_sums_kernel,
        out_shape=jax.ShapeDtypeStruct((slots, half), F32),
        in_specs=[SMEM, VMEM, VMEM, VMEM, any_space],
        out_specs=VMEM,
        cost_estimate=cost(2 * slots * count * half, 2 * count * (half + slots)),
        compiler_params=params(16),
        name="own_sums",
    )(place, turned, held, side, send)
    sends = pl.pallas_call(
        functools.partial(pair_kernel, rest),
        out_shape=(jax.ShapeDtypeStruct((near * rows, half + SIDE), BF16),) * far,
        in_specs=[SMEM] + [VMEM] * 3,
        out_specs=(VMEM,) * far,
        cost_estimate=cost(0, 6 * slots * model, 128 * slots * model),
        compiler_params=params(16),
        name="pair",
    )(place, keep, side, received)
    parts = [sends[0]] + [move(sends[r], ("far",), (r,)) for r in range(1, far)]
    send, their = pl.pallas_call(
        functools.partial(merge_kernel, rest),
        out_shape=(jax.ShapeDtypeStruct((rows, half + SIDE), BF16),) * 2,
        in_specs=[SMEM] + [VMEM] * far,
        out_specs=(VMEM, VMEM),
        compiler_params=params(16),
        name="merge",
    )(place, *parts)
    plane = ("near", "rest")
    mine = [move(their, plane, (1, r)) for r in reversed(range(rest))]
    mine = [send] + [move(send, plane, (0, r)) for r in range(1, rest)] + mine
    combine = pl.pallas_call(
        combine_kernel,
        out_shape=jax.ShapeDtypeStruct((count, slots), BF16),
        in_specs=[VMEM, any_space],
        out_specs=VMEM,
        cost_estimate=cost(8 * count * slots, 6 * count * slots, count * slots),
        compiler_params=params(16),
        name="combine",
    )(logits, send)
    experts, units = expert_out.shape[:2]
    slot_in = pl.pallas_call(
        finish_kernel,
        out_shape=jax.ShapeDtypeStruct((rows, half), BF16),
        in_specs=[any_space] + [VMEM] * len(mine),
        out_specs=VMEM,
        compiler_params=params(16),
        name="finish",
    )(combine, *mine)
    other = swap_pair(slot_in)
    first = pl.pallas_call(
        first_product_kernel,
        out_shape=jax.ShapeDtypeStruct((experts, rows, units), F32),
        in_specs=[SMEM, VMEM, VMEM],
        out_specs=VMEM,
        cost_estimate=cost(2 * rows * units * half * experts, 2 * experts * units * half),
        compiler_params=params(8),
        name="first_product",
    )(place, slot_in, expert_in)
    hidden, send = pl.pallas_call(
        expert_kernel,
        out_shape=(
            jax.ShapeDtypeStruct((experts, rows, units), BF16),
            jax.ShapeDtypeStruct((rows, half), BF16),
        ),
        in_specs=[SMEM, VMEM, VMEM, VMEM, VMEM],
        out_specs=(VMEM, VMEM),
        compiler_params=params(8),
        name="experts",
    )(place, other, first, expert_in, expert_out)
    received = swap_pair(send)
    keep = pl.pallas_call(
        own_kernel,
        out_shape=jax.ShapeDtypeStruct((rows, half), F32),
        in_specs=[SMEM, VMEM, VMEM, any_space],
        out_specs=VMEM,
        cost_estimate=cost(2 * rows * units * half * experts, 2 * experts * units * half),
        compiler_params=params(8),
        name="own",
    )(place, hidden, expert_out, send)
    partial = (keep + received.astype(F32)).astype(BF16)
    groups = far * near
    partials = jnp.broadcast_to(partial, (groups * rest, rows, half))
    partials = lax.all_to_all(partials, ("rest", "far", "near"), split_axis=0, concat_axis=0, tiled=True)
    slot_out = jnp.sum(partials.reshape(rest, groups, rows, half).astype(F32), axis=0)
    slot_out = slot_out.astype(BF16).reshape(slots, half)
    other = swap_pair(slot_out)
    done, blocks = count // 2, 8
    mixed, left = pl.pallas_call(
        mix_kernel,
        out_shape=(
            pltpu.HBM((count, model), BF16),
            jax.ShapeDtypeStruct((count - done, half), BF16),
        ),
        in_specs=[SMEM, VMEM, VMEM],
        out_specs=(HBM, VMEM),
        scratch_shapes=[pltpu.VMEM((done, half), BF16), pltpu.SemaphoreType.DMA((blocks // 2,))],
        cost_estimate=cost(2 * count * slots * half, 2 * count * (half + slots)),
        compiler_params=params(16),
        name="mix",
    )(place, combine, slot_out)
    return pl.pallas_call(
        mix_other_kernel,
        out_shape=jax.ShapeDtypeStruct((count, model), BF16),
        in_specs=[SMEM, VMEM, VMEM, VMEM, HBM],
        out_specs=HBM,
        scratch_shapes=[pltpu.VMEM((count, half), BF16), pltpu.SemaphoreType.DMA((blocks + 1,))],
        input_output_aliases={4: 0},
        cost_estimate=cost(2 * count * slots * half, 2 * count * (half + slots)),
        compiler_params=params(16),
        name="mix_other",
    )(place, combine, other, left, mixed)


def solution(mesh):
    wide, narrow = mesh.shape["wide"], mesh.shape["narrow"]
    cut = Mesh(mesh.devices.reshape(wide // 2, 2, narrow // 2, 2), ("far", "near", "rest", "pair"))
    wide_axes, narrow_axes = ("far", "near"), ("rest", "pair")
    return jax.shard_map(
        shards,
        mesh=cut,
        in_specs=(
            P(wide_axes + narrow_axes, None),
            P(),
            P(wide_axes, None, narrow_axes),
            P(wide_axes, narrow_axes, None),
        ),
        out_specs=P(wide_axes + narrow_axes, None),
        check_vma=False,
    )
```

```python
import functools
import math

import jax
import jax.numpy as jnp
from jax import lax
from jax.experimental import pallas as pl
from jax.experimental.pallas import tpu as pltpu
from jax.sharding import Mesh, PartitionSpec as P

SLOT_PER = 4
SIDE = 128
CHUNK = 256
F32 = jnp.float32
BF16 = jnp.bfloat16
VMEM = pl.BlockSpec(memory_space=pltpu.VMEM)
SMEM = pl.BlockSpec(memory_space=pltpu.SMEM)
HBM = pl.BlockSpec(memory_space=pltpu.HBM)
MIB = 1024 * 1024


def params(mib):
    return pltpu.CompilerParams(vmem_limit_bytes=mib * MIB)


def cost(flops, moved, transcendentals=0):
    return pl.CostEstimate(flops=flops, bytes_accessed=moved, transcendentals=transcendentals)


def in_hbm(value):
    return pltpu.with_memory_space_constraint(value, pltpu.HBM)


def dot(lhs, rhs):
    return jnp.dot(lhs, rhs, preferred_element_type=F32)


def side_state(*columns):
    lane = lax.broadcasted_iota(jnp.int32, (columns[0].shape[0], SIDE), 1)
    out = jnp.zeros((columns[0].shape[0], SIDE), F32)
    for index, value in enumerate(columns):
        out = jnp.where(lane == index, value, out)
    return out


def side_message(peak, total):
    lane = lax.broadcasted_iota(jnp.int32, (peak.shape[0], SIDE), 1)
    out = jnp.zeros((peak.shape[0], SIDE), F32)
    for index, value in enumerate((peak, total)):
        for piece in range(3):
            part = value.astype(BF16).astype(F32)
            out = jnp.where(lane == 3 * index + piece, part, out)
            value = value - part
    return out.astype(BF16)


def read_message(side):
    value = side.astype(F32)
    return (
        value[:, 0:1] + value[:, 1:2] + value[:, 2:3],
        value[:, 3:4] + value[:, 4:5] + value[:, 5:6],
    )


def pair_at(place):
    return place[0] & 1


def near_at(place, rest):
    return place[0] // (2 * rest) & 1


def far_at(place, rest):
    return place[0] // (4 * rest)


def column_half(side, half):
    return pl.ds(pl.multiple_of(side * half, half), half)


def gather_kernel(place, tokens, slot_params, logits, turned, held, side, send, table, sems):
    chunks = tokens.shape[0] // CHUNK
    slots = slot_params.shape[1]
    half = held.shape[1] // 2
    spans = [pl.ds(i * CHUNK, CHUNK) for i in range(chunks)]
    table_copy = pltpu.make_async_copy(slot_params, table, sems.at[chunks])
    table_copy.start()
    copies = [pltpu.make_async_copy(tokens.at[span], held.at[span], sems.at[i]) for i, span in enumerate(spans)]
    for copy in copies:
        copy.start()

    def find_peak(parts, high=None):
        for part in parts:
            top = jnp.max(part.reshape(CHUNK // 8, 8, slots), axis=0)
            high = top if high is None else jnp.maximum(high, top)
        return high

    def weigh(first, parts, peak):
        total = jnp.zeros((8, slots), F32)
        columns = []
        for part in parts:
            weights = jnp.exp(part - peak)
            total = total + jnp.sum(weights.reshape(CHUNK // 8, 8, slots), axis=0)
            columns.append(weights.astype(BF16).T)
        weights = jnp.concatenate(columns, axis=1)
        span = pl.ds(first * CHUNK, len(parts) * CHUNK)
        turned[:, span] = weights
        sums = dot(weights, held[span, column_half(1 - pair_at(place), half)])
        return sums, jnp.sum(total, axis=0, keepdims=True)

    table_copy.wait()
    high = None
    starts = [0] + list(range(1, chunks, 2))
    for first, end in zip(starts, starts[1:] + [chunks]):
        for copy in copies[first:end]:
            copy.wait()
        parts = [dot(held[span, :], table[...]) for span in spans[first:end]]
        for part, span in zip(parts, spans[first:end]):
            logits[span, :] = part
        if end < chunks:
            high = find_peak(parts, high)
    early_peak = jnp.max(high, axis=0, keepdims=True)
    early, early_total = weigh(0, [logits[span, :] for span in spans[:first]], early_peak)
    late_peak = jnp.max(find_peak(parts), axis=0, keepdims=True)
    late, late_total = weigh(first, parts, late_peak)
    peak = jnp.maximum(early_peak, late_peak)
    early_scale, late_scale = jnp.exp(early_peak - peak), jnp.exp(late_peak - peak)
    total = early_total * early_scale + late_total * late_scale
    row = lax.broadcasted_iota(jnp.int32, (8, slots), 0)
    columns = jnp.zeros((8, slots), F32)
    for index, value in enumerate((peak, total, early_scale, late_scale)):
        columns = jnp.where(row == index, value, columns)
    columns = columns.T
    peak, total, early_scale, late_scale = [columns[:, i : i + 1] for i in range(4)]
    send[:, :half] = (early * early_scale + late * late_scale).astype(BF16)
    side[...] = side_state(peak, total, early_scale, late_scale)
    send[:, half:] = side_message(peak, total)


def own_sums_kernel(place, turned, held, side, after, keep):
    columns = column_half(pair_at(place), keep.shape[1])
    early = held.shape[0] - CHUNK
    spans = (pl.ds(0, early), pl.ds(early, CHUNK))
    early, late = [dot(turned[:, span], held[span, columns]) for span in spans]
    keep[...] = early * side[:, 2:3] + late * side[:, 3:4]


def pair_kernel(rest, place, keep, side, received, *sends):
    width = keep.shape[1]
    for r, send in enumerate(sends):
        rows = send.shape[0]
        span = pl.ds(pl.multiple_of((far_at(place, rest) ^ r) * rows, rows), rows)
        peak_mine, total_mine = side[span, 0:1], side[span, 1:2]
        peak_other, total_other = read_message(received[span, width:])
        peak = jnp.maximum(peak_mine, peak_other)
        scale_mine, scale_other = jnp.exp(peak_mine - peak), jnp.exp(peak_other - peak)
        total = total_mine * scale_mine + total_other * scale_other
        sums = keep[span, :] * scale_mine + received[span, :width].astype(F32) * scale_other
        send[:, :width] = sums.astype(BF16)
        send[:, width:] = side_message(peak, total)


def add_parts(parts, width):
    states = [read_message(part[:, width:]) for part in parts]
    peak = states[0][0]
    for other, _ in states[1:]:
        peak = jnp.maximum(peak, other)
    total = jnp.zeros_like(peak)
    sums = jnp.zeros((parts[0].shape[0], width), F32)
    for part, (peak_other, total_other) in zip(parts, states):
        scale = jnp.exp(peak_other - peak)
        total = total + total_other * scale
        sums = sums + part[:, :width].astype(F32) * scale
    return sums, peak, total


def merge_kernel(rest, place, *refs):
    for n, send in enumerate(refs[-2:]):
        rows, width = send.shape[0], send.shape[1] - SIDE
        span = pl.ds(pl.multiple_of((near_at(place, rest) ^ n) * rows, rows), rows)
        sums, peak, total = add_parts([ref[span, :] for ref in refs[:-2]], width)
        send[:, :width] = sums.astype(BF16)
        send[:, width:] = side_message(peak, total)


def finish_kernel(combine, *refs):
    slot_in = refs[-1]
    sums, _, total = add_parts([ref[...] for ref in refs[:-1]], slot_in.shape[1])
    slot_in[...] = (sums / total).astype(BF16)


def first_product_kernel(place, slot_in, expert_in, result):
    half = slot_in.shape[1]
    for e in range(expert_in.shape[0]):
        result[e] = dot(slot_in[...], expert_in[e, column_half(pair_at(place), half), :])


def second_product(hidden, weights, columns):
    row = lax.broadcasted_iota(jnp.int32, (hidden[0].shape[0], 1), 0)
    result = 0.0
    for e, value in enumerate(hidden):
        result = jnp.where(row // SLOT_PER == e, dot(value, weights[e, :, columns]), result)
    return result


def expert_kernel(place, slot_in, first, expert_in, expert_out, hidden, send):
    half = slot_in.shape[1]
    values = []
    for e in range(expert_in.shape[0]):
        product = first[e] + dot(slot_in[...], expert_in[e, column_half(1 - pair_at(place), half), :])
        values.append(jax.nn.gelu(product).astype(BF16))
        hidden[e] = values[e]
    send[...] = second_product(values, expert_out, column_half(1 - pair_at(place), half)).astype(BF16)


def own_kernel(place, hidden, expert_out, after, keep):
    values = [hidden[e] for e in range(hidden.shape[0])]
    keep[...] = second_product(values, expert_out, column_half(pair_at(place), keep.shape[1]))


def combine_kernel(logits, after, combine):
    value = logits[...]
    weights = jnp.exp(value - jnp.max(value, axis=1, keepdims=True))
    combine[...] = (weights / jnp.sum(weights, axis=1, keepdims=True)).astype(BF16)


def mix_kernel(place, combine, slot_out, mixed, rest, held, sems):
    width = slot_out.shape[1]
    tokens, done = combine.shape[0], held.shape[0]
    block = done // sems.shape[0]
    columns = pl.ds(pl.multiple_of(pair_at(place) * width, width), width)
    copies = []
    for i in range(tokens // block):
        rows = pl.ds(i * block, block)
        value = dot(combine[rows, :], slot_out[...]).astype(BF16)
        if i < sems.shape[0]:
            held[rows, :] = value
            copies.append(pltpu.make_async_copy(held.at[rows], mixed.at[rows, columns], sems.at[i]))
            copies[-1].start()
        else:
            rest[pl.ds(i * block - done, block), :] = value
    for copy in copies:
        copy.wait()


def mix_other_kernel(place, combine, slot_out, rest, before, mixed, held, sems):
    width = slot_out.shape[1]
    blocks = sems.shape[0] - 1
    tokens = combine.shape[0]
    done = tokens - rest.shape[0]
    mine = pl.ds(pl.multiple_of(pair_at(place) * width, width), width)
    other = pl.ds(pl.multiple_of((1 - pair_at(place)) * width, width), width)
    copies = [pltpu.make_async_copy(rest, mixed.at[pl.ds(done, tokens - done), mine], sems.at[blocks])]
    copies[0].start()
    block = tokens // blocks
    for i in range(blocks):
        rows = pl.ds(i * block, block)
        held[rows, :] = dot(combine[rows, :], slot_out[...]).astype(BF16)
        copies.append(pltpu.make_async_copy(held.at[rows], mixed.at[rows, other], sems.at[i]))
        copies[-1].start()
    for copy in copies:
        copy.wait()


def move(value, axes, offsets):
    sizes = [lax.axis_size(axis) for axis in axes]
    moves = []
    for index in range(math.prod(sizes)):
        source, target, stride = index, 0, 1
        for size, offset in zip(reversed(sizes), reversed(offsets)):
            target += (source % size ^ offset) * stride
            source //= size
            stride *= size
        moves.append((index, target))
    return lax.ppermute(value, axes, moves)


def swap_pair(value):
    return move(value, ("pair",), (1,))


def shards(tokens, slot_params, expert_in, expert_out):
    count, model = tokens.shape
    slots = slot_params.shape[1]
    far, near, rest = [lax.axis_size(axis) for axis in ("far", "near", "rest")]
    rows = slots // (far * near)
    half = model // 2
    place = lax.axis_index(("far", "near", "rest", "pair")).astype(jnp.int32).reshape(1)
    any_space = pl.BlockSpec(memory_space=pl.ANY)

    logits, turned, held, side, send = pl.pallas_call(
        gather_kernel,
        out_shape=(
            jax.ShapeDtypeStruct((count, slots), F32),
            jax.ShapeDtypeStruct((slots, count), BF16),
            jax.ShapeDtypeStruct((count, model), BF16),
            jax.ShapeDtypeStruct((slots, SIDE), F32),
            jax.ShapeDtypeStruct((slots, half + SIDE), BF16),
        ),
        in_specs=[SMEM, HBM, HBM],
        out_specs=(VMEM,) * 5,
        scratch_shapes=[pltpu.VMEM((model, slots), BF16), pltpu.SemaphoreType.DMA((count // CHUNK + 1,))],
        compiler_params=params(24),
        name="gather",
    )(place, in_hbm(tokens), in_hbm(slot_params))
    received = swap_pair(send)
    keep = pl.pallas_call(
        own_sums_kernel,
        out_shape=jax.ShapeDtypeStruct((slots, half), F32),
        in_specs=[SMEM, VMEM, VMEM, VMEM, any_space],
        out_specs=VMEM,
        cost_estimate=cost(2 * slots * count * half, 2 * count * (half + slots)),
        compiler_params=params(16),
        name="own_sums",
    )(place, turned, held, side, send)
    sends = pl.pallas_call(
        functools.partial(pair_kernel, rest),
        out_shape=(jax.ShapeDtypeStruct((near * rows, half + SIDE), BF16),) * far,
        in_specs=[SMEM] + [VMEM] * 3,
        out_specs=(VMEM,) * far,
        cost_estimate=cost(0, 6 * slots * model, 128 * slots * model),
        compiler_params=params(16),
        name="pair",
    )(place, keep, side, received)
    parts = [sends[0]] + [move(sends[r], ("far",), (r,)) for r in range(1, far)]
    send, their = pl.pallas_call(
        functools.partial(merge_kernel, rest),
        out_shape=(jax.ShapeDtypeStruct((rows, half + SIDE), BF16),) * 2,
        in_specs=[SMEM] + [VMEM] * far,
        out_specs=(VMEM, VMEM),
        compiler_params=params(16),
        name="merge",
    )(place, *parts)
    plane = ("near", "rest")
    mine = [move(their, plane, (1, r)) for r in reversed(range(rest))]
    mine = [send] + [move(send, plane, (0, r)) for r in range(1, rest)] + mine
    combine = pl.pallas_call(
        combine_kernel,
        out_shape=jax.ShapeDtypeStruct((count, slots), BF16),
        in_specs=[VMEM, any_space],
        out_specs=VMEM,
        cost_estimate=cost(8 * count * slots, 6 * count * slots, count * slots),
        compiler_params=params(16),
        name="combine",
    )(logits, send)
    experts, units = expert_out.shape[:2]
    slot_in = pl.pallas_call(
        finish_kernel,
        out_shape=jax.ShapeDtypeStruct((rows, half), BF16),
        in_specs=[any_space] + [VMEM] * len(mine),
        out_specs=VMEM,
        compiler_params=params(16),
        name="finish",
    )(combine, *mine)
    other = swap_pair(slot_in)
    first = pl.pallas_call(
        first_product_kernel,
        out_shape=jax.ShapeDtypeStruct((experts, rows, units), F32),
        in_specs=[SMEM, VMEM, VMEM],
        out_specs=VMEM,
        cost_estimate=cost(2 * rows * units * half * experts, 2 * experts * units * half),
        compiler_params=params(8),
        name="first_product",
    )(place, slot_in, expert_in)
    hidden, send = pl.pallas_call(
        expert_kernel,
        out_shape=(
            jax.ShapeDtypeStruct((experts, rows, units), BF16),
            jax.ShapeDtypeStruct((rows, half), BF16),
        ),
        in_specs=[SMEM, VMEM, VMEM, VMEM, VMEM],
        out_specs=(VMEM, VMEM),
        compiler_params=params(8),
        name="experts",
    )(place, other, first, expert_in, expert_out)
    received = swap_pair(send)
    keep = pl.pallas_call(
        own_kernel,
        out_shape=jax.ShapeDtypeStruct((rows, half), F32),
        in_specs=[SMEM, VMEM, VMEM, any_space],
        out_specs=VMEM,
        cost_estimate=cost(2 * rows * units * half * experts, 2 * experts * units * half),
        compiler_params=params(8),
        name="own",
    )(place, hidden, expert_out, send)
    partial = keep + received.astype(F32)
    travelling = partial.astype(BF16)
    for r in range(1, rest):
        partial = partial + move(travelling, ("rest",), (r,)).astype(F32)
    block = jnp.broadcast_to(partial.astype(BF16), (far * near, rows, half))
    slot_out = lax.all_to_all(block, ("far", "near"), split_axis=0, concat_axis=0, tiled=True)
    slot_out = slot_out.reshape(slots, half)
    other = swap_pair(slot_out)
    done, blocks = count // 2, 8
    mixed, left = pl.pallas_call(
        mix_kernel,
        out_shape=(
            pltpu.HBM((count, model), BF16),
            jax.ShapeDtypeStruct((count - done, half), BF16),
        ),
        in_specs=[SMEM, VMEM, VMEM],
        out_specs=(HBM, VMEM),
        scratch_shapes=[pltpu.VMEM((done, half), BF16), pltpu.SemaphoreType.DMA((blocks // 2,))],
        cost_estimate=cost(2 * count * slots * half, 2 * count * (half + slots)),
        compiler_params=params(16),
        name="mix",
    )(place, combine, slot_out)
    return pl.pallas_call(
        mix_other_kernel,
        out_shape=jax.ShapeDtypeStruct((count, model), BF16),
        in_specs=[SMEM, VMEM, VMEM, VMEM, HBM],
        out_specs=HBM,
        scratch_shapes=[pltpu.VMEM((count, half), BF16), pltpu.SemaphoreType.DMA((blocks + 1,))],
        input_output_aliases={4: 0},
        cost_estimate=cost(2 * count * slots * half, 2 * count * (half + slots)),
        compiler_params=params(16),
        name="mix_other",
    )(place, combine, other, left, mixed)


def solution(mesh):
    wide, narrow = mesh.shape["wide"], mesh.shape["narrow"]
    cut = Mesh(mesh.devices.reshape(wide // 2, 2, narrow // 2, 2), ("far", "near", "rest", "pair"))
    wide_axes, narrow_axes = ("far", "near"), ("rest", "pair")
    return jax.shard_map(
        shards,
        mesh=cut,
        in_specs=(
            P(wide_axes + narrow_axes, None),
            P(),
            P(wide_axes, None, narrow_axes),
            P(wide_axes, narrow_axes, None),
        ),
        out_specs=P(wide_axes + narrow_axes, None),
        check_vma=False,
    )
```

```python
import functools
import math

import jax
import jax.numpy as jnp
from jax import lax
from jax.experimental import pallas as pl
from jax.experimental.pallas import tpu as pltpu
from jax.sharding import Mesh, PartitionSpec as P

SLOT_PER = 4
SIDE = 128
CHUNK = 256
F32 = jnp.float32
BF16 = jnp.bfloat16
VMEM = pl.BlockSpec(memory_space=pltpu.VMEM)
SMEM = pl.BlockSpec(memory_space=pltpu.SMEM)
HBM = pl.BlockSpec(memory_space=pltpu.HBM)
MIB = 1024 * 1024


def params(mib):
    return pltpu.CompilerParams(vmem_limit_bytes=mib * MIB)


def cost(flops, moved, transcendentals=0):
    return pl.CostEstimate(flops=flops, bytes_accessed=moved, transcendentals=transcendentals)


def in_hbm(value):
    return pltpu.with_memory_space_constraint(value, pltpu.HBM)


def dot(lhs, rhs):
    return jnp.dot(lhs, rhs, preferred_element_type=F32)


def side_state(*columns):
    lane = lax.broadcasted_iota(jnp.int32, (columns[0].shape[0], SIDE), 1)
    out = jnp.zeros((columns[0].shape[0], SIDE), F32)
    for index, value in enumerate(columns):
        out = jnp.where(lane == index, value, out)
    return out


def side_message(peak, total):
    lane = lax.broadcasted_iota(jnp.int32, (peak.shape[0], SIDE), 1)
    out = jnp.zeros((peak.shape[0], SIDE), F32)
    for index, value in enumerate((peak, total)):
        for piece in range(3):
            part = value.astype(BF16).astype(F32)
            out = jnp.where(lane == 3 * index + piece, part, out)
            value = value - part
    return out.astype(BF16)


def read_message(side):
    value = side.astype(F32)
    return (
        value[:, 0:1] + value[:, 1:2] + value[:, 2:3],
        value[:, 3:4] + value[:, 4:5] + value[:, 5:6],
    )


def pair_at(place):
    return place[0] & 1


def near_at(place, rest):
    return place[0] // (2 * rest) & 1


def far_at(place, rest):
    return place[0] // (4 * rest)


def column_half(side, half):
    return pl.ds(pl.multiple_of(side * half, half), half)


def gather_kernel(place, tokens, slot_params, logits, turned, held, side, send, table, sems):
    chunks = tokens.shape[0] // CHUNK
    slots = slot_params.shape[1]
    half = held.shape[1] // 2
    spans = [pl.ds(i * CHUNK, CHUNK) for i in range(chunks)]
    table_copy = pltpu.make_async_copy(slot_params, table, sems.at[chunks])
    table_copy.start()
    copies = [pltpu.make_async_copy(tokens.at[span], held.at[span], sems.at[i]) for i, span in enumerate(spans)]
    for copy in copies:
        copy.start()

    def find_peak(parts, high=None):
        for part in parts:
            top = jnp.max(part.reshape(CHUNK // 8, 8, slots), axis=0)
            high = top if high is None else jnp.maximum(high, top)
        return high

    def weigh(first, parts, peak):
        total = jnp.zeros((8, slots), F32)
        columns = []
        for part in parts:
            weights = jnp.exp(part - peak)
            total = total + jnp.sum(weights.reshape(CHUNK // 8, 8, slots), axis=0)
            columns.append(weights.astype(BF16).T)
        weights = jnp.concatenate(columns, axis=1)
        span = pl.ds(first * CHUNK, len(parts) * CHUNK)
        turned[:, span] = weights
        sums = dot(weights, held[span, column_half(1 - pair_at(place), half)])
        return sums, jnp.sum(total, axis=0, keepdims=True)

    table_copy.wait()
    high = None
    starts = [0] + list(range(1, chunks, 2))
    for first, end in zip(starts, starts[1:] + [chunks]):
        for copy in copies[first:end]:
            copy.wait()
        parts = [dot(held[span, :], table[...]) for span in spans[first:end]]
        for part, span in zip(parts, spans[first:end]):
            logits[span, :] = part
        if end < chunks:
            high = find_peak(parts, high)
    early_peak = jnp.max(high, axis=0, keepdims=True)
    early, early_total = weigh(0, [logits[span, :] for span in spans[:first]], early_peak)
    late_peak = jnp.max(find_peak(parts), axis=0, keepdims=True)
    late, late_total = weigh(first, parts, late_peak)
    peak = jnp.maximum(early_peak, late_peak)
    early_scale, late_scale = jnp.exp(early_peak - peak), jnp.exp(late_peak - peak)
    total = early_total * early_scale + late_total * late_scale
    row = lax.broadcasted_iota(jnp.int32, (8, slots), 0)
    columns = jnp.zeros((8, slots), F32)
    for index, value in enumerate((peak, total, early_scale, late_scale)):
        columns = jnp.where(row == index, value, columns)
    columns = columns.T
    peak, total, early_scale, late_scale = [columns[:, i : i + 1] for i in range(4)]
    send[:, :half] = (early * early_scale + late * late_scale).astype(BF16)
    side[...] = side_state(peak, total, early_scale, late_scale)
    send[:, half:] = side_message(peak, total)


def own_sums_kernel(place, turned, held, side, after, keep):
    columns = column_half(pair_at(place), keep.shape[1])
    early = held.shape[0] - CHUNK
    spans = (pl.ds(0, early), pl.ds(early, CHUNK))
    early, late = [dot(turned[:, span], held[span, columns]) for span in spans]
    keep[...] = early * side[:, 2:3] + late * side[:, 3:4]


def pair_kernel(rest, place, keep, side, received, *sends):
    width = keep.shape[1]
    for r, send in enumerate(sends):
        rows = send.shape[0]
        span = pl.ds(pl.multiple_of((far_at(place, rest) ^ r) * rows, rows), rows)
        peak_mine, total_mine = side[span, 0:1], side[span, 1:2]
        peak_other, total_other = read_message(received[span, width:])
        peak = jnp.maximum(peak_mine, peak_other)
        scale_mine, scale_other = jnp.exp(peak_mine - peak), jnp.exp(peak_other - peak)
        total = total_mine * scale_mine + total_other * scale_other
        sums = keep[span, :] * scale_mine + received[span, :width].astype(F32) * scale_other
        send[:, :width] = sums.astype(BF16)
        send[:, width:] = side_message(peak, total)


def add_parts(parts, width):
    states = [read_message(part[:, width:]) for part in parts]
    peak = states[0][0]
    for other, _ in states[1:]:
        peak = jnp.maximum(peak, other)
    total = jnp.zeros_like(peak)
    sums = jnp.zeros((parts[0].shape[0], width), F32)
    for part, (peak_other, total_other) in zip(parts, states):
        scale = jnp.exp(peak_other - peak)
        total = total + total_other * scale
        sums = sums + part[:, :width].astype(F32) * scale
    return sums, peak, total


def merge_kernel(rest, place, *refs):
    for n, send in enumerate(refs[-2:]):
        rows, width = send.shape[0], send.shape[1] - SIDE
        span = pl.ds(pl.multiple_of((near_at(place, rest) ^ n) * rows, rows), rows)
        sums, peak, total = add_parts([ref[span, :] for ref in refs[:-2]], width)
        send[:, :width] = sums.astype(BF16)
        send[:, width:] = side_message(peak, total)


def finish_kernel(combine, *refs):
    slot_in = refs[-1]
    sums, _, total = add_parts([ref[...] for ref in refs[:-1]], slot_in.shape[1])
    slot_in[...] = (sums / total).astype(BF16)


def first_product_kernel(place, slot_in, expert_in, result):
    half = slot_in.shape[1]
    for e in range(expert_in.shape[0]):
        result[e] = dot(slot_in[...], expert_in[e, column_half(pair_at(place), half), :])


def second_product(hidden, weights, columns):
    row = lax.broadcasted_iota(jnp.int32, (hidden[0].shape[0], 1), 0)
    result = 0.0
    for e, value in enumerate(hidden):
        result = jnp.where(row // SLOT_PER == e, dot(value, weights[e, :, columns]), result)
    return result


def expert_kernel(place, slot_in, first, expert_in, expert_out, hidden, send):
    half = slot_in.shape[1]
    values = []
    for e in range(expert_in.shape[0]):
        product = first[e] + dot(slot_in[...], expert_in[e, column_half(1 - pair_at(place), half), :])
        values.append(jax.nn.gelu(product).astype(BF16))
        hidden[e] = values[e]
    send[...] = second_product(values, expert_out, column_half(1 - pair_at(place), half)).astype(BF16)


def own_kernel(place, hidden, expert_out, after, keep):
    values = [hidden[e] for e in range(hidden.shape[0])]
    keep[...] = second_product(values, expert_out, column_half(pair_at(place), keep.shape[1]))


def combine_kernel(logits, after, combine):
    value = logits[...]
    weights = jnp.exp(value - jnp.max(value, axis=1, keepdims=True))
    combine[...] = (weights / jnp.sum(weights, axis=1, keepdims=True)).astype(BF16)


def mix_kernel(place, combine, slot_out, mixed, rest, held, sems):
    width = slot_out.shape[1]
    tokens, done = combine.shape[0], held.shape[0]
    block = done // sems.shape[0]
    columns = pl.ds(pl.multiple_of(pair_at(place) * width, width), width)
    copies = []
    for i in range(tokens // block):
        rows = pl.ds(i * block, block)
        value = dot(combine[rows, :], slot_out[...]).astype(BF16)
        if i < sems.shape[0]:
            held[rows, :] = value
            copies.append(pltpu.make_async_copy(held.at[rows], mixed.at[rows, columns], sems.at[i]))
            copies[-1].start()
        else:
            rest[pl.ds(i * block - done, block), :] = value
    for copy in copies:
        copy.wait()


def mix_other_kernel(place, combine, slot_out, rest, before, mixed, held, sems):
    width = slot_out.shape[1]
    blocks = sems.shape[0] - 1
    tokens = combine.shape[0]
    done = tokens - rest.shape[0]
    mine = pl.ds(pl.multiple_of(pair_at(place) * width, width), width)
    other = pl.ds(pl.multiple_of((1 - pair_at(place)) * width, width), width)
    copies = [pltpu.make_async_copy(rest, mixed.at[pl.ds(done, tokens - done), mine], sems.at[blocks])]
    copies[0].start()
    block = tokens // blocks
    for i in range(blocks):
        rows = pl.ds(i * block, block)
        held[rows, :] = dot(combine[rows, :], slot_out[...]).astype(BF16)
        copies.append(pltpu.make_async_copy(held.at[rows], mixed.at[rows, other], sems.at[i]))
        copies[-1].start()
    for copy in copies:
        copy.wait()


def move(value, axes, offsets):
    sizes = [lax.axis_size(axis) for axis in axes]
    moves = []
    for index in range(math.prod(sizes)):
        source, target, stride = index, 0, 1
        for size, offset in zip(reversed(sizes), reversed(offsets)):
            target += (source % size ^ offset) * stride
            source //= size
            stride *= size
        moves.append((index, target))
    return lax.ppermute(value, axes, moves)


def swap_pair(value):
    return move(value, ("pair",), (1,))


def shards(tokens, slot_params, expert_in, expert_out):
    count, model = tokens.shape
    slots = slot_params.shape[1]
    far, near, rest = [lax.axis_size(axis) for axis in ("far", "near", "rest")]
    rows = slots // (far * near)
    half = model // 2
    place = lax.axis_index(("far", "near", "rest", "pair")).astype(jnp.int32).reshape(1)
    any_space = pl.BlockSpec(memory_space=pl.ANY)

    logits, turned, held, side, send = pl.pallas_call(
        gather_kernel,
        out_shape=(
            jax.ShapeDtypeStruct((count, slots), F32),
            jax.ShapeDtypeStruct((slots, count), BF16),
            jax.ShapeDtypeStruct((count, model), BF16),
            jax.ShapeDtypeStruct((slots, SIDE), F32),
            jax.ShapeDtypeStruct((slots, half + SIDE), BF16),
        ),
        in_specs=[SMEM, HBM, HBM],
        out_specs=(VMEM,) * 5,
        scratch_shapes=[pltpu.VMEM((model, slots), BF16), pltpu.SemaphoreType.DMA((count // CHUNK + 1,))],
        compiler_params=params(24),
        name="gather",
    )(place, in_hbm(tokens), in_hbm(slot_params))
    received = swap_pair(send)
    keep = pl.pallas_call(
        own_sums_kernel,
        out_shape=jax.ShapeDtypeStruct((slots, half), F32),
        in_specs=[SMEM, VMEM, VMEM, VMEM, any_space],
        out_specs=VMEM,
        cost_estimate=cost(2 * slots * count * half, 2 * count * (half + slots)),
        compiler_params=params(16),
        name="own_sums",
    )(place, turned, held, side, send)
    sends = pl.pallas_call(
        functools.partial(pair_kernel, rest),
        out_shape=(jax.ShapeDtypeStruct((near * rows, half + SIDE), BF16),) * far,
        in_specs=[SMEM] + [VMEM] * 3,
        out_specs=(VMEM,) * far,
        cost_estimate=cost(0, 6 * slots * model, 128 * slots * model),
        compiler_params=params(16),
        name="pair",
    )(place, keep, side, received)
    order = [0] + list(range(2, far)) + [1]
    parts = [sends[0]] + [move(sends[r], ("far",), (r,)) for r in order[1:]]
    send, their = pl.pallas_call(
        functools.partial(merge_kernel, rest),
        out_shape=(jax.ShapeDtypeStruct((rows, half + SIDE), BF16),) * 2,
        in_specs=[SMEM] + [VMEM] * far,
        out_specs=(VMEM, VMEM),
        compiler_params=params(16),
        name="merge",
    )(place, *parts)
    plane = ("near", "rest")
    mine = [move(their, plane, (1, r)) for r in reversed(range(rest))]
    mine = [send] + [move(send, plane, (0, r)) for r in range(1, rest)] + mine
    combine = pl.pallas_call(
        combine_kernel,
        out_shape=jax.ShapeDtypeStruct((count, slots), BF16),
        in_specs=[VMEM, any_space],
        out_specs=VMEM,
        cost_estimate=cost(8 * count * slots, 6 * count * slots, count * slots),
        compiler_params=params(16),
        name="combine",
    )(logits, send)
    experts, units = expert_out.shape[:2]
    slot_in = pl.pallas_call(
        finish_kernel,
        out_shape=jax.ShapeDtypeStruct((rows, half), BF16),
        in_specs=[any_space] + [VMEM] * len(mine),
        out_specs=VMEM,
        compiler_params=params(16),
        name="finish",
    )(combine, *mine)
    other = swap_pair(slot_in)
    first = pl.pallas_call(
        first_product_kernel,
        out_shape=jax.ShapeDtypeStruct((experts, rows, units), F32),
        in_specs=[SMEM, VMEM, VMEM],
        out_specs=VMEM,
        cost_estimate=cost(2 * rows * units * half * experts, 2 * experts * units * half),
        compiler_params=params(8),
        name="first_product",
    )(place, slot_in, expert_in)
    hidden, send = pl.pallas_call(
        expert_kernel,
        out_shape=(
            jax.ShapeDtypeStruct((experts, rows, units), BF16),
            jax.ShapeDtypeStruct((rows, half), BF16),
        ),
        in_specs=[SMEM, VMEM, VMEM, VMEM, VMEM],
        out_specs=(VMEM, VMEM),
        compiler_params=params(8),
        name="experts",
    )(place, other, first, expert_in, expert_out)
    received = swap_pair(send)
    keep = pl.pallas_call(
        own_kernel,
        out_shape=jax.ShapeDtypeStruct((rows, half), F32),
        in_specs=[SMEM, VMEM, VMEM, any_space],
        out_specs=VMEM,
        cost_estimate=cost(2 * rows * units * half * experts, 2 * experts * units * half),
        compiler_params=params(8),
        name="own",
    )(place, hidden, expert_out, send)
    partial = (keep + received.astype(F32)).astype(BF16)
    groups = far * near
    partials = jnp.broadcast_to(partial, (groups * rest, rows, half))
    partials = lax.all_to_all(partials, ("rest", "far", "near"), split_axis=0, concat_axis=0, tiled=True)
    slot_out = jnp.sum(partials.reshape(rest, groups, rows, half).astype(F32), axis=0)
    slot_out = slot_out.astype(BF16).reshape(slots, half)
    other = swap_pair(slot_out)
    done, blocks = count // 2, 8
    mixed, left = pl.pallas_call(
        mix_kernel,
        out_shape=(
            pltpu.HBM((count, model), BF16),
            jax.ShapeDtypeStruct((count - done, half), BF16),
        ),
        in_specs=[SMEM, VMEM, VMEM],
        out_specs=(HBM, VMEM),
        scratch_shapes=[pltpu.VMEM((done, half), BF16), pltpu.SemaphoreType.DMA((blocks // 2,))],
        cost_estimate=cost(2 * count * slots * half, 2 * count * (half + slots)),
        compiler_params=params(16),
        name="mix",
    )(place, combine, slot_out)
    return pl.pallas_call(
        mix_other_kernel,
        out_shape=jax.ShapeDtypeStruct((count, model), BF16),
        in_specs=[SMEM, VMEM, VMEM, VMEM, HBM],
        out_specs=HBM,
        scratch_shapes=[pltpu.VMEM((count, half), BF16), pltpu.SemaphoreType.DMA((blocks + 1,))],
        input_output_aliases={4: 0},
        cost_estimate=cost(2 * count * slots * half, 2 * count * (half + slots)),
        compiler_params=params(16),
        name="mix_other",
    )(place, combine, other, left, mixed)


def solution(mesh):
    wide, narrow = mesh.shape["wide"], mesh.shape["narrow"]
    cut = Mesh(mesh.devices.reshape(wide // 2, 2, narrow // 2, 2), ("far", "near", "rest", "pair"))
    wide_axes, narrow_axes = ("far", "near"), ("rest", "pair")
    return jax.shard_map(
        shards,
        mesh=cut,
        in_specs=(
            P(wide_axes + narrow_axes, None),
            P(),
            P(wide_axes, None, narrow_axes),
            P(wide_axes, narrow_axes, None),
        ),
        out_specs=P(wide_axes + narrow_axes, None),
        check_vma=False,
    )
```

```python
import functools
import math

import jax
import jax.numpy as jnp
from jax import lax
from jax.experimental import pallas as pl
from jax.experimental.pallas import tpu as pltpu
from jax.sharding import Mesh, PartitionSpec as P

SLOT_PER = 4
SIDE = 128
CHUNK = 256
F32 = jnp.float32
BF16 = jnp.bfloat16
VMEM = pl.BlockSpec(memory_space=pltpu.VMEM)
SMEM = pl.BlockSpec(memory_space=pltpu.SMEM)
HBM = pl.BlockSpec(memory_space=pltpu.HBM)
MIB = 1024 * 1024


def params(mib):
    return pltpu.CompilerParams(vmem_limit_bytes=mib * MIB)


def cost(flops, moved, transcendentals=0):
    return pl.CostEstimate(flops=flops, bytes_accessed=moved, transcendentals=transcendentals)


def in_hbm(value):
    return pltpu.with_memory_space_constraint(value, pltpu.HBM)


def dot(lhs, rhs):
    return jnp.dot(lhs, rhs, preferred_element_type=F32)


def side_state(*columns):
    lane = lax.broadcasted_iota(jnp.int32, (columns[0].shape[0], SIDE), 1)
    out = jnp.zeros((columns[0].shape[0], SIDE), F32)
    for index, value in enumerate(columns):
        out = jnp.where(lane == index, value, out)
    return out


def side_message(peak, total):
    lane = lax.broadcasted_iota(jnp.int32, (peak.shape[0], SIDE), 1)
    out = jnp.zeros((peak.shape[0], SIDE), F32)
    for index, value in enumerate((peak, total)):
        for piece in range(3):
            part = value.astype(BF16).astype(F32)
            out = jnp.where(lane == 3 * index + piece, part, out)
            value = value - part
    return out.astype(BF16)


def read_message(side):
    value = side.astype(F32)
    return (
        value[:, 0:1] + value[:, 1:2] + value[:, 2:3],
        value[:, 3:4] + value[:, 4:5] + value[:, 5:6],
    )


def pair_at(place):
    return place[0] & 1


def near_at(place, rest):
    return place[0] // (2 * rest) & 1


def far_at(place, rest):
    return place[0] // (4 * rest)


def column_half(side, half):
    return pl.ds(pl.multiple_of(side * half, half), half)


def gather_kernel(place, tokens, slot_params, logits, turned, held, side, send, table, sems):
    chunks = tokens.shape[0] // CHUNK
    slots = slot_params.shape[1]
    half = held.shape[1] // 2
    spans = [pl.ds(i * CHUNK, CHUNK) for i in range(chunks)]
    table_copy = pltpu.make_async_copy(slot_params, table, sems.at[chunks])
    table_copy.start()
    copies = [pltpu.make_async_copy(tokens.at[span], held.at[span], sems.at[i]) for i, span in enumerate(spans)]
    for copy in copies:
        copy.start()

    def find_peak(parts, high=None):
        for part in parts:
            top = jnp.max(part.reshape(CHUNK // 8, 8, slots), axis=0)
            high = top if high is None else jnp.maximum(high, top)
        return high

    def weigh(first, parts, peak):
        total = jnp.zeros((8, slots), F32)
        columns = []
        for part in parts:
            weights = jnp.exp(part - peak)
            total = total + jnp.sum(weights.reshape(CHUNK // 8, 8, slots), axis=0)
            columns.append(weights.astype(BF16).T)
        weights = jnp.concatenate(columns, axis=1)
        span = pl.ds(first * CHUNK, len(parts) * CHUNK)
        turned[:, span] = weights
        sums = dot(weights, held[span, column_half(1 - pair_at(place), half)])
        return sums, jnp.sum(total, axis=0, keepdims=True)

    table_copy.wait()
    high = None
    starts = [0] + list(range(1, chunks, 2))
    for first, end in zip(starts, starts[1:] + [chunks]):
        for copy in copies[first:end]:
            copy.wait()
        parts = [dot(held[span, :], table[...]) for span in spans[first:end]]
        for part, span in zip(parts, spans[first:end]):
            logits[span, :] = part
        if end < chunks:
            high = find_peak(parts, high)
    early_peak = jnp.max(high, axis=0, keepdims=True)
    early, early_total = weigh(0, [logits[span, :] for span in spans[:first]], early_peak)
    late_peak = jnp.max(find_peak(parts), axis=0, keepdims=True)
    late, late_total = weigh(first, parts, late_peak)
    peak = jnp.maximum(early_peak, late_peak)
    early_scale, late_scale = jnp.exp(early_peak - peak), jnp.exp(late_peak - peak)
    total = early_total * early_scale + late_total * late_scale
    row = lax.broadcasted_iota(jnp.int32, (8, slots), 0)
    columns = jnp.zeros((8, slots), F32)
    for index, value in enumerate((peak, total, early_scale, late_scale)):
        columns = jnp.where(row == index, value, columns)
    columns = columns.T
    peak, total, early_scale, late_scale = [columns[:, i : i + 1] for i in range(4)]
    send[:, :half] = (early * early_scale + late * late_scale).astype(BF16)
    side[...] = side_state(peak, total, early_scale, late_scale)
    send[:, half:] = side_message(peak, total)


def own_sums_kernel(place, turned, held, side, after, keep):
    columns = column_half(pair_at(place), keep.shape[1])
    early = held.shape[0] - CHUNK
    spans = (pl.ds(0, early), pl.ds(early, CHUNK))
    early, late = [dot(turned[:, span], held[span, columns]) for span in spans]
    keep[...] = early * side[:, 2:3] + late * side[:, 3:4]


def pair_kernel(rest, place, keep, side, received, *sends):
    width = keep.shape[1]
    for r, send in enumerate(sends):
        rows = send.shape[0]
        span = pl.ds(pl.multiple_of((far_at(place, rest) ^ r) * rows, rows), rows)
        peak_mine, total_mine = side[span, 0:1], side[span, 1:2]
        peak_other, total_other = read_message(received[span, width:])
        peak = jnp.maximum(peak_mine, peak_other)
        scale_mine, scale_other = jnp.exp(peak_mine - peak), jnp.exp(peak_other - peak)
        total = total_mine * scale_mine + total_other * scale_other
        sums = keep[span, :] * scale_mine + received[span, :width].astype(F32) * scale_other
        send[:, :width] = sums.astype(BF16)
        send[:, width:] = side_message(peak, total)


def add_parts(parts, width):
    states = [read_message(part[:, width:]) for part in parts]
    peak = states[0][0]
    for other, _ in states[1:]:
        peak = jnp.maximum(peak, other)
    total = jnp.zeros_like(peak)
    sums = jnp.zeros((parts[0].shape[0], width), F32)
    for part, (peak_other, total_other) in zip(parts, states):
        scale = jnp.exp(peak_other - peak)
        total = total + total_other * scale
        sums = sums + part[:, :width].astype(F32) * scale
    return sums, peak, total


def merge_kernel(rest, place, *refs):
    for n, send in enumerate(refs[-2:]):
        rows, width = send.shape[0], send.shape[1] - SIDE
        span = pl.ds(pl.multiple_of((near_at(place, rest) ^ n) * rows, rows), rows)
        sums, peak, total = add_parts([ref[span, :] for ref in refs[:-2]], width)
        send[:, :width] = sums.astype(BF16)
        send[:, width:] = side_message(peak, total)


def finish_kernel(combine, *refs):
    slot_in = refs[-1]
    sums, _, total = add_parts([ref[...] for ref in refs[:-1]], slot_in.shape[1])
    slot_in[...] = (sums / total).astype(BF16)


def first_product_kernel(place, slot_in, expert_in, result):
    half = slot_in.shape[1]
    for e in range(expert_in.shape[0]):
        result[e] = dot(slot_in[...], expert_in[e, column_half(pair_at(place), half), :])


def second_product(hidden, weights, columns):
    row = lax.broadcasted_iota(jnp.int32, (hidden[0].shape[0], 1), 0)
    result = 0.0
    for e, value in enumerate(hidden):
        result = jnp.where(row // SLOT_PER == e, dot(value, weights[e, :, columns]), result)
    return result


def expert_kernel(place, slot_in, first, expert_in, expert_out, hidden, send):
    half = slot_in.shape[1]
    values = []
    for e in range(expert_in.shape[0]):
        product = first[e] + dot(slot_in[...], expert_in[e, column_half(1 - pair_at(place), half), :])
        values.append(jax.nn.gelu(product).astype(BF16))
        hidden[e] = values[e]
    send[...] = second_product(values, expert_out, column_half(1 - pair_at(place), half)).astype(BF16)


def own_kernel(place, hidden, expert_out, after, keep):
    values = [hidden[e] for e in range(hidden.shape[0])]
    keep[...] = second_product(values, expert_out, column_half(pair_at(place), keep.shape[1]))


def combine_kernel(logits, after, combine):
    value = logits[...]
    weights = jnp.exp(value - jnp.max(value, axis=1, keepdims=True))
    combine[...] = (weights / jnp.sum(weights, axis=1, keepdims=True)).astype(BF16)


def mix_kernel(place, combine, slot_out, mixed, rest, held, sems):
    width = slot_out.shape[1]
    tokens, done = combine.shape[0], held.shape[0]
    block = done // sems.shape[0]
    columns = pl.ds(pl.multiple_of(pair_at(place) * width, width), width)
    copies = []
    for i in range(tokens // block):
        rows = pl.ds(i * block, block)
        value = dot(combine[rows, :], slot_out[...]).astype(BF16)
        if i < sems.shape[0]:
            held[rows, :] = value
            copies.append(pltpu.make_async_copy(held.at[rows], mixed.at[rows, columns], sems.at[i]))
            copies[-1].start()
        else:
            rest[pl.ds(i * block - done, block), :] = value
    for copy in copies:
        copy.wait()


def mix_other_kernel(place, combine, slot_out, rest, before, mixed, held, sems):
    width = slot_out.shape[1]
    blocks = sems.shape[0] - 1
    tokens = combine.shape[0]
    done = tokens - rest.shape[0]
    mine = pl.ds(pl.multiple_of(pair_at(place) * width, width), width)
    other = pl.ds(pl.multiple_of((1 - pair_at(place)) * width, width), width)
    copies = [pltpu.make_async_copy(rest, mixed.at[pl.ds(done, tokens - done), mine], sems.at[blocks])]
    copies[0].start()
    block = tokens // blocks
    for i in range(blocks):
        rows = pl.ds(i * block, block)
        held[rows, :] = dot(combine[rows, :], slot_out[...]).astype(BF16)
        copies.append(pltpu.make_async_copy(held.at[rows], mixed.at[rows, other], sems.at[i]))
        copies[-1].start()
    for copy in copies:
        copy.wait()


def move(value, axes, offsets):
    sizes = [lax.axis_size(axis) for axis in axes]
    moves = []
    for index in range(math.prod(sizes)):
        source, target, stride = index, 0, 1
        for size, offset in zip(reversed(sizes), reversed(offsets)):
            target += (source % size ^ offset) * stride
            source //= size
            stride *= size
        moves.append((index, target))
    return lax.ppermute(value, axes, moves)


def swap_pair(value):
    return move(value, ("pair",), (1,))


def shards(tokens, slot_params, expert_in, expert_out):
    count, model = tokens.shape
    slots = slot_params.shape[1]
    far, near, rest = [lax.axis_size(axis) for axis in ("far", "near", "rest")]
    rows = slots // (far * near)
    half = model // 2
    place = lax.axis_index(("far", "near", "rest", "pair")).astype(jnp.int32).reshape(1)
    any_space = pl.BlockSpec(memory_space=pl.ANY)

    logits, turned, held, side, send = pl.pallas_call(
        gather_kernel,
        out_shape=(
            jax.ShapeDtypeStruct((count, slots), F32),
            jax.ShapeDtypeStruct((slots, count), BF16),
            jax.ShapeDtypeStruct((count, model), BF16),
            jax.ShapeDtypeStruct((slots, SIDE), F32),
            jax.ShapeDtypeStruct((slots, half + SIDE), BF16),
        ),
        in_specs=[SMEM, HBM, HBM],
        out_specs=(VMEM,) * 5,
        scratch_shapes=[pltpu.VMEM((model, slots), BF16), pltpu.SemaphoreType.DMA((count // CHUNK + 1,))],
        compiler_params=params(24),
        name="gather",
    )(place, in_hbm(tokens), in_hbm(slot_params))
    received = swap_pair(send)
    keep = pl.pallas_call(
        own_sums_kernel,
        out_shape=jax.ShapeDtypeStruct((slots, half), F32),
        in_specs=[SMEM, VMEM, VMEM, VMEM, any_space],
        out_specs=VMEM,
        cost_estimate=cost(2 * slots * count * half, 2 * count * (half + slots)),
        compiler_params=params(16),
        name="own_sums",
    )(place, turned, held, side, send)
    sends = pl.pallas_call(
        functools.partial(pair_kernel, rest),
        out_shape=(jax.ShapeDtypeStruct((near * rows, half + SIDE), BF16),) * far,
        in_specs=[SMEM] + [VMEM] * 3,
        out_specs=(VMEM,) * far,
        cost_estimate=cost(0, 6 * slots * model, 128 * slots * model),
        compiler_params=params(16),
        name="pair",
    )(place, keep, side, received)
    order = [0] + list(range(far - 1, 0, -1))
    parts = [sends[0]] + [move(sends[r], ("far",), (r,)) for r in order[1:]]
    send, their = pl.pallas_call(
        functools.partial(merge_kernel, rest),
        out_shape=(jax.ShapeDtypeStruct((rows, half + SIDE), BF16),) * 2,
        in_specs=[SMEM] + [VMEM] * far,
        out_specs=(VMEM, VMEM),
        compiler_params=params(16),
        name="merge",
    )(place, *parts)
    plane = ("near", "rest")
    mine = [move(their, plane, (1, r)) for r in reversed(range(rest))]
    mine = [send] + [move(send, plane, (0, r)) for r in range(1, rest)] + mine
    combine = pl.pallas_call(
        combine_kernel,
        out_shape=jax.ShapeDtypeStruct((count, slots), BF16),
        in_specs=[VMEM, any_space],
        out_specs=VMEM,
        cost_estimate=cost(8 * count * slots, 6 * count * slots, count * slots),
        compiler_params=params(16),
        name="combine",
    )(logits, send)
    experts, units = expert_out.shape[:2]
    slot_in = pl.pallas_call(
        finish_kernel,
        out_shape=jax.ShapeDtypeStruct((rows, half), BF16),
        in_specs=[any_space] + [VMEM] * len(mine),
        out_specs=VMEM,
        compiler_params=params(16),
        name="finish",
    )(combine, *mine)
    other = swap_pair(slot_in)
    first = pl.pallas_call(
        first_product_kernel,
        out_shape=jax.ShapeDtypeStruct((experts, rows, units), F32),
        in_specs=[SMEM, VMEM, VMEM],
        out_specs=VMEM,
        cost_estimate=cost(2 * rows * units * half * experts, 2 * experts * units * half),
        compiler_params=params(8),
        name="first_product",
    )(place, slot_in, expert_in)
    hidden, send = pl.pallas_call(
        expert_kernel,
        out_shape=(
            jax.ShapeDtypeStruct((experts, rows, units), BF16),
            jax.ShapeDtypeStruct((rows, half), BF16),
        ),
        in_specs=[SMEM, VMEM, VMEM, VMEM, VMEM],
        out_specs=(VMEM, VMEM),
        compiler_params=params(8),
        name="experts",
    )(place, other, first, expert_in, expert_out)
    received = swap_pair(send)
    keep = pl.pallas_call(
        own_kernel,
        out_shape=jax.ShapeDtypeStruct((rows, half), F32),
        in_specs=[SMEM, VMEM, VMEM, any_space],
        out_specs=VMEM,
        cost_estimate=cost(2 * rows * units * half * experts, 2 * experts * units * half),
        compiler_params=params(8),
        name="own",
    )(place, hidden, expert_out, send)
    partial = (keep + received.astype(F32)).astype(BF16)
    groups = far * near
    partials = jnp.broadcast_to(partial, (groups * rest, rows, half))
    partials = lax.all_to_all(partials, ("rest", "far", "near"), split_axis=0, concat_axis=0, tiled=True)
    slot_out = jnp.sum(partials.reshape(rest, groups, rows, half).astype(F32), axis=0)
    slot_out = slot_out.astype(BF16).reshape(slots, half)
    other = swap_pair(slot_out)
    done, blocks = count // 2, 8
    mixed, left = pl.pallas_call(
        mix_kernel,
        out_shape=(
            pltpu.HBM((count, model), BF16),
            jax.ShapeDtypeStruct((count - done, half), BF16),
        ),
        in_specs=[SMEM, VMEM, VMEM],
        out_specs=(HBM, VMEM),
        scratch_shapes=[pltpu.VMEM((done, half), BF16), pltpu.SemaphoreType.DMA((blocks // 2,))],
        cost_estimate=cost(2 * count * slots * half, 2 * count * (half + slots)),
        compiler_params=params(16),
        name="mix",
    )(place, combine, slot_out)
    return pl.pallas_call(
        mix_other_kernel,
        out_shape=jax.ShapeDtypeStruct((count, model), BF16),
        in_specs=[SMEM, VMEM, VMEM, VMEM, HBM],
        out_specs=HBM,
        scratch_shapes=[pltpu.VMEM((count, half), BF16), pltpu.SemaphoreType.DMA((blocks + 1,))],
        input_output_aliases={4: 0},
        cost_estimate=cost(2 * count * slots * half, 2 * count * (half + slots)),
        compiler_params=params(16),
        name="mix_other",
    )(place, combine, other, left, mixed)


def solution(mesh):
    wide, narrow = mesh.shape["wide"], mesh.shape["narrow"]
    cut = Mesh(mesh.devices.reshape(wide // 2, 2, narrow // 2, 2), ("far", "near", "rest", "pair"))
    wide_axes, narrow_axes = ("far", "near"), ("rest", "pair")
    return jax.shard_map(
        shards,
        mesh=cut,
        in_specs=(
            P(wide_axes + narrow_axes, None),
            P(),
            P(wide_axes, None, narrow_axes),
            P(wide_axes, narrow_axes, None),
        ),
        out_specs=P(wide_axes + narrow_axes, None),
        check_vma=False,
    )
```
